512 devices in a mesh: wide: 128 (over y, z, core), narrow: 4 (over x).
Axes of the slice: x: 4, y: 8, z: 8, core: 2. Of those that a mesh axis runs over, the one named last changes fastest.
Arguments:
- coords: float32 [1536, 3, 512], P(('wide', 'narrow')), may hold values from 0 to 64, as said below
- noise_var: float32 [1536, 512], P(('wide', 'narrow')), may hold values from 1 to 2
- observed: float32 [1536, 512], P(('wide', 'narrow')), may hold values from -16 to 16
- warm_start: float32 [1536, 512], P(('wide', 'narrow')), may hold values from -3 to 3
- leaf_basis: bfloat16 [1536, 512, 64], P(('wide', 'narrow')), may hold values from -0.25 to 0.25
- leaf_transfer: bfloat16 [1536, 64, 64], P(('wide', 'narrow')), may hold values from -0.21875 to 0.21875
- leaf_coupling: bfloat16 [1536, 8, 64, 64], P(('wide', 'narrow')), may hold values from -0.25 to 0.25
- group_coupling: bfloat16 [128, 6, 64, 64], P('wide'), may hold values from -0.3125 to 0.3125
- top_transfer: bfloat16 [128, 64, 64], replicated, may hold values from -0.375 to 0.375
- top_coupling: bfloat16 [16, 4, 64, 64], replicated, may hold values from -0.375 to 0.375
- near_list: int32 [1536, 4], P(('wide', 'narrow')), may hold values from 0 to 1535, as said below
- near_count: int32 [1536], P(('wide', 'narrow')), may hold values from 1 to 4, as said below
- far_list: int32 [1536, 8], P(('wide', 'narrow')), may hold values from 0 to 1535, as said below
- far_count: int32 [1536], P(('wide', 'narrow')), may hold values from 1 to 8, as said below
- group_far: int32 [128, 6], P('wide'), may hold values from 0 to 127, as said below
- parent: int32 [128], replicated, may hold values from 0 to 15, never falling along the last dimension, each value on 1 to 16 neighbouring positions
- top_far: int32 [16, 4], replicated, may hold values from 0 to 15, as said below
Outputs:
- solution_field: float32 [1536, 512], P(('wide', 'narrow'))
- residual: float32 [1536, 512], P(('wide', 'narrow'))
The draws below stay inside these ranges and needn't reach their ends.
Inputs may be any that keep to these rules, and one draw needn't show every extreme that they name: `coords`: coordinates in box units; leaf b's points lie near the centre of its box on the Morton curve. `near_list`: slots 0 to near_count[b] - 1 of row b are used, later slots are to be ignored; slot 0 is b itself; the entries of a row are distinct and lie in b's level-one box or in the level-one box before or after it. `near_count`: some leaf box of some device uses all 4 slots in every draw. `far_list`: slots 0 to far_count[b] - 1 of row b are used, later slots are to be ignored; the entries of a row are distinct, lie in b's own level-one box and are not in b's near list. `far_count`: some leaf box of some device uses all 8 slots in every draw. `group_far`: the entries of a row g are distinct and differ from g. `parent`: never falls along the level-one boxes; each level-two box has 1 to 16 children. `top_far`: the entries of a row p are distinct and differ from p.
All inputs are finite; a program needn't handle non-finite values.
Results may differ from the reference program's by a relative error of at most 0.0003.
Values may be sent and summed in bfloat16 or wider, within the bound.
No kernel may reach another device: no remote copies, remote signals or barrier semaphores. Data moves between devices by JAX's collectives and lax.ppermute only.
A program may use at most 64 MiB of HBM per device.

```python
import math
import jax
import jax.numpy as jnp
import numpy as np
from jax import lax

LEAF_POINTS = 512
RANK = 64
NEAR = 4
FAR_LEAF = 8
FAR_GROUP = 6
ITERS = 2
LEAF_DEV = 3
GROUP_LEAVES = 12
LEAVES = 1536
TOP_BOXES = 16
TOP_KIDS = 16
FAR_TOP = 4
N_WIDE = 128


def device_limits(key, most):
    devices = LEAVES // LEAF_DEV
    key_limit, key_pick, key_fill = jax.random.split(key, 3)
    limits = jax.random.randint(key_limit, (devices,), 1, most + 1)
    filled = jax.random.randint(key_fill, (devices,), 0, 4) == 0
    chosen = jax.random.randint(key_pick, (), 0, devices)
    filled = filled | (jnp.arange(devices) == chosen)
    return jnp.where(filled, most, limits)


def leaf_counts(key, most):
    key_limit, key_each = jax.random.split(key)
    per_leaf = jnp.repeat(device_limits(key_limit, most), LEAF_DEV)
    counts = jax.random.randint(key_each, (LEAVES,), 1, most + 1)
    counts = jnp.minimum(counts, per_leaf)
    first_leaf = jnp.arange(LEAVES) % LEAF_DEV == 0
    return jnp.where(first_leaf, per_leaf, counts).astype(jnp.int32)


def leaf_lists(key):
    key_near, key_far = jax.random.split(key)
    leaf_index = jnp.arange(LEAVES, dtype=jnp.int32)
    span = 3 * GROUP_LEAVES
    group_start = leaf_index // GROUP_LEAVES * GROUP_LEAVES
    window = group_start[:, None] - GROUP_LEAVES + jnp.arange(span, dtype=jnp.int32)[None, :]
    inside = (window >= 0) & (window < LEAVES)
    scores = jax.random.randint(key_near, (LEAVES, span), 0, 2 ** 20) * span + jnp.arange(span, dtype=jnp.int32)[None, :]
    scores = jnp.where(window == leaf_index[:, None], -1, scores)
    scores = jnp.where(inside, scores, 2 ** 30)
    ranking = jnp.argsort(scores, axis=1)
    near = jnp.take_along_axis(window, ranking[:, :NEAR], axis=1)
    members = group_start[:, None] + jnp.arange(GROUP_LEAVES, dtype=jnp.int32)[None, :]
    listed = jnp.any(members[:, :, None] == near[:, None, :], axis=2)
    far_scores = jax.random.randint(key_far, (LEAVES, GROUP_LEAVES), 0, 2 ** 20) * GROUP_LEAVES + jnp.arange(GROUP_LEAVES, dtype=jnp.int32)[None, :]
    far_scores = jnp.where(listed, 2 ** 30, far_scores)
    far_ranking = jnp.argsort(far_scores, axis=1)
    far = jnp.take_along_axis(members, far_ranking[:, :FAR_LEAF], axis=1)
    return (near.astype(jnp.int32), far.astype(jnp.int32))


def distinct_others(key, boxes, slots):
    scores = jax.random.randint(key, (boxes, boxes), 0, 2 ** 20) * boxes + jnp.arange(boxes, dtype=jnp.int32)[None, :]
    scores = jnp.where(jnp.eye(boxes, dtype=jnp.int32) == 1, 2 ** 30, scores)
    return jnp.argsort(scores, axis=1)[:, :slots].astype(jnp.int32)


def draw_coords(key, part):
    key = jax.random.fold_in(key, 11)
    key_spread, key_jitter = jax.random.split(key)
    leaf_index = jnp.arange(LEAVES, dtype=jnp.int32)
    position_list = []
    for component in range(3):
        lattice = jnp.zeros((LEAVES,), jnp.int32)
        for level_index in range(6):
            bit_value = jnp.bitwise_and(jnp.right_shift(leaf_index, 3 * level_index + component), 1)
            lattice = lattice + jnp.left_shift(bit_value, level_index)
        position_list.append(lattice)
    centre = jnp.stack(position_list, axis=1).astype(jnp.float32) + 0.5
    spread = jnp.exp(jax.random.uniform(key_spread, (LEAVES,), jnp.float32, math.log(0.15), math.log(0.5)))
    jitter = jax.random.uniform(key_jitter, (LEAVES, 3, LEAF_POINTS), jnp.float32, -1.0, 1.0)
    return centre[:, :, None] + spread[:, None, None] * jitter


def draw_observed(key, part):
    key = jax.random.fold_in(key, 13)
    position = jnp.arange(LEAVES, dtype=jnp.float32) / (LEAVES - 1)
    growth = 1.0 + 2.0 * position
    values = jnp.clip(jax.random.normal(key, (LEAVES, LEAF_POINTS), jnp.float32), -5.0, 5.0) * growth[:, None]
    return values


def draw_near_list(key, part):
    return leaf_lists(key)[0]


def draw_far_list(key, part):
    return leaf_lists(key)[1]


def draw_near_count(key, part):
    key = jax.random.fold_in(key, 5)
    return leaf_counts(key, NEAR)


def draw_far_count(key, part):
    key = jax.random.fold_in(key, 7)
    return leaf_counts(key, FAR_LEAF)


def draw_group_far(key, part):
    key = jax.random.fold_in(key, 9)
    return distinct_others(key, N_WIDE, FAR_GROUP)


def draw_top_far(key, part):
    key = jax.random.fold_in(key, 17)
    return distinct_others(key, TOP_BOXES, FAR_TOP)


def levels(own_key, extent, pieces, low, largest):
    loudness, own = 1.0, jax.random.fold_in(own_key, 6)
    for axis_at, shards_of in pieces:
        steps = jnp.exp(jax.random.uniform(jax.random.fold_in(own, axis_at), (shards_of,), jnp.float32, low / len(pieces), largest / len(pieces)))
        loudness = loudness * jnp.repeat(steps, extent[axis_at] // shards_of).reshape([-1 if axis == axis_at else 1 for axis in range(len(extent))])
    return loudness


def profile(count, total, limit, lean):
    weights = [(1 << 20) // math.isqrt(standing ** lean) + 1 for standing in range(2, count + 1)]
    surplus, given = total - limit - (count - 1), [1] * (count - 1)
    while surplus > 0:
        candidates = [i for i in range(count - 1) if given[i] < limit]
        mass, remaining = sum([weights[i] for i in candidates]), surplus
        for i in candidates:
            extra = min(limit - given[i], max(1, remaining * weights[i] // mass), surplus)
            given[i] = given[i] + extra
            surplus = surplus - extra
    return np.array([limit] + given)


def uneven_parts(stream_key, amount, total, most, slope):
    if amount == 2:
        one = jax.random.randint(stream_key, (), max(1, total - most), min(most, total - 1) + 1)
        return jnp.stack([one, total - one])
    sizes = jnp.asarray(profile(amount, total, most, slope), jnp.int32)
    couples = (amount - 1) // 2
    source_of, taker = sizes[1:1 + 2 * couples:2], sizes[2:2 + 2 * couples:2]
    slack = jnp.minimum(source_of - 1, most - taker)
    moved = jax.random.randint(jax.random.fold_in(stream_key, 1), (couples,), 0, 1 << 20) % (slack + 1)
    sizes = sizes.at[1:1 + 2 * couples:2].set(source_of - moved).at[2:2 + 2 * couples:2].set(taker + moved)
    return sizes[jax.random.permutation(jax.random.fold_in(stream_key, 2), amount)]


def scatter_about(key, dims, scale, reach, cuts=(), kind=jnp.bfloat16):
    loudness = levels(key, dims, cuts, -0.22, 0.18) if cuts else 1.0
    array = jax.random.normal(key, dims, jnp.float32) * scale * loudness
    return jnp.minimum(jnp.maximum(array, -reach), reach).astype(kind)


def setup_inputs(seed: int = 0) -> dict:
    keys = jax.random.split(jax.random.key(seed), 18)
    return {
        "coords": draw_coords(jax.random.fold_in(keys[17], 71), 0),
        "noise_var": jnp.clip(1.0 + 1.0 * jax.random.uniform(keys[1], (LEAVES, LEAF_POINTS), jnp.float32) ** levels(keys[1], (LEAVES, LEAF_POINTS), ((0, 512),), -0.2, 0.2), 1.0, 2.0),
        "observed": draw_observed(jax.random.fold_in(keys[17], 71), 0),
        "warm_start": scatter_about(keys[3], (LEAVES, LEAF_POINTS), 0.5, 3.0, ((0, 512),), jnp.float32),
        "leaf_basis": scatter_about(keys[4], (LEAVES, LEAF_POINTS, RANK), LEAF_POINTS ** -0.5, 0.25, ((0, 512),)),
        "leaf_transfer": scatter_about(keys[5], (LEAVES, RANK, RANK), (RANK * GROUP_LEAVES) ** -0.5, 0.21875, ((0, 512),)),
        "leaf_coupling": scatter_about(keys[6], (LEAVES, FAR_LEAF, RANK, RANK), (RANK * FAR_LEAF) ** -0.5, 0.25, ((0, 512),)),
        "group_coupling": scatter_about(keys[7], (N_WIDE, FAR_GROUP, RANK, RANK), (RANK * FAR_GROUP) ** -0.5, 0.3125, ((0, 128),)),
        "top_transfer": scatter_about(keys[8], (N_WIDE, RANK, RANK), (4 * RANK) ** -0.5, 0.375),
        "top_coupling": scatter_about(keys[9], (TOP_BOXES, FAR_TOP, RANK, RANK), (RANK * FAR_TOP) ** -0.5, 0.375),
        "near_list": draw_near_list(jax.random.fold_in(keys[17], 71), 0),
        "near_count": draw_near_count(jax.random.fold_in(keys[17], 71), 0),
        "far_list": draw_far_list(jax.random.fold_in(keys[17], 71), 0),
        "far_count": draw_far_count(jax.random.fold_in(keys[17], 71), 0),
        "group_far": draw_group_far(jax.random.fold_in(keys[17], 71), 0),
        "parent": jnp.searchsorted(jnp.cumsum(uneven_parts(keys[15], TOP_BOXES, N_WIDE, TOP_KIDS, 2)), jnp.arange(N_WIDE), side="right").astype(jnp.int32),
        "top_far": draw_top_far(jax.random.fold_in(keys[17], 71), 0),
    }


amplitude = 1.0 / 16.0
length_scale = 1.5
root_three = 1.7320508075688772
highest = lax.Precision.HIGHEST

def kernel_block(target, source):
    squared = jnp.zeros(target.shape[:-2] + (target.shape[-1], source.shape[-1]), jnp.float32)
    for component in range(3):
        between = target[..., component, :, None] - source[..., component, None, :]
        squared = squared + between * between
    scaled = root_three / length_scale * jnp.sqrt(squared)
    return amplitude * (1.0 + scaled) * jnp.exp(-scaled)

def near_terms(coords, values, near_list, near_count):
    slot_ids = jnp.arange(NEAR)

    def one_leaf(packed):
        own_points, sources, used_slots = packed
        kernel_tile = kernel_block(own_points[None], jnp.take(coords, sources, axis=0))
        weights_on = (slot_ids < used_slots).astype(jnp.float32)
        source_values = jnp.take(values, sources, axis=0) * weights_on[:, None]
        return jnp.einsum('sij,sj->i', kernel_tile, source_values, precision=highest)
    return lax.map(one_leaf, (coords, near_list, near_count))

def reference(coords, noise_var, observed, warm_start, leaf_basis, leaf_transfer, leaf_coupling, group_coupling, top_transfer, top_coupling, near_list, near_count, far_list, far_count, group_far, parent, top_far):
    basis_float = leaf_basis.astype(jnp.float32)
    transfer_float = leaf_transfer.astype(jnp.float32)
    coupling_float = leaf_coupling.astype(jnp.float32)
    group_float = group_coupling.astype(jnp.float32)
    top_float = top_transfer.astype(jnp.float32)
    top_pair_float = top_coupling.astype(jnp.float32)
    parent_table = (parent[:, None] == jnp.arange(TOP_BOXES)[None, :]).astype(jnp.float32)
    far_mask = (jnp.arange(FAR_LEAF)[None, :] < far_count[:, None]).astype(jnp.float32)

    def operator_apply(values):
        coefficients = jnp.einsum('bpr,bp->br', basis_float, values, precision=highest)
        group_coef = jnp.einsum('gcrs,gcr->gs', transfer_float.reshape(N_WIDE, GROUP_LEAVES, RANK, RANK), coefficients.reshape(N_WIDE, GROUP_LEAVES, RANK), precision=highest)
        lifted = jnp.einsum('grs,gr->gs', top_float, group_coef, precision=highest)
        top_coef = jnp.dot(parent_table.T, lifted, precision=highest)
        top_in = jnp.einsum('psrt,pst->pr', top_pair_float, jnp.take(top_coef, top_far, axis=0), precision=highest)
        group_in = jnp.einsum('gsrt,gst->gr', group_float, jnp.take(group_coef, group_far, axis=0), precision=highest)
        down_top = jnp.dot(parent_table, top_in, precision=highest)
        group_in = group_in + jnp.einsum('grs,gs->gr', top_float, down_top, precision=highest)
        far_coef = jnp.take(coefficients, far_list, axis=0) * far_mask[:, :, None]
        leaf_in = jnp.einsum('bsrt,bst->br', coupling_float, far_coef, precision=highest)
        leaf_in = leaf_in + jnp.einsum('brs,bs->br', transfer_float, jnp.repeat(group_in, GROUP_LEAVES, axis=0), precision=highest)
        far_part = jnp.einsum('bpr,br->bp', basis_float, leaf_in, precision=highest)
        return noise_var * values + near_terms(coords, values, near_list, near_count) + far_part
    residual = observed - operator_apply(warm_start)
    solution_field = warm_start
    direction = residual
    norm_now = jnp.sum(residual * residual)
    for iteration in range(ITERS):
        mapped = operator_apply(direction)
        step_size = norm_now / jnp.sum(direction * mapped)
        solution_field = solution_field + step_size * direction
        residual = residual - step_size * mapped
        norm_next = jnp.sum(residual * residual)
        direction = residual + norm_next / norm_now * direction
        norm_now = norm_next
    return (solution_field, residual)
```

```python
import jax
import jax.numpy as jnp
from jax import lax
from jax.sharding import PartitionSpec as P

amplitude = 1.0 / 16.0
length_scale = 1.5
root_three = 1.7320508075688772
highest = lax.Precision.HIGHEST


def kernel_block(target, source):
    squared = jnp.zeros(target.shape[:-2] + (target.shape[-1], source.shape[-1]), jnp.float32)
    for component in range(3):
        between = target[..., component, :, None] - source[..., component, None, :]
        squared = squared + between * between
    scaled = root_three / length_scale * jnp.sqrt(squared)
    return amplitude * (1.0 + scaled) * jnp.exp(-scaled)


def window(group):
    wide = lax.axis_size("wide")
    up = [(i, i + 1) for i in range(wide - 1)]
    down = [(j, i) for i, j in up]
    before = lax.ppermute(group, "wide", up)
    after = lax.ppermute(group, "wide", down)
    return before, after


def wide_all_to_all(row):
    wide = lax.axis_size("wide")
    spread = jnp.broadcast_to(row[None], (wide,) + row.shape)
    return lax.all_to_all(spread, "wide", 0, 0, tiled=True), 0


def wide_doubling(row):
    wide = lax.axis_size("wide")
    rows, step = row[None], 1
    while step < wide:
        other = lax.ppermute(rows, "wide", [(i, i ^ step) for i in range(wide)])
        rows = jnp.concatenate([rows, other], axis=0)
        step *= 2
    return rows, lax.axis_index("wide")


def wide_two_phase(row):
    wide = lax.axis_size("wide")
    inner = [list(range(i, i + 16)) for i in range(0, wide, 16)]
    outer = [list(range(i, wide, 16)) for i in range(16)]
    rows = lax.all_gather(row[None], "wide", axis=0, tiled=True, axis_index_groups=inner)
    return lax.all_gather(rows, "wide", axis=0, tiled=True, axis_index_groups=outer), 0


def local(
    coords,
    noise_var,
    observed,
    warm_start,
    leaf_basis,
    leaf_transfer,
    leaf_coupling,
    group_coupling,
    top_transfer,
    top_coupling,
    near_list,
    near_count,
    far_list,
    far_count,
    group_far,
    parent,
    top_far,
):
    leaves = noise_var.shape[0]
    narrow = lax.axis_size("narrow")
    group_len = leaves * narrow
    groups = parent.shape[0]
    wide_index = lax.axis_index("wide")
    near_local = jnp.clip(near_list - (wide_index - 1) * group_len, 0, 3 * group_len - 1)
    far_local = jnp.clip(far_list - wide_index * group_len, 0, group_len - 1)
    near_mask = (jnp.arange(near_list.shape[1])[None, :] < near_count[:, None]).astype(jnp.float32)
    far_mask = (jnp.arange(far_list.shape[1])[None, :] < far_count[:, None]).astype(jnp.float32)
    basis_float = leaf_basis.astype(jnp.float32)
    transfer_float = leaf_transfer.astype(jnp.float32)
    coupling_float = leaf_coupling.astype(jnp.float32)
    group_float = group_coupling[0].astype(jnp.float32)
    own_top = lax.dynamic_index_in_dim(top_transfer, wide_index, 0, False).astype(jnp.float32)
    own_parent = lax.dynamic_index_in_dim(parent, wide_index, 0, False)
    top_boxes = lax.dynamic_index_in_dim(top_far, own_parent, 0, False)
    top_pair = lax.dynamic_index_in_dim(top_coupling, own_parent, 0, False).astype(jnp.float32)

    group_coords = lax.all_gather(coords, "narrow", axis=0, tiled=True)
    before, after = window(group_coords)
    coord_window = jnp.concatenate([before, group_coords, after], axis=0)
    sources = jnp.take(coord_window, near_local, axis=0)
    tiles = kernel_block(coords[:, None], sources) * near_mask[:, :, None, None]

    def operator_apply(values, scalar, wide_gather):
        coefficients = jnp.einsum("bpr,bp->br", basis_float, values, precision=highest)
        partial_coef = jnp.einsum("crs,cr->s", transfer_float, coefficients, precision=highest)
        lifted = jnp.einsum("rs,r->s", own_top, partial_coef, precision=highest)
        packed = jnp.concatenate(
            [
                values.reshape(-1),
                coefficients.reshape(-1),
                jnp.zeros((64,), jnp.float32),
                partial_coef,
                lifted,
                jnp.broadcast_to(scalar, (128,)),
            ]
        ).reshape(16, 128)
        group = lax.all_gather(packed[None], "narrow", axis=0, tiled=True)
        field_group = group[:, :12].reshape(group_len, 512)
        coef_group = group[:, 12:14].reshape(narrow, 256)[:, :192].reshape(group_len, 64)
        before, after = window(field_group)
        rows, turn = wide_gather(jnp.sum(group[:, 14:], axis=0))
        places = jnp.arange(groups) ^ turn
        far_rows = (group_far[0][:, None] == places[None, :]).astype(jnp.float32)
        parents = jnp.take(parent, places, axis=0)
        top_rows = (top_boxes[:, None] == parents[None, :]).astype(jnp.float32)
        picked = jnp.dot(
            jnp.concatenate([far_rows, top_rows], axis=0), rows[:, 0], precision=highest
        )
        total = jnp.sum(rows[:, 1, 0])
        group_in = jnp.einsum("srt,st->r", group_float, picked[:6, :64], precision=highest)
        top_in = jnp.einsum("srt,st->r", top_pair, picked[6:, 64:], precision=highest)
        group_in = group_in + jnp.dot(own_top, top_in, precision=highest)
        far_coef = jnp.take(coef_group, far_local, axis=0) * far_mask[:, :, None]
        leaf_in = jnp.einsum("bsrt,bst->br", coupling_float, far_coef, precision=highest)
        leaf_in = leaf_in + jnp.einsum("brs,s->br", transfer_float, group_in, precision=highest)
        far_part = jnp.einsum("bpr,br->bp", basis_float, leaf_in, precision=highest)
        field_window = jnp.concatenate([before, field_group, after], axis=0)
        near_values = jnp.take(field_window, near_local, axis=0)
        near_part = jnp.einsum("bsij,bsj->bi", tiles, near_values, precision=highest)
        return noise_var * values + near_part + far_part, total

    mapped, _ = operator_apply(warm_start, jnp.float32(0), wide_all_to_all)
    residual = observed - mapped
    first, norm_now = operator_apply(residual, jnp.sum(residual * residual), wide_doubling)
    scale = lax.rsqrt(norm_now)
    unit = first * scale
    second, curve = operator_apply(unit, jnp.sum(residual * first), wide_two_phase)
    step_size = norm_now / curve
    lower = residual - step_size * first
    lower_mapped = first - (step_size / scale) * second
    sums = jnp.stack(
        [
            jnp.sum(lower * lower),
            jnp.sum(lower * lower_mapped),
            jnp.sum(residual * lower_mapped + lower * first),
        ]
    )
    sums = jnp.sum(
        lax.all_gather(jnp.pad(sums, (0, 125))[None], ("wide", "narrow"), axis=0, tiled=True), axis=0
    )
    ratio = sums[0] / norm_now
    second_step = sums[0] / (sums[1] + ratio * (sums[2] + ratio * curve))
    solution_field = warm_start + step_size * residual
    solution_field = solution_field + second_step * (lower + ratio * residual)
    return (solution_field, lower - second_step * (lower_mapped + ratio * first))


def solution(mesh):
    placed = (
        P(("wide", "narrow"), None, None),
        P(("wide", "narrow"), None),
        P(("wide", "narrow"), None),
        P(("wide", "narrow"), None),
        P(("wide", "narrow"), None, None),
        P(("wide", "narrow"), None, None),
        P(("wide", "narrow"), None, None, None),
        P("wide", None, None, None),
        P(),
        P(),
        P(("wide", "narrow"), None),
        P(("wide", "narrow")),
        P(("wide", "narrow"), None),
        P(("wide", "narrow")),
        P("wide", None),
        P(),
        P(),
    )
    return jax.shard_map(
        local,
        mesh=mesh,
        in_specs=placed,
        out_specs=(P(("wide", "narrow"), None), P(("wide", "narrow"), None)),
        check_vma=False,
    )
```

```python
import jax
import jax.numpy as jnp
from jax import lax
from jax.sharding import PartitionSpec as P

amplitude = 1.0 / 16.0
length_scale = 1.5
root_three = 1.7320508075688772
highest = lax.Precision.HIGHEST


def kernel_block(target, source):
    squared = jnp.zeros(target.shape[:-2] + (target.shape[-1], source.shape[-1]), jnp.float32)
    for component in range(3):
        between = target[..., component, :, None] - source[..., component, None, :]
        squared = squared + between * between
    scaled = root_three / length_scale * jnp.sqrt(squared)
    return amplitude * (1.0 + scaled) * jnp.exp(-scaled)


def exchange(block, members, stride):
    devices = lax.axis_size("wide") * lax.axis_size("narrow")
    span = members * stride
    groups = [
        [base + offset + stride * i for i in range(members)]
        for base in range(0, devices, span)
        for offset in range(stride)
    ]
    copies = jnp.broadcast_to(block[None], (members,) + block.shape)
    return lax.all_to_all(
        copies, ("wide", "narrow"), 0, 0, tiled=True, axis_index_groups=groups
    )


def neighbours(group, together):
    wide = lax.axis_size("wide")
    across = []
    for first in range(together - 1, wide - 1, together):
        across += [(first, first + 1), (first + 1, first)]
    extra = [lax.ppermute(group, "wide", across)]
    if together == 1:
        across = [(i, i ^ 1) for i in range(wide)]
        swaps = [(i, i + 1 if i % 2 else i - 1) for i in range(1, wide - 1)]
        extra = [lax.ppermute(group, "wide", across), lax.ppermute(group, "wide", swaps)]
    return extra


def local(
    coords,
    noise_var,
    observed,
    warm_start,
    leaf_basis,
    leaf_transfer,
    leaf_coupling,
    group_coupling,
    top_transfer,
    top_coupling,
    near_list,
    near_count,
    far_list,
    far_count,
    group_far,
    parent,
    top_far,
):
    leaves = noise_var.shape[0]
    narrow = lax.axis_size("narrow")
    group_len = leaves * narrow
    groups = parent.shape[0]
    wide_index = lax.axis_index("wide")

    def near_places(together):
        base = wide_index // together * together
        group = near_list // group_len
        inside = (group >= base) & (group < base + together)
        outside = jnp.where((group ^ 1) == wide_index, 1, 2) if together == 1 else together
        place = jnp.where(inside, group - base, outside)
        return jnp.clip(place * group_len + near_list % group_len, 0, (together + 2) * group_len)

    far_local = jnp.clip(far_list - wide_index * group_len, 0, group_len - 1)
    near_mask = (jnp.arange(near_list.shape[1])[None, :] < near_count[:, None]).astype(jnp.float32)
    far_mask = (jnp.arange(far_list.shape[1])[None, :] < far_count[:, None]).astype(jnp.float32)
    basis_float = leaf_basis.astype(jnp.float32)
    transfer_float = leaf_transfer.astype(jnp.float32)
    coupling_float = leaf_coupling.astype(jnp.float32)
    group_float = group_coupling[0].astype(jnp.float32)
    own_top = lax.dynamic_index_in_dim(top_transfer, wide_index, 0, False).astype(jnp.float32)
    own_parent = lax.dynamic_index_in_dim(parent, wide_index, 0, False)
    top_boxes = lax.dynamic_index_in_dim(top_far, own_parent, 0, False)
    top_pair = lax.dynamic_index_in_dim(top_coupling, own_parent, 0, False).astype(jnp.float32)

    def operator_apply(values, scalar, together, tiles):
        coefficients = jnp.einsum("bpr,bp->br", basis_float, values, precision=highest)
        partial_coef = jnp.einsum("crs,cr->s", transfer_float, coefficients, precision=highest)
        lifted = jnp.einsum("rs,r->s", own_top, partial_coef, precision=highest)
        packed = [
            values.reshape(-1),
            coefficients.reshape(-1),
            jnp.zeros((64,), jnp.float32),
            partial_coef,
            lifted,
            jnp.broadcast_to(scalar, (128,)),
        ]
        if tiles is None:
            packed.append(coords.reshape(-1))
        packed = jnp.concatenate(packed).reshape(-1, 128)
        blocks = exchange(packed, narrow * together, 1)
        blocks = blocks.reshape((together, narrow) + packed.shape)
        own = lax.dynamic_index_in_dim(blocks, wide_index % together, 0, False)
        coef_group = own[:, 12:14].reshape(narrow, 256)[:, :192].reshape(group_len, 64)
        carried = jnp.concatenate([own[:, :12], own[:, 16:]], axis=1)
        extra = neighbours(carried, together)
        rows = exchange(jnp.sum(blocks[:, :, 14:16], axis=1), groups // together, narrow * together)
        rows = rows.reshape(groups, 2, 128)
        far_rows = (group_far[0][:, None] == jnp.arange(groups)[None, :]).astype(jnp.float32)
        top_rows = (top_boxes[:, None] == parent[None, :]).astype(jnp.float32)
        picked = jnp.dot(
            jnp.concatenate([far_rows, top_rows], axis=0), rows[:, 0], precision=highest
        )
        total = jnp.sum(rows[:, 1, 0])
        group_in = jnp.einsum("srt,st->r", group_float, picked[:6, :64], precision=highest)
        top_in = jnp.einsum("srt,st->r", top_pair, picked[6:, 64:], precision=highest)
        group_in = group_in + jnp.dot(own_top, top_in, precision=highest)
        far_coef = jnp.take(coef_group, far_local, axis=0) * far_mask[:, :, None]
        leaf_in = jnp.einsum("bsrt,bst->br", coupling_float, far_coef, precision=highest)
        leaf_in = leaf_in + jnp.einsum("brs,s->br", transfer_float, group_in, precision=highest)
        far_part = jnp.einsum("bpr,br->bp", basis_float, leaf_in, precision=highest)
        inside = jnp.concatenate([blocks[:, :, :12], blocks[:, :, 16:]], axis=2)
        whole = jnp.concatenate([inside] + [one[None] for one in extra], axis=0)
        places = near_places(together)
        near_values = jnp.take(whole[:, :, :12].reshape(-1, 512), places, axis=0)
        if tiles is None:
            sources = jnp.take(whole[:, :, 12:].reshape(-1, 3, 512), places, axis=0)
            tiles = kernel_block(coords[:, None], sources) * near_mask[:, :, None, None]
            tiles = lax.optimization_barrier(tiles)
        near_part = jnp.einsum("bsij,bsj->bi", tiles, near_values, precision=highest)
        return noise_var * values + near_part + far_part, total, tiles

    mapped, _, tiles = operator_apply(warm_start, jnp.float32(0), 2, None)
    residual = observed - mapped
    first, norm_now, _ = operator_apply(residual, jnp.sum(residual * residual), 1, tiles)
    scale = lax.rsqrt(norm_now)
    unit = first * scale
    second, curve, _ = operator_apply(unit, jnp.sum(residual * first), 8, tiles)
    step_size = norm_now / curve
    lower = residual - step_size * first
    lower_mapped = first - (step_size / scale) * second
    sums = jnp.stack(
        [
            jnp.sum(lower * lower),
            jnp.sum(lower * lower_mapped),
            jnp.sum(residual * lower_mapped + lower * first),
        ]
    )
    sums = jnp.sum(exchange(jnp.pad(sums, (0, 125)), 32, 1), axis=0)
    sums = jnp.sum(exchange(sums, 16, 32), axis=0)
    ratio = sums[0] / norm_now
    second_step = sums[0] / (sums[1] + ratio * (sums[2] + ratio * curve))
    solution_field = warm_start + step_size * residual
    solution_field = solution_field + second_step * (lower + ratio * residual)
    return (solution_field, lower - second_step * (lower_mapped + ratio * first))


def solution(mesh):
    placed = (
        P(("wide", "narrow"), None, None),
        P(("wide", "narrow"), None),
        P(("wide", "narrow"), None),
        P(("wide", "narrow"), None),
        P(("wide", "narrow"), None, None),
        P(("wide", "narrow"), None, None),
        P(("wide", "narrow"), None, None, None),
        P("wide", None, None, None),
        P(),
        P(),
        P(("wide", "narrow"), None),
        P(("wide", "narrow")),
        P(("wide", "narrow"), None),
        P(("wide", "narrow")),
        P("wide", None),
        P(),
        P(),
    )
    return jax.shard_map(
        local,
        mesh=mesh,
        in_specs=placed,
        out_specs=(P(("wide", "narrow"), None), P(("wide", "narrow"), None)),
        check_vma=False,
    )
```

```python
import functools

import jax
import jax.numpy as jnp
from jax import lax
from jax.experimental import pallas as pl
from jax.experimental.pallas import tpu as pltpu
from jax.sharding import PartitionSpec as P

amplitude = 1.0 / 16.0
rate = 1.7320508075688772 / 1.5
log2_e = 1.4426950408889634
LEAVES = 3
NARROW = 4
GROUP = LEAVES * NARROW
POINTS = 512
RANK = 64
NEAR = 4
FAR = 8
FAR_GROUP = 6
FAR_TOP = 4
LANES = 128
PIECES = POINTS // LANES
FIELD = LEAVES * PIECES
PACK = FIELD + 4
COORDS = 3 * FIELD
PAIR = 2 * NARROW
WINDOW = 3 * GROUP
CHUNK = 32
VMEM = pl.BlockSpec(memory_space=pltpu.VMEM)
SMEM = pl.BlockSpec(memory_space=pltpu.SMEM)
f32 = jnp.float32


def shape(*dims, dtype=f32):
    return jax.ShapeDtypeStruct(dims, dtype)


def cost(flops, bytes_accessed):
    return pl.CostEstimate(flops=flops, bytes_accessed=bytes_accessed, transcendentals=0)


def rows_of(array):
    return lax.broadcasted_iota(jnp.int32, array.shape, 0)


def times(vectors, matrix, transposed):
    high = vectors.astype(jnp.bfloat16).astype(f32)
    rest = vectors - high
    middle = rest.astype(jnp.bfloat16).astype(f32)
    parts = jnp.concatenate([high, middle, rest - middle], axis=0).astype(jnp.bfloat16)
    dims = (((1,), (1 if transposed else 0,)), ((), ()))
    out = lax.dot_general(parts, matrix, dims, preferred_element_type=f32)
    count = vectors.shape[0]
    return out[:count] + (out[count : 2 * count] + out[2 * count :])


def row_by_leaf(terms):
    out = jnp.zeros_like(terms[0])
    for leaf, term in enumerate(terms):
        out = jnp.where(rows_of(term) == leaf, term, out)
    return out


def fold_half(row):
    return row[:, :RANK] + row[:, RANK:]


def lane_sums(product):
    total = jnp.sum(product, axis=0, keepdims=True)
    total = total[:, :128] + total[:, 128:256] + (total[:, 256:384] + total[:, 384:])
    return fold_half(total)


def pack(values, scalar, basis, transfer, packed):
    for leaf in range(LEAVES):
        for piece in range(PIECES):
            packed[0, pl.ds(leaf * PIECES + piece, 1), :] = values[
                leaf : leaf + 1, piece * LANES : (piece + 1) * LANES
            ]
    coefs = row_by_leaf([times(values, basis[leaf], True) for leaf in range(LEAVES)])
    partial = row_by_leaf([times(coefs, transfer[leaf], False) for leaf in range(LEAVES)])
    partial = jnp.sum(partial, axis=0, keepdims=True)
    empty = jnp.zeros((1, RANK), f32)
    beside = [scalar, empty, empty]
    for leaf in range(LEAVES):
        packed[0, pl.ds(FIELD + leaf, 1), :] = jnp.concatenate(
            [coefs[leaf : leaf + 1], beside[leaf]], axis=1
        )
    packed[0, pl.ds(FIELD + 3, 1), :] = jnp.concatenate([partial, empty], axis=1)
    whole = packed[0]
    for copy in range(1, PAIR):
        packed[copy] = whole


def padded(ref, scratch):
    scratch[...] = jnp.zeros(scratch.shape, f32)
    scratch[0:LEAVES, :] = ref[...]
    return scratch[...]


def begin_kernel(warm, coords, basis, transfer, packed, values, scratch):
    field = padded(warm, scratch)
    values[...] = field
    for leaf in range(LEAVES):
        for axis in range(3):
            for piece in range(PIECES):
                packed[0, pl.ds(PACK + (leaf * 3 + axis) * PIECES + piece, 1), :] = coords[
                    leaf, axis : axis + 1, piece * LANES : (piece + 1) * LANES
                ]
    pack(field, jnp.zeros((1, RANK), f32), basis, transfer, packed)


def fold_kernel(blocks, top_transfer, copies, fields):
    own = lax.rem(lax.axis_index("wide"), 2)
    sums = []
    for row in (FIELD + 3, FIELD):
        for group in range(2):
            first = group * NARROW
            line = [blocks[first + i, row : row + 1, :] for i in range(NARROW)]
            line = (line[0] + line[1]) + (line[2] + line[3])
            if row == FIELD + 3:
                partial = jnp.broadcast_to(line[:, :RANK], (8, RANK))
                lifted = times(partial, top_transfer[group], False)[:1]
                line = jnp.concatenate([line[:, :RANK], lifted], axis=1)
            sums.append(line)
    sums = jnp.concatenate(sums, axis=0)
    copies[...] = jnp.broadcast_to(sums[None], copies.shape)
    for i in range(NARROW):
        device = own * NARROW + i
        fields[i, 0:FIELD, :] = blocks[device, 0:FIELD, :]
        if fields.shape[1] > FIELD:
            fields[i, FIELD:, :] = blocks[device, PACK:, :]


def near_kernel(evaluate, *refs):
    if evaluate:
        (near_list, near_count, far_list, far_count, blocks, extra, values, noise, coupling,
         columns, tiles, base, leaf_far, window, sources, scratch, coefs, totals) = refs
    else:
        (near_list, near_count, far_list, far_count, blocks, extra, values, noise, coupling,
         tiles, base, leaf_far, window, scratch, coefs, totals) = refs
    wide = lax.axis_index("wide")
    own = lax.rem(wide, 2)
    first_group = wide - own

    for device in range(PAIR):
        for leaf in range(LEAVES):
            at = device * LEAVES + leaf
            window[at] = blocks[device, leaf * PIECES : (leaf + 1) * PIECES, :]
            if evaluate:
                rows = PACK + leaf * FIELD
                sources[at] = blocks[device, rows : rows + FIELD, :]
    for device in range(NARROW):
        for leaf in range(LEAVES):
            at = (PAIR + device) * LEAVES + leaf
            window[at] = extra[device, leaf * PIECES : (leaf + 1) * PIECES, :]
            if evaluate:
                rows = FIELD + leaf * FIELD
                sources[at] = extra[device, rows : rows + FIELD, :]

    coefs[...] = jnp.zeros(coefs.shape, f32)
    for device in range(NARROW):
        coefs[device * LEAVES : (device + 1) * LEAVES, :] = blocks[
            own * NARROW + device, FIELD : FIELD + LEAVES, :
        ]
    lane = lax.broadcasted_iota(jnp.int32, (16, LANES), 1)
    row = lax.broadcasted_iota(jnp.int32, (16, LANES), 0)
    far_rows = []
    for leaf in range(LEAVES):
        out = times(coefs[:, :RANK], coupling[leaf].reshape(FAR * RANK, RANK), True)
        total = jnp.zeros((16, LANES), f32)
        for two in range(FAR // 2):
            at = []
            for slot in (2 * two, 2 * two + 1):
                member = far_list[leaf, slot] - wide * GROUP
                at.append(jnp.where(slot < far_count[leaf], member, -1))
            listed = jnp.where(lane < RANK, at[0], at[1]) == row
            total = total + jnp.where(listed, out[:, two * LANES : (two + 1) * LANES], 0.0)
        far_rows.append(fold_half(jnp.sum(total, axis=0, keepdims=True)))
    leaf_far[...] = row_by_leaf([jnp.broadcast_to(one, (8, RANK)) for one in far_rows])

    def place(leaf, slot):
        listed = near_list[leaf, slot]
        group = lax.div(listed, GROUP)
        member = listed - group * GROUP
        turn = group - first_group
        turn = jnp.where((turn >= 0) & (turn < 2), turn, 2)
        return jnp.where(slot < near_count[leaf], turn * GROUP + member, wide * 0)

    eye = lax.broadcasted_iota(jnp.int32, (LANES, LANES), 0) == lax.broadcasted_iota(
        jnp.int32, (LANES, LANES), 1
    )
    near_rows = []
    for leaf in range(LEAVES):
        places = [place(leaf, slot) for slot in range(NEAR)]
        weights = [
            jnp.where(slot < near_count[leaf], 1.0, 0.0).astype(f32) for slot in range(NEAR)
        ]
        fields = [window[places[slot]] * weights[slot] for slot in range(NEAR)]

        def step(chunk, _):
            start = pl.multiple_of(chunk * CHUNK, CHUNK)
            acc = jnp.zeros((CHUNK, LANES), f32)
            if evaluate:
                column = columns[leaf, pl.ds(start, CHUNK), :]
                target = [
                    jnp.broadcast_to(column[:, axis : axis + 1], (CHUNK, LANES)) for axis in range(3)
                ]
            for slot in range(NEAR):
                for piece in range(PIECES):
                    cut = slice(piece * LANES, (piece + 1) * LANES)
                    if evaluate:
                        squared = None
                        for axis in range(3):
                            at = axis * PIECES + piece
                            between = target[axis] - sources[places[slot], pl.ds(at, 1), :]
                            between = between * between
                            squared = between if squared is None else squared + between
                        squared = jnp.maximum(squared, 1e-30)
                        distance = squared * lax.rsqrt(squared)
                        decay = jnp.exp2(distance * (-rate * log2_e))
                        tile = (distance * (amplitude * rate) + amplitude) * decay
                        tiles[leaf * NEAR + slot, pl.ds(start, CHUNK), cut] = tile
                    else:
                        tile = tiles[leaf * NEAR + slot, pl.ds(start, CHUNK), cut]
                    acc = acc + tile * fields[slot][piece : piece + 1, :]
            totals[pl.ds(start, CHUNK), :] = acc
            return 0

        lax.fori_loop(0, POINTS // CHUNK, step, 0)
        pieces = []
        for piece in range(PIECES):
            column = jnp.sum(totals[piece * LANES : (piece + 1) * LANES, :], axis=1, keepdims=True)
            pieces.append(jnp.sum(jnp.where(eye, column, 0.0), axis=0, keepdims=True))
        near_rows.append(jnp.concatenate(pieces, axis=1))
    near = row_by_leaf([jnp.broadcast_to(one, (8, POINTS)) for one in near_rows])
    base[...] = padded(noise, scratch) * values[...] + near


def near_apply(lists, blocks, extra, values, noise, coupling, columns, tiles):
    evaluate = tiles is None
    rows = NEAR * LEAVES
    small = [shape(8, POINTS), shape(8, RANK)]
    scratch = [pltpu.VMEM((WINDOW, PIECES, LANES), f32)]
    if evaluate:
        scratch.append(pltpu.VMEM((WINDOW, FIELD, LANES), f32))
    scratch += [
        pltpu.VMEM((8, POINTS), f32),
        pltpu.VMEM((16, LANES), f32),
        pltpu.VMEM((POINTS, LANES), f32),
    ]
    last = columns if evaluate else tiles
    return pl.pallas_call(
        functools.partial(near_kernel, evaluate),
        out_shape=([shape(rows, POINTS, POINTS)] if evaluate else []) + small,
        in_specs=[SMEM] * 4 + [VMEM] * 6,
        out_specs=[VMEM] * (3 if evaluate else 2),
        scratch_shapes=scratch,
        cost_estimate=cost(3 * 10**8 if evaluate else 10**7, 2 * 10**6),
        compiler_params=pltpu.CompilerParams(vmem_limit_bytes=(24 if evaluate else 24) << 20),
    )(*lists, blocks, extra, values, noise, coupling, last)


def far_field(rows, base, leaf_far, group_far, parent, top_far, places, group_coupling,
              own_pair, top_transfer, transfer, basis):
    wide = lax.axis_index("wide")
    count = rows.shape[0]
    at = lax.broadcasted_iota(jnp.int32, (16, count), 1)
    row = lax.broadcasted_iota(jnp.int32, (16, count), 0)
    kind = at & 3
    chosen = (row == FAR_GROUP + FAR_TOP) & (kind >= 2)
    for slot in range(FAR_GROUP):
        group = group_far[0, slot]
        spot = lax.div(group, 2) * 4 + lax.rem(group, 2)
        chosen = chosen | ((row == slot) & (at == spot))
    own_parent = parent[wide]
    for slot in range(FAR_TOP):
        box = top_far[slot, own_parent]
        chosen = chosen | ((row == FAR_GROUP + slot) & (places[...] == box))
    select = jnp.where(chosen, 1.0, 0.0).astype(jnp.bfloat16)
    gathered = rows[...]
    picked = jnp.zeros((16, LANES), f32)
    for part in range(3):
        piece = gathered.astype(jnp.bfloat16)
        gathered = gathered - piece.astype(f32)
        picked = picked + jnp.dot(select, piece, preferred_element_type=f32)

    def listed(vectors, matrices, slots, first):
        out = times(vectors, matrices[...].reshape(slots * RANK, RANK), True)
        lane = lax.broadcasted_iota(jnp.int32, (16, LANES), 1)
        line = lax.broadcasted_iota(jnp.int32, (16, LANES), 0)
        total = jnp.zeros((16, LANES), f32)
        for two in range(slots // 2):
            own = line == first + 2 * two + jnp.where(lane < RANK, 0, 1)
            total = total + jnp.where(own, out[:, two * LANES : (two + 1) * LANES], 0.0)
        return fold_half(jnp.sum(total, axis=0, keepdims=True))

    top_in = listed(picked[:, RANK:], own_pair, FAR_TOP, FAR_GROUP)
    group_in = listed(picked[:, :RANK], group_coupling, FAR_GROUP, 0)
    group_in = group_in + times(jnp.broadcast_to(top_in, (8, RANK)), top_transfer[lax.rem(wide, 2)], True)
    leaf_in = leaf_far[...] + row_by_leaf(
        [times(group_in, transfer[leaf], True) for leaf in range(LEAVES)]
    )
    far = row_by_leaf([times(leaf_in, basis[leaf], False) for leaf in range(LEAVES)])
    sums = picked[FAR_GROUP + FAR_TOP : FAR_GROUP + FAR_TOP + 1, RANK:]
    return base[...] + far, jnp.sum(sums, axis=1, keepdims=True)


def residual_kernel(*refs):
    *common, observed, packed, residual, scratch = refs
    mapped, _ = far_field(*common)
    field = padded(observed, scratch) - mapped
    residual[...] = field
    pack(field, lane_sums(field * field), common[-1], common[-2], packed)


def second_kernel(*refs):
    *common, residual, packed, first, unit, norm = refs
    mapped, norm_now = far_field(*common)
    first[...] = mapped
    field = mapped * lax.rsqrt(norm_now)
    unit[...] = field
    norm[...] = jnp.broadcast_to(norm_now, norm.shape)
    scalar = lane_sums(residual[...] * mapped)
    pack(field, scalar, common[-1], common[-2], packed)


def third_kernel(*refs):
    *common, residual, first, norm, copies, lower, lower_mapped, step, curve = refs
    mapped, bend = far_field(*common)
    norm_now = norm[:1, :1]
    size = norm_now / bend
    before, image = residual[...], first[...]
    low = before - size * image
    low_mapped = image - (size * jnp.sqrt(norm_now)) * mapped
    lower[...] = low
    lower_mapped[...] = low_mapped
    step[...] = jnp.broadcast_to(size, step.shape)
    curve[...] = jnp.broadcast_to(bend, curve.shape)
    products = [low * low, low * low_mapped, before * low_mapped + low * image]
    sums = jnp.zeros((8, RANK), f32)
    for at, product in enumerate(products):
        sums = jnp.where(rows_of(sums) == at, lane_sums(product), sums)
    sums = jnp.concatenate([sums, jnp.zeros((8, RANK), f32)], axis=1)
    copies[...] = jnp.broadcast_to(sums[None], copies.shape)


def total_kernel(blocks, copies):
    total = blocks[0]
    for device in range(1, blocks.shape[0]):
        total = total + blocks[device]
    copies[...] = jnp.broadcast_to(total[None], copies.shape)


def end_kernel(blocks, warm, residual, first, lower, lower_mapped, norm, step, curve,
               solution_field, last_residual):
    total = blocks[0]
    for device in range(1, blocks.shape[0]):
        total = total + blocks[device]
    total = jnp.sum(total, axis=1, keepdims=True)
    norm_next, bend, cross = total[0:1], total[1:2], total[2:3]
    norm_now, size = norm[:1, :1], step[:1, :1]
    ratio = norm_next / norm_now
    second = norm_next / (bend + ratio * (cross + ratio * curve[:1, :1]))
    keep = slice(0, LEAVES)
    solution_field[...] = warm[...] + size * residual[keep] + second * (
        lower[keep] + ratio * residual[keep]
    )
    last_residual[...] = lower[keep] - second * (lower_mapped[keep] + ratio * first[keep])


def simple(kernel, out_shape, in_specs, scratch=()):
    return pl.pallas_call(
        kernel,
        out_shape=out_shape,
        in_specs=in_specs,
        out_specs=[VMEM] * len(out_shape),
        scratch_shapes=list(scratch),
        cost_estimate=cost(10**6, 10**6),
        compiler_params=pltpu.CompilerParams(vmem_limit_bytes=8 << 20),
    )


def exchange(copies, stride):
    members = copies.shape[0]
    devices = lax.axis_size("wide") * lax.axis_size("narrow")
    span = members * stride
    groups = [
        [base + offset + stride * i for i in range(members)]
        for base in range(0, devices, span)
        for offset in range(stride)
    ]
    return lax.all_to_all(
        copies, ("wide", "narrow"), 0, 0, tiled=True, axis_index_groups=groups
    )


def neighbours(fields):
    wide = lax.axis_size("wide")
    across = []
    for first in range(1, wide - 1, 2):
        across += [(first, first + 1), (first + 1, first)]
    return lax.ppermute(fields, "wide", across)


def local(
    coords,
    noise_var,
    observed,
    warm_start,
    leaf_basis,
    leaf_transfer,
    leaf_coupling,
    group_coupling,
    top_transfer,
    top_coupling,
    near_list,
    near_count,
    far_list,
    far_count,
    group_far,
    parent,
    top_far,
):
    groups = parent.shape[0]
    pairs = groups // 2
    lists = (near_list, near_count, far_list, far_count)
    basis = jnp.transpose(leaf_basis, (0, 2, 1))
    columns = jnp.transpose(coords, (0, 2, 1))
    top_far = top_far.T
    places = jnp.pad(parent.reshape(pairs, 2), ((0, 0), (0, 2)), constant_values=-1)
    places = places.reshape(1, 4 * pairs)
    wide = lax.axis_index("wide")
    tops = lax.dynamic_slice_in_dim(top_transfer, wide // 2 * 2, 2, 0)
    own_pair = lax.dynamic_index_in_dim(
        top_coupling, lax.dynamic_index_in_dim(parent, wide, 0, False), 0, False
    )

    def gather(packed, values, tiles):
        blocks = exchange(packed, 1)
        copies, fields = simple(
            fold_kernel,
            [shape(pairs, 4, LANES), shape(NARROW, packed.shape[1] - 4, LANES)],
            [VMEM] * 2,
        )(blocks, tops)
        extra = neighbours(fields)
        rows = exchange(copies, PAIR).reshape(4 * pairs, LANES)
        out = near_apply(
            lists, blocks, extra, values, noise_var, leaf_coupling, columns, tiles
        )
        base, leaf_far = out[-2:]
        common = (
            rows, base, leaf_far, group_far, parent, top_far, places, group_coupling[0],
            own_pair, tops, leaf_transfer, basis,
        )
        return common, out[0] if tiles is None else tiles

    common_specs = [VMEM] * 3 + [SMEM] * 3 + [VMEM] * 6
    wide_field, packed_shape = shape(8, POINTS), shape(PAIR, PACK, LANES)
    scratch = [pltpu.VMEM((8, POINTS), f32)]
    scalar = shape(8, LANES)

    packed, values = simple(
        begin_kernel,
        [shape(PAIR, PACK + COORDS, LANES), wide_field],
        [VMEM] * 4,
        scratch,
    )(warm_start, coords, basis, leaf_transfer)
    common, tiles = gather(packed, values, None)
    packed, residual = simple(
        residual_kernel, [packed_shape, wide_field], common_specs + [VMEM], scratch
    )(*common, observed)
    common, _ = gather(packed, residual, tiles)
    packed, first, unit, norm = simple(
        second_kernel, [packed_shape, wide_field, wide_field, scalar], common_specs + [VMEM]
    )(*common, residual)
    common, _ = gather(packed, unit, tiles)
    sums, lower, lower_mapped, step, curve = simple(
        third_kernel,
        [shape(PAIR, 8, LANES), wide_field, wide_field, scalar, scalar],
        common_specs + [VMEM] * 3,
    )(*common, residual, first, norm)
    blocks = exchange(sums, 1)
    (copies,) = simple(total_kernel, [shape(pairs, 8, LANES)], [VMEM])(blocks)
    blocks = exchange(copies, PAIR)
    own = shape(LEAVES, POINTS)
    return tuple(
        simple(end_kernel, [own, own], [VMEM] * 9)(
            blocks, warm_start, residual, first, lower, lower_mapped, norm, step, curve
        )
    )


def solution(mesh):
    placed = (
        P(("wide", "narrow"), None, None),
        P(("wide", "narrow"), None),
        P(("wide", "narrow"), None),
        P(("wide", "narrow"), None),
        P(("wide", "narrow"), None, None),
        P(("wide", "narrow"), None, None),
        P(("wide", "narrow"), None, None, None),
        P("wide", None, None, None),
        P(),
        P(),
        P(("wide", "narrow"), None),
        P(("wide", "narrow")),
        P(("wide", "narrow"), None),
        P(("wide", "narrow")),
        P("wide", None),
        P(),
        P(),
    )
    return jax.shard_map(
        local,
        mesh=mesh,
        in_specs=placed,
        out_specs=(P(("wide", "narrow"), None), P(("wide", "narrow"), None)),
        check_vma=False,
    )
```

```python
import functools

import jax
import jax.numpy as jnp
from jax import lax
from jax.experimental import pallas as pl
from jax.experimental.pallas import tpu as pltpu
from jax.sharding import PartitionSpec as P

amplitude = 1.0 / 16.0
rate = 1.7320508075688772 / 1.5
log2_e = 1.4426950408889634
LEAVES = 3
NARROW = 4
GROUP = LEAVES * NARROW
POINTS = 512
RANK = 64
NEAR = 4
FAR = 8
FAR_GROUP = 6
FAR_TOP = 4
LANES = 128
PIECES = POINTS // LANES
FIELD = LEAVES * PIECES
PACK = FIELD + 4
COORDS = 3 * FIELD
PAIR = 2 * NARROW
WINDOW = 3 * GROUP
NEAR_LIST = 0
NEAR_COUNT = NEAR_LIST + LEAVES * NEAR
FAR_LIST = NEAR_COUNT + LEAVES
FAR_COUNT = FAR_LIST + LEAVES * FAR
GROUP_FAR = FAR_COUNT + LEAVES
TOP_FAR = GROUP_FAR + FAR_GROUP
PARENT = TOP_FAR + FAR_TOP
CHUNK = 64
QUARTER = 128
VMEM = pl.BlockSpec(memory_space=pltpu.VMEM)
SMEM = pl.BlockSpec(memory_space=pltpu.SMEM)
HBM = pl.BlockSpec(memory_space=pltpu.HBM)
f32 = jnp.float32


def shape(*dims, dtype=f32):
    return jax.ShapeDtypeStruct(dims, dtype)


def in_hbm(*arrays):
    return tuple(pltpu.with_memory_space_constraint(one, pltpu.HBM) for one in arrays)


def cost(flops, bytes_accessed):
    return pl.CostEstimate(flops=flops, bytes_accessed=bytes_accessed, transcendentals=0)


def rows_of(array):
    return lax.broadcasted_iota(jnp.int32, array.shape, 0)


def times(vectors, matrix, transposed):
    high = vectors.astype(jnp.bfloat16).astype(f32)
    rest = vectors - high
    middle = rest.astype(jnp.bfloat16).astype(f32)
    parts = jnp.concatenate([high, middle, rest - middle], axis=0).astype(jnp.bfloat16)
    dims = (((1,), (1 if transposed else 0,)), ((), ()))
    out = lax.dot_general(parts, matrix, dims, preferred_element_type=f32)
    count = vectors.shape[0]
    return out[:count] + (out[count : 2 * count] + out[2 * count :])


def row_by_leaf(terms):
    out = jnp.zeros_like(terms[0])
    for leaf, term in enumerate(terms):
        out = jnp.where(rows_of(term) == leaf, term, out)
    return out


def fold_half(row):
    return row[:, :RANK] + row[:, RANK:]


def lane_sums(product):
    total = jnp.sum(product, axis=0, keepdims=True)
    total = total[:, :128] + total[:, 128:256] + (total[:, 256:384] + total[:, 384:])
    return fold_half(total)


def pack(values, scalar, basis, transfer, packed):
    for leaf in range(LEAVES):
        for piece in range(PIECES):
            packed[0, pl.ds(leaf * PIECES + piece, 1), :] = values[
                leaf : leaf + 1, piece * LANES : (piece + 1) * LANES
            ]
    coefs = row_by_leaf([times(values, basis[leaf], True) for leaf in range(LEAVES)])
    partial = row_by_leaf([times(coefs, transfer[leaf], False) for leaf in range(LEAVES)])
    partial = jnp.sum(partial, axis=0, keepdims=True)
    empty = jnp.zeros((1, RANK), f32)
    beside = [scalar, empty, empty]
    for leaf in range(LEAVES):
        packed[0, pl.ds(FIELD + leaf, 1), :] = jnp.concatenate(
            [coefs[leaf : leaf + 1], beside[leaf]], axis=1
        )
    packed[0, pl.ds(FIELD + 3, 1), :] = jnp.concatenate([partial, empty], axis=1)
    whole = packed[0]
    for copy in range(1, PAIR):
        packed[copy] = whole


def padded(ref, scratch):
    scratch[...] = jnp.zeros(scratch.shape, f32)
    scratch[0:LEAVES, :] = ref[...]
    return scratch[...]


def fetch(pairs, sems):
    copies = [pltpu.make_async_copy(one, two, sems.at[i]) for i, (one, two) in enumerate(pairs)]
    for copy in copies:
        copy.start()
    return copies


def begin_kernel(warm_in, coords_in, basis_in, transfer_in, packed, values, basis, transfer,
                 warm, coords, scratch, sems):
    pairs = [(warm_in, warm), (coords_in, coords), (basis_in, basis), (transfer_in, transfer)]
    for copy in fetch(pairs, sems):
        copy.wait()
    field = padded(warm, scratch)
    values[...] = field
    for leaf in range(LEAVES):
        for axis in range(3):
            for piece in range(PIECES):
                packed[0, pl.ds(PACK + (leaf * 3 + axis) * PIECES + piece, 1), :] = coords[
                    leaf, axis : axis + 1, piece * LANES : (piece + 1) * LANES
                ]
    pack(field, jnp.zeros((1, RANK), f32), basis, transfer, packed)


def fold_kernel(blocks, top_transfer, copies):
    sums = []
    for row in (FIELD + 3, FIELD):
        for group in range(2):
            first = group * NARROW
            line = [blocks[first + i, row : row + 1, :] for i in range(NARROW)]
            line = (line[0] + line[1]) + (line[2] + line[3])
            if row == FIELD + 3:
                partial = jnp.broadcast_to(line[:, :RANK], (8, RANK))
                lifted = times(partial, top_transfer[group], False)[:1]
                line = jnp.concatenate([line[:, :RANK], lifted], axis=1)
            sums.append(line)
    sums = jnp.concatenate(sums, axis=0)
    copies[...] = jnp.broadcast_to(sums[None], copies.shape)


def selection(table, parent):
    count = 2 * parent.shape[1]
    at = lax.broadcasted_iota(jnp.int32, (16, count), 1)
    row = lax.broadcasted_iota(jnp.int32, (16, count), 0)
    kind = at & 3
    group = lax.broadcasted_iota(jnp.int32, (parent.shape[1], count), 0)
    spot = lax.broadcasted_iota(jnp.int32, (parent.shape[1], count), 1)
    spread = jnp.where((group >> 1) * 4 + (group & 1) == spot, 1.0, 0.0).astype(jnp.bfloat16)
    parents = jnp.broadcast_to(parent[...], (16, parent.shape[1])).astype(f32)
    parents = jnp.dot(parents.astype(jnp.bfloat16), spread, preferred_element_type=f32)
    chosen = (row == FAR_GROUP + FAR_TOP) & (kind >= 2)
    for slot in range(FAR_GROUP):
        one = table[GROUP_FAR + slot]
        chosen = chosen | ((row == slot) & (at == (one >> 1) * 4 + (one & 1)))
    for slot in range(FAR_TOP):
        box = table[TOP_FAR + slot].astype(f32)
        chosen = chosen | ((row == FAR_GROUP + slot) & (kind < 2) & (parents == box))
    return jnp.where(chosen, 1.0, 0.0).astype(jnp.bfloat16)


def near_kernel(evaluate, *refs):
    if evaluate:
        (table, blocks, shifted, values, coords_in, noise_in, coupling_in, group_in, observed_in,
         parent_in, top_in, tiles, base, leaf_far, select, own_pair, noise, coupling, group,
         observed, window, sources, coords, columns, parent, scratch, near, coefs, totals, spread,
         kept, sems, tile_sems) = refs
        wide = lax.axis_index("wide")
        copies = fetch(
            [
                (coords_in, coords), (parent_in, parent), (coupling_in, coupling),
                (noise_in, noise), (group_in, group), (observed_in, observed),
                (top_in.at[table[PARENT]], own_pair),
            ],
            sems,
        )
    else:
        (table, blocks, shifted, values, noise, coupling, tiles, base, leaf_far,
         window, scratch, near, coefs, totals, spread, kept, tile_sems) = refs
        wide = lax.axis_index("wide")
    own = lax.rem(wide, 2)
    first_group = wide - own

    def tile_copy(leaf, quarter):
        part = (pl.ds(leaf * NEAR, NEAR), pl.ds(quarter * QUARTER, QUARTER), slice(None))
        sem = tile_sems.at[leaf * PIECES + quarter]
        if evaluate:
            return pltpu.make_async_copy(kept.at[part], tiles.at[part], sem)
        return pltpu.make_async_copy(tiles.at[part], kept.at[part], sem)

    if not evaluate:
        for leaf in range(LEAVES):
            for quarter in range(PIECES):
                tile_copy(leaf, quarter).start()

    for device in range(PAIR + NARROW):
        for leaf in range(LEAVES):
            at = device * LEAVES + leaf
            if device < PAIR:
                held, index = blocks, device
            else:
                held, index = shifted, own * NARROW + device - PAIR
            window[at] = held[index, leaf * PIECES : (leaf + 1) * PIECES, :]
            if evaluate:
                rows = PACK + leaf * FIELD
                sources[at] = held[index, rows : rows + FIELD, :]

    if evaluate:
        copies[0].wait()
        copies[1].wait()
        for leaf in range(LEAVES):
            columns[leaf] = jnp.transpose(padded(coords.at[leaf], scratch))
        select[...] = selection(table, parent)

    def leaf_step(leaf, _):
        for slot in range(NEAR):
            listed = table[NEAR_LIST + leaf * NEAR + slot]
            used = slot < table[NEAR_COUNT + leaf]
            of_group = lax.div(listed, GROUP)
            turn = of_group - first_group
            turn = jnp.where((turn >= 0) & (turn < 2), turn, 2)
            place = jnp.where(used, turn * GROUP + listed - of_group * GROUP, 0)
            weight = jnp.where(used, 1.0, 0.0).astype(f32)
            field = window[place] * weight
            for piece in range(PIECES):
                spread[slot, piece] = jnp.broadcast_to(field[piece : piece + 1], (8, LANES))
            if evaluate:
                point = sources[place]
                for at in range(FIELD):
                    spread[slot, PIECES + at] = jnp.broadcast_to(point[at : at + 1], (8, LANES))

        def quarter_step(quarter, _):
            if not evaluate:
                tile_copy(leaf, quarter).wait()

            def step(chunk, _):
                start = pl.multiple_of(quarter * QUARTER + chunk * CHUNK, CHUNK)
                acc = jnp.zeros((CHUNK // 8, 8, LANES), f32)
                if evaluate:
                    column = columns[leaf, pl.ds(start, CHUNK), :]
                    target = [
                        jnp.broadcast_to(column[:, axis : axis + 1], (CHUNK, LANES)).reshape(
                            CHUNK // 8, 8, LANES
                        )
                        for axis in range(3)
                    ]
                for slot in range(NEAR):
                    for piece in range(PIECES):
                        cut = slice(piece * LANES, (piece + 1) * LANES)
                        where = (leaf * NEAR + slot, pl.ds(start, CHUNK), cut)
                        if evaluate:
                            squared = None
                            for axis in range(3):
                                source = spread[slot, PIECES + axis * PIECES + piece]
                                between = target[axis] - source[None]
                                between = between * between
                                squared = between if squared is None else squared + between
                            squared = jnp.maximum(squared, 1e-30)
                            distance = squared * lax.rsqrt(squared)
                            decay = jnp.exp2(distance * (-rate * log2_e))
                            tile = (distance * (amplitude * rate) + amplitude) * decay
                            kept[where] = tile.reshape(CHUNK, LANES)
                        else:
                            tile = kept[where].reshape(CHUNK // 8, 8, LANES)
                        acc = acc + tile * spread[slot, piece][None]
                totals[pl.ds(start, CHUNK), :] = acc.reshape(CHUNK, LANES)
                return 0

            lax.fori_loop(0, QUARTER // CHUNK, step, 0)
            if evaluate:
                tile_copy(leaf, quarter).start()
            return 0

        lax.fori_loop(0, PIECES, quarter_step, 0)
        eye = lax.broadcasted_iota(jnp.int32, (LANES, LANES), 0) == lax.broadcasted_iota(
            jnp.int32, (LANES, LANES), 1
        )
        pieces = []
        for piece in range(PIECES):
            column = jnp.sum(totals[piece * LANES : (piece + 1) * LANES, :], axis=1, keepdims=True)
            pieces.append(jnp.sum(jnp.where(eye, column, 0.0), axis=0, keepdims=True))
        near[pl.ds(leaf, 1), :] = jnp.concatenate(pieces, axis=1)
        return 0

    near[...] = jnp.zeros(near.shape, f32)
    lax.fori_loop(0, LEAVES, leaf_step, 0)

    if evaluate:
        for copy in copies[2:]:
            copy.wait()
    coefs[...] = jnp.zeros(coefs.shape, f32)
    for device in range(NARROW):
        coefs[device * LEAVES : (device + 1) * LEAVES, :] = blocks[
            own * NARROW + device, FIELD : FIELD + LEAVES, :
        ]
    lane = lax.broadcasted_iota(jnp.int32, (16, LANES), 1)
    row = lax.broadcasted_iota(jnp.int32, (16, LANES), 0)
    far_rows = []
    for leaf in range(LEAVES):
        out = times(coefs[:, :RANK], coupling[leaf].reshape(FAR * RANK, RANK), True)
        total = jnp.zeros((16, LANES), f32)
        for two in range(FAR // 2):
            at = []
            for slot in (2 * two, 2 * two + 1):
                member = table[FAR_LIST + leaf * FAR + slot] - wide * GROUP
                at.append(jnp.where(slot < table[FAR_COUNT + leaf], member, -1))
            listed = jnp.where(lane < RANK, at[0], at[1]) == row
            total = total + jnp.where(listed, out[:, two * LANES : (two + 1) * LANES], 0.0)
        far_rows.append(fold_half(jnp.sum(total, axis=0, keepdims=True)))
    leaf_far[...] = row_by_leaf([jnp.broadcast_to(one, (8, RANK)) for one in far_rows])
    base[...] = padded(noise, scratch) * values[...] + near[...]
    if evaluate:
        for leaf in range(LEAVES):
            for quarter in range(PIECES):
                tile_copy(leaf, quarter).wait()


def near_apply(evaluate, operands):
    tiles = shape(NEAR * LEAVES, POINTS, POINTS)
    bf16 = jnp.bfloat16
    out_shape = [shape(8, POINTS), shape(8, RANK)]
    out_specs = [VMEM] * 2
    scratch = [pltpu.VMEM((WINDOW, PIECES, LANES), f32)]
    if evaluate:
        out_shape = [pltpu.HBM(tiles.shape, f32)] + out_shape + [
            shape(16, 256 * operands[9].shape[1] // LANES, dtype=bf16),
            shape(FAR_TOP, RANK, RANK, dtype=bf16),
            shape(LEAVES, POINTS),
            shape(LEAVES, FAR, RANK, RANK, dtype=bf16),
            shape(FAR_GROUP, RANK, RANK, dtype=bf16),
            shape(LEAVES, POINTS),
        ]
        out_specs = [HBM] + [VMEM] * 8
        scratch += [
            pltpu.VMEM((WINDOW, FIELD, LANES), f32),
            pltpu.VMEM((LEAVES, 3, POINTS), f32),
            pltpu.VMEM((LEAVES, POINTS, 8), f32),
            pltpu.VMEM(operands[9].shape, jnp.int32),
        ]
    scratch += [
        pltpu.VMEM((8, POINTS), f32),
        pltpu.VMEM((8, POINTS), f32),
        pltpu.VMEM((16, LANES), f32),
        pltpu.VMEM((POINTS, LANES), f32),
        pltpu.VMEM((NEAR, PIECES + FIELD, 8, LANES), f32),
        pltpu.VMEM(tiles.shape, f32),
    ]
    if evaluate:
        scratch.append(pltpu.SemaphoreType.DMA((7,)))
    scratch.append(pltpu.SemaphoreType.DMA((LEAVES * PIECES,)))
    places = [HBM] * 7 if evaluate else [VMEM, VMEM, HBM]
    return pl.pallas_call(
        functools.partial(near_kernel, evaluate),
        out_shape=out_shape,
        in_specs=[SMEM] + [VMEM] * 3 + places,
        out_specs=out_specs,
        scratch_shapes=scratch,
        cost_estimate=cost(3 * 10**8 if evaluate else 3 * 10**7, 2 * 10**7),
        compiler_params=pltpu.CompilerParams(vmem_limit_bytes=24 << 20),
    )(*operands)


def far_field(rows, base, leaf_far, select, group_coupling, own_pair, top_transfer, transfer,
              basis):
    wide = lax.axis_index("wide")
    gathered = rows[...]
    picked = jnp.zeros((16, LANES), f32)
    for part in range(3):
        piece = gathered.astype(jnp.bfloat16)
        gathered = gathered - piece.astype(f32)
        picked = picked + jnp.dot(select[...], piece, preferred_element_type=f32)

    def listed(vectors, matrices, slots, first):
        out = times(vectors, matrices[...].reshape(slots * RANK, RANK), True)
        lane = lax.broadcasted_iota(jnp.int32, (16, LANES), 1)
        line = lax.broadcasted_iota(jnp.int32, (16, LANES), 0)
        total = jnp.zeros((16, LANES), f32)
        for two in range(slots // 2):
            own = line == first + 2 * two + jnp.where(lane < RANK, 0, 1)
            total = total + jnp.where(own, out[:, two * LANES : (two + 1) * LANES], 0.0)
        return fold_half(jnp.sum(total, axis=0, keepdims=True))

    top_in = listed(picked[:, RANK:], own_pair, FAR_TOP, FAR_GROUP)
    group_in = listed(picked[:, :RANK], group_coupling, FAR_GROUP, 0)
    group_in = group_in + times(jnp.broadcast_to(top_in, (8, RANK)), top_transfer[lax.rem(wide, 2)], True)
    leaf_in = leaf_far[...] + row_by_leaf(
        [times(group_in, transfer[leaf], True) for leaf in range(LEAVES)]
    )
    far = row_by_leaf([times(leaf_in, basis[leaf], False) for leaf in range(LEAVES)])
    sums = picked[FAR_GROUP + FAR_TOP : FAR_GROUP + FAR_TOP + 1, RANK:]
    return base[...] + far, jnp.sum(sums, axis=1, keepdims=True)


def residual_kernel(*refs):
    *common, observed, packed, residual, scratch = refs
    mapped, _ = far_field(*common)
    field = padded(observed, scratch) - mapped
    residual[...] = field
    pack(field, lane_sums(field * field), common[-1], common[-2], packed)


def second_kernel(*refs):
    *common, residual, packed, first, unit, norm = refs
    mapped, norm_now = far_field(*common)
    first[...] = mapped
    field = mapped * lax.rsqrt(norm_now)
    unit[...] = field
    norm[...] = jnp.broadcast_to(norm_now, norm.shape)
    scalar = lane_sums(residual[...] * mapped)
    pack(field, scalar, common[-1], common[-2], packed)


def third_kernel(*refs):
    *common, residual, first, norm, copies, lower, lower_mapped, step, curve = refs
    mapped, bend = far_field(*common)
    norm_now = norm[:1, :1]
    size = norm_now / bend
    before, image = residual[...], first[...]
    low = before - size * image
    low_mapped = image - (size * jnp.sqrt(norm_now)) * mapped
    lower[...] = low
    lower_mapped[...] = low_mapped
    step[...] = jnp.broadcast_to(size, step.shape)
    curve[...] = jnp.broadcast_to(bend, curve.shape)
    products = [low * low, low * low_mapped, before * low_mapped + low * image]
    sums = [lane_sums(product) for product in products] + [jnp.zeros((1, RANK), f32)]
    first_row = jnp.concatenate(sums[:2], axis=1)
    second_row = jnp.concatenate(sums[2:], axis=1)
    block = jnp.broadcast_to(first_row, (8, LANES))
    block = jnp.where(rows_of(block) == 0, block, second_row)
    copies[...] = jnp.broadcast_to(block[None], copies.shape)


def total_kernel(blocks, copies):
    total = blocks[0]
    for device in range(1, blocks.shape[0]):
        total = total + blocks[device]
    copies[...] = jnp.broadcast_to(total[:2][None], copies.shape)


def step_kernel(warm, residual, step, moved):
    moved[...] = warm[...] + step[:1, :1] * residual[...]


def end_kernel(blocks, moved, residual, first, lower, lower_mapped, norm, curve,
               solution_field, last_residual):
    total = jnp.sum(blocks[...], axis=0)
    norm_next = jnp.sum(total[:1, :RANK], axis=1, keepdims=True)
    bend = jnp.sum(total[:1, RANK:], axis=1, keepdims=True)
    cross = jnp.sum(total[1:2, :RANK], axis=1, keepdims=True)
    norm_now = norm[:1, :1]
    ratio = norm_next / norm_now
    second = norm_next / (bend + ratio * (cross + ratio * curve[:1, :1]))
    keep = slice(0, LEAVES)
    solution_field[...] = moved[keep] + second * (lower[keep] + ratio * residual[keep])
    last_residual[...] = lower[keep] - second * (lower_mapped[keep] + ratio * first[keep])


def simple(kernel, out_shape, in_specs, scratch=()):
    return pl.pallas_call(
        kernel,
        out_shape=out_shape,
        in_specs=in_specs,
        out_specs=[VMEM] * len(out_shape),
        scratch_shapes=list(scratch),
        cost_estimate=cost(10**6, 10**6),
        compiler_params=pltpu.CompilerParams(vmem_limit_bytes=8 << 20),
    )


def exchange(copies, stride, shift=0):
    members = copies.shape[0]
    devices = lax.axis_size("wide") * lax.axis_size("narrow")
    span = members * stride
    groups = [
        [(base + offset + stride * i + shift) % devices for i in range(members)]
        for base in range(0, devices, span)
        for offset in range(stride)
    ]
    return lax.all_to_all(
        copies, ("wide", "narrow"), 0, 0, tiled=True, axis_index_groups=groups
    )


def local(
    coords,
    noise_var,
    observed,
    warm_start,
    leaf_basis,
    leaf_transfer,
    leaf_coupling,
    group_coupling,
    top_transfer,
    top_coupling,
    near_list,
    near_count,
    far_list,
    far_count,
    group_far,
    parent,
    top_far,
):
    groups = parent.shape[0]
    pairs = groups // 2
    wide = lax.axis_index("wide")
    own_parent = lax.dynamic_slice_in_dim(parent, wide, 1, 0)
    own_tops = lax.dynamic_slice_in_dim(top_far, own_parent[0], 1, 0)
    table = [near_list, near_count, far_list, far_count, group_far, own_tops, own_parent]
    table = jnp.concatenate([one.reshape(-1) for one in table])
    tops = lax.dynamic_slice_in_dim(top_transfer, wide // 2 * 2, 2, 0)
    field, scalar = shape(8, POINTS), shape(8, LANES)
    packed_shape = shape(PAIR, PACK, LANES)
    scratch = [pltpu.VMEM((8, POINTS), f32)]

    def gather(packed, rest, evaluate):
        blocks = exchange(packed, 1)
        shifted = exchange(packed, 1, NARROW)
        (copies,) = simple(fold_kernel, [shape(pairs, 4, LANES)], [VMEM] * 2)(blocks, tops)
        rows = exchange(copies, PAIR).reshape(4 * pairs, LANES)
        return rows, near_apply(evaluate, (table, blocks, shifted) + rest)

    packed, values, basis, transfer = simple(
        begin_kernel,
        [
            shape(PAIR, PACK + COORDS, LANES),
            field,
            shape(LEAVES, RANK, POINTS, dtype=jnp.bfloat16),
            shape(LEAVES, RANK, RANK, dtype=jnp.bfloat16),
        ],
        [HBM] * 4,
        [pltpu.VMEM((LEAVES, POINTS), f32), pltpu.VMEM((LEAVES, 3, POINTS), f32)]
        + scratch
        + [pltpu.SemaphoreType.DMA((4,))],
    )(*in_hbm(warm_start, coords, jnp.transpose(leaf_basis, (0, 2, 1)), leaf_transfer))
    rows, near = gather(
        packed,
        (values,)
        + in_hbm(
            coords, noise_var, leaf_coupling, group_coupling[0], observed,
            parent.reshape(1, groups), top_coupling,
        ),
        True,
    )
    tiles, base, leaf_far, select, own_pair, noise, coupling, group, observed = near
    far_data = (select, group, own_pair, tops, transfer, basis)
    packed, residual = simple(
        residual_kernel, [packed_shape, field], [VMEM] * 10, scratch
    )(rows, base, leaf_far, *far_data, observed)

    rows, near = gather(packed, (residual, noise, coupling) + in_hbm(tiles), False)
    packed, first, unit, norm = simple(
        second_kernel, [packed_shape, field, field, scalar], [VMEM] * 10
    )(rows, *near, *far_data, residual)

    rows, near = gather(packed, (unit, noise, coupling) + in_hbm(tiles), False)
    sums, lower, lower_mapped, step, curve = simple(
        third_kernel,
        [shape(PAIR, 8, LANES), field, field, scalar, scalar],
        [VMEM] * 12,
    )(rows, *near, *far_data, residual, first, norm)
    blocks = exchange(sums, 1)
    (copies,) = simple(total_kernel, [shape(pairs, 2, LANES)], [VMEM])(blocks)
    blocks = exchange(copies, PAIR)
    (moved,) = simple(step_kernel, [field], [VMEM] * 3)(values, residual, step)
    own = shape(LEAVES, POINTS)
    return tuple(
        simple(end_kernel, [own, own], [VMEM] * 8)(
            blocks, moved, residual, first, lower, lower_mapped, norm, curve
        )
    )


def solution(mesh):
    placed = (
        P(("wide", "narrow"), None, None),
        P(("wide", "narrow"), None),
        P(("wide", "narrow"), None),
        P(("wide", "narrow"), None),
        P(("wide", "narrow"), None, None),
        P(("wide", "narrow"), None, None),
        P(("wide", "narrow"), None, None, None),
        P("wide", None, None, None),
        P(),
        P(),
        P(("wide", "narrow"), None),
        P(("wide", "narrow")),
        P(("wide", "narrow"), None),
        P(("wide", "narrow")),
        P("wide", None),
        P(),
        P(),
    )
    return jax.shard_map(
        local,
        mesh=mesh,
        in_specs=placed,
        out_specs=(P(("wide", "narrow"), None), P(("wide", "narrow"), None)),
        check_vma=False,
    )
```

```python
import functools

import jax
import jax.numpy as jnp
from jax import lax
from jax.experimental import pallas as pl
from jax.experimental.pallas import tpu as pltpu
from jax.sharding import PartitionSpec as P

amplitude = 1.0 / 16.0
rate = 1.7320508075688772 / 1.5
log2_e = 1.4426950408889634
LEAVES = 3
NARROW = 4
GROUP = LEAVES * NARROW
POINTS = 512
RANK = 64
NEAR = 4
FAR = 8
FAR_GROUP = 6
FAR_TOP = 4
LANES = 128
PIECES = POINTS // LANES
FIELD = LEAVES * PIECES
PACK = FIELD + 4
COORDS = 3 * FIELD
PAIR = 2 * NARROW
WINDOW = 3 * GROUP
CHUNK = 64
QUARTER = 128
VMEM = pl.BlockSpec(memory_space=pltpu.VMEM)
HBM = pl.BlockSpec(memory_space=pltpu.HBM)
f32 = jnp.float32


def shape(*dims, dtype=f32):
    return jax.ShapeDtypeStruct(dims, dtype)


def in_hbm(*arrays):
    return tuple(pltpu.with_memory_space_constraint(one, pltpu.HBM) for one in arrays)


def cost(flops, bytes_accessed):
    return pl.CostEstimate(flops=flops, bytes_accessed=bytes_accessed, transcendentals=0)


def rows_of(array):
    return lax.broadcasted_iota(jnp.int32, array.shape, 0)


def times(vectors, matrix, transposed):
    high = vectors.astype(jnp.bfloat16).astype(f32)
    rest = vectors - high
    middle = rest.astype(jnp.bfloat16).astype(f32)
    parts = jnp.concatenate([high, middle, rest - middle], axis=0).astype(jnp.bfloat16)
    dims = (((1,), (1 if transposed else 0,)), ((), ()))
    out = lax.dot_general(parts, matrix, dims, preferred_element_type=f32)
    count = vectors.shape[0]
    return out[:count] + (out[count : 2 * count] + out[2 * count :])


def row_by_leaf(terms):
    out = jnp.zeros_like(terms[0])
    for leaf, term in enumerate(terms):
        out = jnp.where(rows_of(term) == leaf, term, out)
    return out


def fold_half(row):
    return row[:, :RANK] + row[:, RANK:]


def lane_sums(product):
    total = jnp.sum(product, axis=0, keepdims=True)
    total = total[:, :128] + total[:, 128:256] + (total[:, 256:384] + total[:, 384:])
    return fold_half(total)


def pack(values, scalar, basis, transfer, packed):
    for leaf in range(LEAVES):
        for piece in range(PIECES):
            packed[0, pl.ds(leaf * PIECES + piece, 1), :] = values[
                leaf : leaf + 1, piece * LANES : (piece + 1) * LANES
            ]
    coefs = row_by_leaf([times(values, basis[leaf], True) for leaf in range(LEAVES)])
    partial = row_by_leaf([times(coefs, transfer[leaf], False) for leaf in range(LEAVES)])
    partial = jnp.sum(partial, axis=0, keepdims=True)
    empty = jnp.zeros((1, RANK), f32)
    beside = [scalar, empty, empty]
    for leaf in range(LEAVES):
        packed[0, pl.ds(FIELD + leaf, 1), :] = jnp.concatenate(
            [coefs[leaf : leaf + 1], beside[leaf]], axis=1
        )
    packed[0, pl.ds(FIELD + 3, 1), :] = jnp.concatenate([partial, empty], axis=1)
    whole = packed[0]
    for copy in range(1, PAIR):
        packed[copy] = whole


def padded(ref, scratch):
    scratch[...] = jnp.zeros(scratch.shape, f32)
    scratch[0:LEAVES, :] = ref[...]
    return scratch[...]


def fetch(pairs, sems):
    copies = [pltpu.make_async_copy(one, two, sems.at[i]) for i, (one, two) in enumerate(pairs)]
    for copy in copies:
        copy.start()
    return copies


def begin_kernel(warm_in, coords_in, basis_in, transfer_in, packed, values, basis, transfer,
                 warm, coords, scratch, sems):
    pairs = [(warm_in, warm), (coords_in, coords), (basis_in, basis), (transfer_in, transfer)]
    for copy in fetch(pairs, sems):
        copy.wait()
    field = padded(warm, scratch)
    values[...] = field
    for leaf in range(LEAVES):
        for axis in range(3):
            for piece in range(PIECES):
                packed[0, pl.ds(PACK + (leaf * 3 + axis) * PIECES + piece, 1), :] = coords[
                    leaf, axis : axis + 1, piece * LANES : (piece + 1) * LANES
                ]
    pack(field, jnp.zeros((1, RANK), f32), basis, transfer, packed)


def fold_kernel(blocks, top_transfer, copies, fields):
    sums = []
    for row in (FIELD + 3, FIELD):
        for group in range(2):
            first = group * NARROW
            line = [blocks[first + i, row : row + 1, :] for i in range(NARROW)]
            line = (line[0] + line[1]) + (line[2] + line[3])
            if row == FIELD + 3:
                partial = jnp.broadcast_to(line[:, :RANK], (8, RANK))
                lifted = times(partial, top_transfer[group], False)[:1]
                line = jnp.concatenate([line[:, :RANK], lifted], axis=1)
            sums.append(line)
    sums = jnp.concatenate(sums, axis=0)
    copies[...] = jnp.broadcast_to(sums[None], copies.shape)
    own = lax.rem(lax.axis_index("wide"), 2)
    for i in range(NARROW):
        device = own * NARROW + i
        fields[i, 0:FIELD, :] = blocks[device, 0:FIELD, :]
        if fields.shape[1] > FIELD:
            fields[i, FIELD:, :] = blocks[device, PACK:, :]


def selection(group_far, top_far, own_parent, parent):
    count = 2 * parent.shape[1]
    at = lax.broadcasted_iota(jnp.int32, (16, count), 1)
    row = lax.broadcasted_iota(jnp.int32, (16, count), 0)
    kind = at & 3
    group = lax.broadcasted_iota(jnp.int32, (parent.shape[1], count), 0)
    spot = lax.broadcasted_iota(jnp.int32, (parent.shape[1], count), 1)
    spread = jnp.where((group >> 1) * 4 + (group & 1) == spot, 1.0, 0.0).astype(jnp.bfloat16)
    parents = jnp.broadcast_to(parent[...], (16, parent.shape[1])).astype(f32)
    parents = jnp.dot(parents.astype(jnp.bfloat16), spread, preferred_element_type=f32)
    chosen = (row == FAR_GROUP + FAR_TOP) & (kind >= 2)
    for slot in range(FAR_GROUP):
        one = group_far[0, slot]
        chosen = chosen | ((row == slot) & (at == (one >> 1) * 4 + (one & 1)))
    for slot in range(FAR_TOP):
        box = top_far[slot, own_parent].astype(f32)
        chosen = chosen | ((row == FAR_GROUP + slot) & (kind < 2) & (parents == box))
    return jnp.where(chosen, 1.0, 0.0).astype(jnp.bfloat16)


def tile_copy(evaluate, slots, kept, tiles, sems, leaf, quarter):
    part = (pl.ds(leaf * slots, slots), pl.ds(quarter * QUARTER, QUARTER), slice(None))
    source, target = (kept, tiles) if evaluate else (tiles, kept)
    return pltpu.make_async_copy(source.at[part], target.at[part], sems.at[leaf * PIECES + quarter])


def begin_tiles(slots, kept, tiles, sems):
    for leaf in range(LEAVES):
        for quarter in range(PIECES):
            tile_copy(False, slots, kept, tiles, sems, leaf, quarter).start()


def tile_products(evaluate, slots, fill, near, columns, spread, totals, kept, tiles, sems):
    def leaf_step(leaf, _):
        for slot in range(slots):
            field, point = fill(leaf, slot)
            for piece in range(PIECES):
                spread[slot, piece] = jnp.broadcast_to(field(piece), (8, LANES))
            if evaluate:
                for at in range(FIELD):
                    spread[slot, PIECES + at] = jnp.broadcast_to(point(at), (8, LANES))

        def quarter_step(quarter, _):
            if not evaluate:
                tile_copy(False, slots, kept, tiles, sems, leaf, quarter).wait()

            def step(chunk, _):
                start = pl.multiple_of(quarter * QUARTER + chunk * CHUNK, CHUNK)
                acc = jnp.zeros((CHUNK // 8, 8, LANES), f32)
                if evaluate:
                    column = columns[leaf, pl.ds(start, CHUNK), :]
                    target = [
                        jnp.broadcast_to(column[:, axis : axis + 1], (CHUNK, LANES)).reshape(
                            CHUNK // 8, 8, LANES
                        )
                        for axis in range(3)
                    ]
                for slot in range(slots):
                    for piece in range(PIECES):
                        cut = slice(piece * LANES, (piece + 1) * LANES)
                        where = (leaf * slots + slot, pl.ds(start, CHUNK), cut)
                        if evaluate:
                            squared = None
                            for axis in range(3):
                                source = spread[slot, PIECES + axis * PIECES + piece]
                                between = target[axis] - source[None]
                                between = between * between
                                squared = between if squared is None else squared + between
                            squared = jnp.maximum(squared, 1e-30)
                            distance = squared * lax.rsqrt(squared)
                            decay = jnp.exp2(distance * (-rate * log2_e))
                            tile = (distance * (amplitude * rate) + amplitude) * decay
                            kept[where] = tile.reshape(CHUNK, LANES)
                        else:
                            tile = kept[where].reshape(CHUNK // 8, 8, LANES)
                        acc = acc + tile * spread[slot, piece][None]
                totals[pl.ds(start, CHUNK), :] = acc.reshape(CHUNK, LANES)
                return 0

            lax.fori_loop(0, QUARTER // CHUNK, step, 0)
            if evaluate:
                tile_copy(True, slots, kept, tiles, sems, leaf, quarter).start()
            return 0

        lax.fori_loop(0, PIECES, quarter_step, 0)
        eye = lax.broadcasted_iota(jnp.int32, (LANES, LANES), 0) == lax.broadcasted_iota(
            jnp.int32, (LANES, LANES), 1
        )
        pieces = []
        for piece in range(PIECES):
            column = jnp.sum(totals[piece * LANES : (piece + 1) * LANES, :], axis=1, keepdims=True)
            pieces.append(jnp.sum(jnp.where(eye, column, 0.0), axis=0, keepdims=True))
        near[pl.ds(leaf, 1), :] = jnp.concatenate(pieces, axis=1)
        return 0

    near[...] = jnp.zeros(near.shape, f32)
    lax.fori_loop(0, LEAVES, leaf_step, 0)


def end_tiles(slots, kept, tiles, sems):
    for leaf in range(LEAVES):
        for quarter in range(PIECES):
            tile_copy(True, slots, kept, tiles, sems, leaf, quarter).wait()


def own_kernel(evaluate, *refs):
    if evaluate:
        values, coords_in, tiles, own_near, coords, columns, scratch, sem, *loop = refs
        (copy,) = fetch([(coords_in, coords)], sem)
        copy.wait()
        for leaf in range(LEAVES):
            columns[leaf] = jnp.transpose(padded(coords.at[leaf], scratch))
    else:
        values, tiles, own_near, *loop = refs
        coords = columns = None
    spread, totals, kept, sems = loop
    if not evaluate:
        begin_tiles(1, kept, tiles, sems)

    def fill(leaf, slot):
        def field(piece):
            part = values[:, piece * LANES : (piece + 1) * LANES]
            return jnp.sum(jnp.where(rows_of(part) == leaf, part, 0.0), axis=0, keepdims=True)

        def point(at):
            axis, piece = divmod(at, PIECES)
            return coords[leaf, axis : axis + 1, piece * LANES : (piece + 1) * LANES]

        return field, point

    tile_products(evaluate, 1, fill, own_near, columns, spread, totals, kept, tiles, sems)
    if evaluate:
        end_tiles(1, kept, tiles, sems)


def near_kernel(evaluate, *refs):
    if evaluate:
        (near_list_in, near_count_in, far_list_in, far_count_in, blocks, extra, values, own_near,
         coords_in, noise_in, coupling_in, group_in, observed_in, parent_in, parents_in,
         group_far_in, top_far_in, top_in, tiles, base, leaf_far, select, own_pair, noise,
         coupling, group, observed, near_list, near_count, far_list, far_count, sems, window,
         sources, coords, columns, parent, parents, group_far, top_far, scratch, near, coefs,
         spread, totals, kept, tile_sems) = refs
    else:
        (near_list_in, near_count_in, far_list_in, far_count_in, blocks, extra, values, own_near,
         noise, coupling, tiles, base, leaf_far, near_list, near_count, far_list, far_count, sems,
         window, scratch, near, coefs, spread, totals, kept, tile_sems) = refs
    slots = NEAR - 1
    pairs = [
        (near_list_in, near_list), (near_count_in, near_count),
        (far_list_in, far_list), (far_count_in, far_count),
    ]
    if evaluate:
        pairs += [
            (parent_in, parent), (group_far_in, group_far), (top_far_in, top_far),
            (parents_in, parents), (coords_in, coords), (coupling_in, coupling),
            (noise_in, noise), (group_in, group), (observed_in, observed),
        ]
    copies = fetch(pairs, sems)
    if not evaluate:
        begin_tiles(slots, kept, tiles, tile_sems)
    wide = lax.axis_index("wide")
    own = lax.rem(wide, 2)
    first_group = wide - own
    for device in range(PAIR + NARROW):
        held, index = (blocks, device) if device < PAIR else (extra, device - PAIR)
        more = PACK if device < PAIR else FIELD
        for leaf in range(LEAVES):
            at = device * LEAVES + leaf
            window[at] = held[index, leaf * PIECES : (leaf + 1) * PIECES, :]
            if evaluate:
                rows = more + leaf * FIELD
                sources[at] = held[index, rows : rows + FIELD, :]
    coefs[...] = jnp.zeros(coefs.shape, f32)
    for device in range(NARROW):
        coefs[device * LEAVES : (device + 1) * LEAVES, :] = blocks[
            own * NARROW + device, FIELD : FIELD + LEAVES, :
        ]
    for copy in copies:
        copy.wait()
    if evaluate:
        own_parent = parent[wide]
        top_copy = pltpu.make_async_copy(top_in.at[own_parent], own_pair, sems.at[0])
        top_copy.start()
        for leaf in range(LEAVES):
            columns[leaf] = jnp.transpose(padded(coords.at[leaf], scratch))
        select[...] = selection(group_far, top_far, own_parent, parents)

    lane = lax.broadcasted_iota(jnp.int32, (16, LANES), 1)
    row = lax.broadcasted_iota(jnp.int32, (16, LANES), 0)
    far_rows = []
    for leaf in range(LEAVES):
        out = times(coefs[:, :RANK], coupling[leaf].reshape(FAR * RANK, RANK), True)
        total = jnp.zeros((16, LANES), f32)
        for two in range(FAR // 2):
            at = []
            for slot in (2 * two, 2 * two + 1):
                member = far_list[leaf, slot] - wide * GROUP
                at.append(jnp.where(slot < far_count[leaf], member, -1))
            listed = jnp.where(lane < RANK, at[0], at[1]) == row
            total = total + jnp.where(listed, out[:, two * LANES : (two + 1) * LANES], 0.0)
        far_rows.append(fold_half(jnp.sum(total, axis=0, keepdims=True)))
    leaf_far[...] = row_by_leaf([jnp.broadcast_to(one, (8, RANK)) for one in far_rows])
    local_part = padded(noise, scratch) * values[...] + own_near[...]

    def fill(leaf, slot):
        listed = near_list[leaf, slot + 1]
        used = slot + 1 < near_count[leaf]
        of_group = lax.div(listed, GROUP)
        turn = of_group - first_group
        turn = jnp.where((turn >= 0) & (turn < 2), turn, 2)
        place = jnp.where(used, turn * GROUP + listed - of_group * GROUP, 0)
        field = window[place] * jnp.where(used, 1.0, 0.0).astype(f32)
        points = sources[place] if evaluate else None
        return lambda piece: field[piece : piece + 1], lambda at: points[at : at + 1]

    tile_products(
        evaluate, slots, fill, near, columns if evaluate else None, spread, totals, kept, tiles,
        tile_sems,
    )
    base[...] = local_part + near[...]
    if evaluate:
        top_copy.wait()
        end_tiles(slots, kept, tiles, tile_sems)


def loop_scratch(slots):
    return [
        pltpu.VMEM((slots, PIECES + FIELD, 8, LANES), f32),
        pltpu.VMEM((POINTS, LANES), f32),
        pltpu.VMEM((slots * LEAVES, POINTS, POINTS), f32),
        pltpu.SemaphoreType.DMA((LEAVES * PIECES,)),
    ]


def column_scratch():
    return [pltpu.VMEM((LEAVES, 3, POINTS), f32), pltpu.VMEM((LEAVES, POINTS, 8), f32)]


def own_apply(evaluate, values, other):
    out_shape, out_specs, scratch = [shape(8, POINTS)], [VMEM], []
    if evaluate:
        out_shape = [pltpu.HBM((LEAVES, POINTS, POINTS), f32)] + out_shape
        out_specs = [HBM] + out_specs
        scratch = column_scratch() + [
            pltpu.VMEM((8, POINTS), f32), pltpu.SemaphoreType.DMA((1,))
        ]
    return pl.pallas_call(
        functools.partial(own_kernel, evaluate),
        out_shape=out_shape,
        in_specs=[VMEM, HBM],
        out_specs=out_specs,
        scratch_shapes=scratch + loop_scratch(1),
        cost_estimate=cost(10**8, 4 * 10**6),
        compiler_params=pltpu.CompilerParams(vmem_limit_bytes=16 << 20),
    )(values, *in_hbm(other))


def near_apply(evaluate, lists, near_data, other):
    bf16 = jnp.bfloat16
    slots = NEAR - 1
    smem = [
        pltpu.SMEM((LEAVES, NEAR), jnp.int32),
        pltpu.SMEM((LEAVES,), jnp.int32),
        pltpu.SMEM((LEAVES, FAR), jnp.int32),
        pltpu.SMEM((LEAVES,), jnp.int32),
    ]
    out_shape = [shape(8, POINTS), shape(8, RANK)]
    out_specs = [VMEM] * 2
    scratch = smem + [
        pltpu.SemaphoreType.DMA((13 if evaluate else 4,)),
        pltpu.VMEM((WINDOW, PIECES, LANES), f32),
    ]
    if evaluate:
        groups = other[5].shape[0]
        out_shape = [pltpu.HBM((slots * LEAVES, POINTS, POINTS), f32)] + out_shape + [
            shape(16, 2 * groups, dtype=bf16),
            shape(FAR_TOP, RANK, RANK, dtype=bf16),
            shape(LEAVES, POINTS),
            shape(LEAVES, FAR, RANK, RANK, dtype=bf16),
            shape(FAR_GROUP, RANK, RANK, dtype=bf16),
            shape(LEAVES, POINTS),
        ]
        out_specs = [HBM] + [VMEM] * 8
        scratch += [pltpu.VMEM((WINDOW, FIELD, LANES), f32)] + column_scratch() + [
            pltpu.SMEM((groups,), jnp.int32),
            pltpu.VMEM((1, groups), jnp.int32),
            pltpu.SMEM((1, FAR_GROUP), jnp.int32),
            pltpu.SMEM(other[8].shape, jnp.int32),
        ]
    scratch += [
        pltpu.VMEM((8, POINTS), f32),
        pltpu.VMEM((8, POINTS), f32),
        pltpu.VMEM((16, LANES), f32),
    ] + loop_scratch(slots)
    places = [HBM] * 10 if evaluate else [VMEM, VMEM, HBM]
    other = in_hbm(*other) if evaluate else other[:2] + in_hbm(*other[2:])
    return pl.pallas_call(
        functools.partial(near_kernel, evaluate),
        out_shape=out_shape,
        in_specs=[HBM] * 4 + [VMEM] * 4 + places,
        out_specs=out_specs,
        scratch_shapes=scratch,
        cost_estimate=cost(3 * 10**8, 2 * 10**7),
        compiler_params=pltpu.CompilerParams(vmem_limit_bytes=24 << 20),
    )(*in_hbm(*lists), *near_data, *other)


def far_field(rows, base, leaf_far, select, group_coupling, own_pair, top_transfer, transfer,
              basis):
    wide = lax.axis_index("wide")
    gathered = rows[...]
    picked = jnp.zeros((16, LANES), f32)
    for part in range(3):
        piece = gathered.astype(jnp.bfloat16)
        gathered = gathered - piece.astype(f32)
        picked = picked + jnp.dot(select[...], piece, preferred_element_type=f32)

    def listed(vectors, matrices, slots, first):
        out = times(vectors, matrices[...].reshape(slots * RANK, RANK), True)
        lane = lax.broadcasted_iota(jnp.int32, (16, LANES), 1)
        line = lax.broadcasted_iota(jnp.int32, (16, LANES), 0)
        total = jnp.zeros((16, LANES), f32)
        for two in range(slots // 2):
            own = line == first + 2 * two + jnp.where(lane < RANK, 0, 1)
            total = total + jnp.where(own, out[:, two * LANES : (two + 1) * LANES], 0.0)
        return fold_half(jnp.sum(total, axis=0, keepdims=True))

    top_in = listed(picked[:, RANK:], own_pair, FAR_TOP, FAR_GROUP)
    group_in = listed(picked[:, :RANK], group_coupling, FAR_GROUP, 0)
    group_in = group_in + times(jnp.broadcast_to(top_in, (8, RANK)), top_transfer[lax.rem(wide, 2)], True)
    leaf_in = leaf_far[...] + row_by_leaf(
        [times(group_in, transfer[leaf], True) for leaf in range(LEAVES)]
    )
    far = row_by_leaf([times(leaf_in, basis[leaf], False) for leaf in range(LEAVES)])
    sums = picked[FAR_GROUP + FAR_TOP : FAR_GROUP + FAR_TOP + 1, RANK:]
    return base[...] + far, jnp.sum(sums, axis=1, keepdims=True)


def residual_kernel(*refs):
    *common, observed, packed, residual, scratch = refs
    mapped, _ = far_field(*common)
    field = padded(observed, scratch) - mapped
    residual[...] = field
    pack(field, lane_sums(field * field), common[-1], common[-2], packed)


def second_kernel(*refs):
    *common, residual, packed, first, unit, norm = refs
    mapped, norm_now = far_field(*common)
    first[...] = mapped
    field = mapped * lax.rsqrt(norm_now)
    unit[...] = field
    norm[...] = jnp.broadcast_to(norm_now, norm.shape)
    scalar = lane_sums(residual[...] * mapped)
    pack(field, scalar, common[-1], common[-2], packed)


def third_kernel(*refs):
    *common, residual, first, norm, copies, lower, lower_mapped, step, curve = refs
    mapped, bend = far_field(*common)
    norm_now = norm[:1, :1]
    size = norm_now / bend
    before, image = residual[...], first[...]
    low = before - size * image
    low_mapped = image - (size * jnp.sqrt(norm_now)) * mapped
    lower[...] = low
    lower_mapped[...] = low_mapped
    step[...] = jnp.broadcast_to(size, step.shape)
    curve[...] = jnp.broadcast_to(bend, curve.shape)
    products = [low * low, low * low_mapped, before * low_mapped + low * image]
    sums = [lane_sums(product) for product in products] + [jnp.zeros((1, RANK), f32)]
    first_row = jnp.concatenate(sums[:2], axis=1)
    second_row = jnp.concatenate(sums[2:], axis=1)
    block = jnp.broadcast_to(first_row, (8, LANES))
    block = jnp.where(rows_of(block) == 0, block, second_row)
    copies[...] = jnp.broadcast_to(block[None], copies.shape)


def total_kernel(blocks, copies):
    total = blocks[0]
    for device in range(1, blocks.shape[0]):
        total = total + blocks[device]
    copies[...] = jnp.broadcast_to(total[:2][None], copies.shape)


def step_kernel(warm, residual, step, moved):
    moved[...] = warm[...] + step[:1, :1] * residual[...]


def end_kernel(blocks, moved, residual, first, lower, lower_mapped, norm, curve,
               solution_field, last_residual):
    total = jnp.sum(blocks[...], axis=0)
    norm_next = jnp.sum(total[:1, :RANK], axis=1, keepdims=True)
    bend = jnp.sum(total[:1, RANK:], axis=1, keepdims=True)
    cross = jnp.sum(total[1:2, :RANK], axis=1, keepdims=True)
    norm_now = norm[:1, :1]
    ratio = norm_next / norm_now
    second = norm_next / (bend + ratio * (cross + ratio * curve[:1, :1]))
    keep = slice(0, LEAVES)
    solution_field[...] = moved[keep] + second * (lower[keep] + ratio * residual[keep])
    last_residual[...] = lower[keep] - second * (lower_mapped[keep] + ratio * first[keep])


def simple(kernel, out_shape, in_specs, scratch=()):
    return pl.pallas_call(
        kernel,
        out_shape=out_shape,
        in_specs=in_specs,
        out_specs=[VMEM] * len(out_shape),
        scratch_shapes=list(scratch),
        cost_estimate=cost(10**6, 10**6),
        compiler_params=pltpu.CompilerParams(vmem_limit_bytes=8 << 20),
    )


def exchange(copies, stride):
    members = copies.shape[0]
    devices = lax.axis_size("wide") * lax.axis_size("narrow")
    span = members * stride
    groups = [
        [base + offset + stride * i for i in range(members)]
        for base in range(0, devices, span)
        for offset in range(stride)
    ]
    return lax.all_to_all(
        copies, ("wide", "narrow"), 0, 0, tiled=True, axis_index_groups=groups
    )


def neighbours(fields):
    wide = lax.axis_size("wide")
    across = []
    for first in range(1, wide - 1, 2):
        across += [(first, first + 1), (first + 1, first)]
    return lax.ppermute(fields, "wide", across)


def local(
    coords,
    noise_var,
    observed,
    warm_start,
    leaf_basis,
    leaf_transfer,
    leaf_coupling,
    group_coupling,
    top_transfer,
    top_coupling,
    near_list,
    near_count,
    far_list,
    far_count,
    group_far,
    parent,
    top_far,
):
    groups = parent.shape[0]
    pairs = groups // 2
    wide = lax.axis_index("wide")
    lists = (near_list, near_count, far_list, far_count)
    tops = lax.dynamic_slice_in_dim(top_transfer, wide // 2 * 2, 2, 0)
    field, scalar = shape(8, POINTS), shape(8, LANES)
    packed_shape = shape(PAIR, PACK, LANES)
    scratch = [pltpu.VMEM((8, POINTS), f32)]

    def gather(packed, values, own_other, other, evaluate):
        blocks = exchange(packed, 1)
        *own_tiles, own_near = own_apply(evaluate, values, own_other)
        copies, fields = simple(
            fold_kernel,
            [shape(pairs, 4, LANES), shape(NARROW, packed.shape[1] - 4, LANES)],
            [VMEM] * 2,
        )(blocks, tops)
        extra = neighbours(fields)
        rows = exchange(copies, PAIR).reshape(4 * pairs, LANES)
        near = near_apply(evaluate, lists, (blocks, extra, values, own_near), other)
        return rows, near, own_tiles

    packed, values, basis, transfer = simple(
        begin_kernel,
        [
            shape(PAIR, PACK + COORDS, LANES),
            field,
            shape(LEAVES, RANK, POINTS, dtype=jnp.bfloat16),
            shape(LEAVES, RANK, RANK, dtype=jnp.bfloat16),
        ],
        [HBM] * 4,
        [pltpu.VMEM((LEAVES, POINTS), f32), pltpu.VMEM((LEAVES, 3, POINTS), f32)]
        + scratch
        + [pltpu.SemaphoreType.DMA((4,))],
    )(*in_hbm(warm_start, coords, jnp.transpose(leaf_basis, (0, 2, 1)), leaf_transfer))
    rows, near, (own_tiles,) = gather(
        packed,
        values,
        coords,
        (
            coords, noise_var, leaf_coupling, group_coupling[0], observed,
            parent, parent.reshape(1, groups), group_far, top_far.T, top_coupling,
        ),
        True,
    )
    tiles, base, leaf_far, select, own_pair, noise, coupling, group, observed = near
    far_data = (select, group, own_pair, tops, transfer, basis)
    packed, residual = simple(
        residual_kernel, [packed_shape, field], [VMEM] * 10, scratch
    )(rows, base, leaf_far, *far_data, observed)

    rows, near, _ = gather(packed, residual, own_tiles, (noise, coupling, tiles), False)
    packed, first, unit, norm = simple(
        second_kernel, [packed_shape, field, field, scalar], [VMEM] * 10
    )(rows, *near, *far_data, residual)

    rows, near, _ = gather(packed, unit, own_tiles, (noise, coupling, tiles), False)
    sums, lower, lower_mapped, step, curve = simple(
        third_kernel,
        [shape(2 * PAIR, 8, LANES), field, field, scalar, scalar],
        [VMEM] * 12,
    )(rows, *near, *far_data, residual, first, norm)
    blocks = exchange(sums, 1)
    (copies,) = simple(total_kernel, [shape(pairs // 2, 2, LANES)], [VMEM])(blocks)
    blocks = exchange(copies, 2 * PAIR)
    (moved,) = simple(step_kernel, [field], [VMEM] * 3)(values, residual, step)
    own = shape(LEAVES, POINTS)
    return tuple(
        simple(end_kernel, [own, own], [VMEM] * 8)(
            blocks, moved, residual, first, lower, lower_mapped, norm, curve
        )
    )


def solution(mesh):
    placed = (
        P(("wide", "narrow"), None, None),
        P(("wide", "narrow"), None),
        P(("wide", "narrow"), None),
        P(("wide", "narrow"), None),
        P(("wide", "narrow"), None, None),
        P(("wide", "narrow"), None, None),
        P(("wide", "narrow"), None, None, None),
        P("wide", None, None, None),
        P(),
        P(),
        P(("wide", "narrow"), None),
        P(("wide", "narrow")),
        P(("wide", "narrow"), None),
        P(("wide", "narrow")),
        P("wide", None),
        P(),
        P(),
    )
    return jax.shard_map(
        local,
        mesh=mesh,
        in_specs=placed,
        out_specs=(P(("wide", "narrow"), None), P(("wide", "narrow"), None)),
        check_vma=False,
    )
```

```python
import functools

import jax
import jax.numpy as jnp
from jax import lax
from jax.experimental import pallas as pl
from jax.experimental.pallas import tpu as pltpu
from jax.sharding import PartitionSpec as P

amplitude = 1.0 / 16.0
rate = 1.7320508075688772 / 1.5
log2_e = 1.4426950408889634
LEAVES = 3
NARROW = 4
GROUP = LEAVES * NARROW
POINTS = 512
RANK = 64
NEAR = 4
FAR = 8
FAR_GROUP = 6
FAR_TOP = 4
LANES = 128
PIECES = POINTS // LANES
FIELD = LEAVES * PIECES
PACK = FIELD + 4
COORDS = 3 * FIELD
PAIR = 2 * NARROW
WINDOW = 3 * GROUP
CHUNK = 64
QUARTER = 128
VMEM = pl.BlockSpec(memory_space=pltpu.VMEM)
HBM = pl.BlockSpec(memory_space=pltpu.HBM)
f32 = jnp.float32


def shape(*dims, dtype=f32):
    return jax.ShapeDtypeStruct(dims, dtype)


def in_hbm(*arrays):
    return tuple(pltpu.with_memory_space_constraint(one, pltpu.HBM) for one in arrays)


def cost(flops, bytes_accessed):
    return pl.CostEstimate(flops=flops, bytes_accessed=bytes_accessed, transcendentals=0)


def rows_of(array):
    return lax.broadcasted_iota(jnp.int32, array.shape, 0)


def times(vectors, matrix, transposed):
    high = vectors.astype(jnp.bfloat16).astype(f32)
    rest = vectors - high
    middle = rest.astype(jnp.bfloat16).astype(f32)
    parts = jnp.concatenate([high, middle, rest - middle], axis=0).astype(jnp.bfloat16)
    dims = (((1,), (1 if transposed else 0,)), ((), ()))
    out = lax.dot_general(parts, matrix, dims, preferred_element_type=f32)
    count = vectors.shape[0]
    return out[:count] + (out[count : 2 * count] + out[2 * count :])


def row_by_leaf(terms):
    out = jnp.zeros_like(terms[0])
    for leaf, term in enumerate(terms):
        out = jnp.where(rows_of(term) == leaf, term, out)
    return out


def fold_half(row):
    return row[:, :RANK] + row[:, RANK:]


def lane_sums(product):
    total = jnp.sum(product, axis=0, keepdims=True)
    total = total[:, :128] + total[:, 128:256] + (total[:, 256:384] + total[:, 384:])
    return fold_half(total)


def pack(values, scalar, basis, transfer, packed):
    for leaf in range(LEAVES):
        for piece in range(PIECES):
            packed[0, pl.ds(leaf * PIECES + piece, 1), :] = values[
                leaf : leaf + 1, piece * LANES : (piece + 1) * LANES
            ]
    coefs = row_by_leaf([times(values, basis[leaf], True) for leaf in range(LEAVES)])
    partial = row_by_leaf([times(coefs, transfer[leaf], False) for leaf in range(LEAVES)])
    partial = jnp.sum(partial, axis=0, keepdims=True)
    empty = jnp.zeros((1, RANK), f32)
    beside = [scalar, empty, empty]
    for leaf in range(LEAVES):
        packed[0, pl.ds(FIELD + leaf, 1), :] = jnp.concatenate(
            [coefs[leaf : leaf + 1], beside[leaf]], axis=1
        )
    packed[0, pl.ds(FIELD + 3, 1), :] = jnp.concatenate([partial, empty], axis=1)
    whole = packed[0]
    for copy in range(1, PAIR):
        packed[copy] = whole


def padded(ref, scratch):
    scratch[...] = jnp.zeros(scratch.shape, f32)
    scratch[0:LEAVES, :] = ref[...]
    return scratch[...]


def fetch(pairs, sems):
    copies = [pltpu.make_async_copy(one, two, sems.at[i]) for i, (one, two) in enumerate(pairs)]
    for copy in copies:
        copy.start()
    return copies


def begin_kernel(warm_in, coords_in, basis_in, transfer_in, packed, values, basis, transfer,
                 warm, coords, scratch, sems):
    pairs = [(warm_in, warm), (coords_in, coords), (basis_in, basis), (transfer_in, transfer)]
    for copy in fetch(pairs, sems):
        copy.wait()
    field = padded(warm, scratch)
    values[...] = field
    for leaf in range(LEAVES):
        for axis in range(3):
            for piece in range(PIECES):
                packed[0, pl.ds(PACK + (leaf * 3 + axis) * PIECES + piece, 1), :] = coords[
                    leaf, axis : axis + 1, piece * LANES : (piece + 1) * LANES
                ]
    pack(field, jnp.zeros((1, RANK), f32), basis, transfer, packed)


def fold_kernel(blocks, top_transfer, *refs):
    copies, fields = refs[-2:]
    sums = []
    for row in (FIELD + 3, FIELD):
        for group in range(2):
            first = group * NARROW
            line = [blocks[first + i, row : row + 1, :] for i in range(NARROW)]
            line = (line[0] + line[1]) + (line[2] + line[3])
            if row == FIELD + 3:
                partial = jnp.broadcast_to(line[:, :RANK], (8, RANK))
                lifted = times(partial, top_transfer[group], False)[:1]
                line = jnp.concatenate([line[:, :RANK], lifted], axis=1)
            sums.append(line)
    sums = jnp.concatenate(sums, axis=0)
    copies[...] = jnp.broadcast_to(sums[None], copies.shape)
    own = lax.rem(lax.axis_index("wide"), 2)
    for i in range(NARROW):
        device = own * NARROW + i
        fields[i, 0:FIELD, :] = blocks[device, 0:FIELD, :]
        if fields.shape[1] > FIELD:
            fields[i, FIELD:, :] = blocks[device, PACK:, :]


def selection(group_far, top_far, own_parent, parent):
    count = 2 * parent.shape[1]
    at = lax.broadcasted_iota(jnp.int32, (16, count), 1)
    row = lax.broadcasted_iota(jnp.int32, (16, count), 0)
    kind = at & 3
    group = lax.broadcasted_iota(jnp.int32, (parent.shape[1], count), 0)
    spot = lax.broadcasted_iota(jnp.int32, (parent.shape[1], count), 1)
    spread = jnp.where((group >> 1) * 4 + (group & 1) == spot, 1.0, 0.0).astype(jnp.bfloat16)
    parents = jnp.broadcast_to(parent[...], (16, parent.shape[1])).astype(f32)
    parents = jnp.dot(parents.astype(jnp.bfloat16), spread, preferred_element_type=f32)
    chosen = (row == FAR_GROUP + FAR_TOP) & (kind >= 2)
    for slot in range(FAR_GROUP):
        one = group_far[0, slot]
        chosen = chosen | ((row == slot) & (at == (one >> 1) * 4 + (one & 1)))
    for slot in range(FAR_TOP):
        box = top_far[slot, own_parent].astype(f32)
        chosen = chosen | ((row == FAR_GROUP + slot) & (kind < 2) & (parents == box))
    return jnp.where(chosen, 1.0, 0.0).astype(jnp.bfloat16)


def tile_copy(evaluate, slots, kept, tiles, sems, leaf, quarter):
    part = (pl.ds(leaf * slots, slots), pl.ds(quarter * QUARTER, QUARTER), slice(None))
    source, target = (kept, tiles) if evaluate else (tiles, kept)
    return pltpu.make_async_copy(source.at[part], target.at[part], sems.at[leaf * PIECES + quarter])


def begin_tiles(slots, kept, tiles, sems):
    for leaf in range(LEAVES):
        for quarter in range(PIECES):
            tile_copy(False, slots, kept, tiles, sems, leaf, quarter).start()


def tile_products(evaluate, slots, fill, near, columns, spread, totals, kept, tiles, sems):
    def leaf_step(leaf, _):
        for slot in range(slots):
            field, point = fill(leaf, slot)
            for piece in range(PIECES):
                spread[slot, piece] = jnp.broadcast_to(field(piece), (8, LANES))
            if evaluate:
                for at in range(FIELD):
                    spread[slot, PIECES + at] = jnp.broadcast_to(point(at), (8, LANES))

        def quarter_step(quarter, _):
            if not evaluate:
                tile_copy(False, slots, kept, tiles, sems, leaf, quarter).wait()

            def step(chunk, _):
                start = pl.multiple_of(quarter * QUARTER + chunk * CHUNK, CHUNK)
                acc = jnp.zeros((CHUNK // 8, 8, LANES), f32)
                if evaluate:
                    column = columns[leaf, pl.ds(start, CHUNK), :]
                    target = [
                        jnp.broadcast_to(column[:, axis : axis + 1], (CHUNK, LANES)).reshape(
                            CHUNK // 8, 8, LANES
                        )
                        for axis in range(3)
                    ]
                for slot in range(slots):
                    for piece in range(PIECES):
                        cut = slice(piece * LANES, (piece + 1) * LANES)
                        where = (leaf * slots + slot, pl.ds(start, CHUNK), cut)
                        if evaluate:
                            squared = None
                            for axis in range(3):
                                source = spread[slot, PIECES + axis * PIECES + piece]
                                between = target[axis] - source[None]
                                between = between * between
                                squared = between if squared is None else squared + between
                            squared = jnp.maximum(squared, 1e-30)
                            distance = squared * lax.rsqrt(squared)
                            decay = jnp.exp2(distance * (-rate * log2_e))
                            tile = (distance * (amplitude * rate) + amplitude) * decay
                            kept[where] = tile.reshape(CHUNK, LANES)
                        else:
                            tile = kept[where].reshape(CHUNK // 8, 8, LANES)
                        acc = acc + tile * spread[slot, piece][None]
                totals[pl.ds(start, CHUNK), :] = acc.reshape(CHUNK, LANES)
                return 0

            lax.fori_loop(0, QUARTER // CHUNK, step, 0)
            if evaluate:
                tile_copy(True, slots, kept, tiles, sems, leaf, quarter).start()
            return 0

        lax.fori_loop(0, PIECES, quarter_step, 0)
        eye = lax.broadcasted_iota(jnp.int32, (LANES, LANES), 0) == lax.broadcasted_iota(
            jnp.int32, (LANES, LANES), 1
        )
        pieces = []
        for piece in range(PIECES):
            column = jnp.sum(totals[piece * LANES : (piece + 1) * LANES, :], axis=1, keepdims=True)
            pieces.append(jnp.sum(jnp.where(eye, column, 0.0), axis=0, keepdims=True))
        near[pl.ds(leaf, 1), :] = jnp.concatenate(pieces, axis=1)
        return 0

    near[...] = jnp.zeros(near.shape, f32)
    lax.fori_loop(0, LEAVES, leaf_step, 0)


def end_tiles(slots, kept, tiles, sems):
    for leaf in range(LEAVES):
        for quarter in range(PIECES):
            tile_copy(True, slots, kept, tiles, sems, leaf, quarter).wait()


def leaf_coupling(blocks, coupling, far_list, far_count, coefs, leaf_far):
    wide = lax.axis_index("wide")
    own = lax.rem(wide, 2)
    coefs[...] = jnp.zeros(coefs.shape, f32)
    for device in range(NARROW):
        coefs[device * LEAVES : (device + 1) * LEAVES, :] = blocks[
            own * NARROW + device, FIELD : FIELD + LEAVES, :
        ]
    lane = lax.broadcasted_iota(jnp.int32, (16, LANES), 1)
    row = lax.broadcasted_iota(jnp.int32, (16, LANES), 0)
    far_rows = []
    for leaf in range(LEAVES):
        out = times(coefs[:, :RANK], coupling[leaf].reshape(FAR * RANK, RANK), True)
        total = jnp.zeros((16, LANES), f32)
        for two in range(FAR // 2):
            at = []
            for slot in (2 * two, 2 * two + 1):
                member = far_list[leaf, slot] - wide * GROUP
                at.append(jnp.where(slot < far_count[leaf], member, -1))
            listed = jnp.where(lane < RANK, at[0], at[1]) == row
            total = total + jnp.where(listed, out[:, two * LANES : (two + 1) * LANES], 0.0)
        far_rows.append(fold_half(jnp.sum(total, axis=0, keepdims=True)))
    leaf_far[...] = row_by_leaf([jnp.broadcast_to(one, (8, RANK)) for one in far_rows])


def own_kernel(evaluate, *refs):
    if evaluate:
        values, coords_in, tiles, own_near, coords, columns, scratch, sem, *loop = refs
        (copy,) = fetch([(coords_in, coords)], sem)
        copy.wait()
        for leaf in range(LEAVES):
            columns[leaf] = jnp.transpose(padded(coords.at[leaf], scratch))
    else:
        (values, tiles, blocks, coupling, far_list_in, far_count_in, own_near, leaf_far, far_list,
         far_count, coefs, sem, *loop) = refs
        coords = columns = None
    spread, totals, kept, sems = loop
    if not evaluate:
        copies = fetch([(far_list_in, far_list), (far_count_in, far_count)], sem)
        begin_tiles(1, kept, tiles, sems)
        for copy in copies:
            copy.wait()
        leaf_coupling(blocks, coupling, far_list, far_count, coefs, leaf_far)

    def fill(leaf, slot):
        def field(piece):
            part = values[:, piece * LANES : (piece + 1) * LANES]
            return jnp.sum(jnp.where(rows_of(part) == leaf, part, 0.0), axis=0, keepdims=True)

        def point(at):
            axis, piece = divmod(at, PIECES)
            return coords[leaf, axis : axis + 1, piece * LANES : (piece + 1) * LANES]

        return field, point

    tile_products(evaluate, 1, fill, own_near, columns, spread, totals, kept, tiles, sems)
    if evaluate:
        end_tiles(1, kept, tiles, sems)


def mid_kernel(
    blocks, far_list_in, far_count_in, parent_in, group_far_in, top_far_in, parents_in,
    coupling_in, noise_in, group_in, observed_in, top_in,
    leaf_far, select, own_pair, noise, coupling, group, observed,
    far_list, far_count, parent, group_far, top_far, parents, coefs, sems,
):
    copies = fetch(
        [
            (parent_in, parent), (group_far_in, group_far), (top_far_in, top_far),
            (parents_in, parents), (far_list_in, far_list), (far_count_in, far_count),
            (coupling_in, coupling), (noise_in, noise), (group_in, group),
            (observed_in, observed),
        ],
        sems,
    )
    for copy in copies[:4]:
        copy.wait()
    own_parent = parent[lax.axis_index("wide")]
    top_copy = pltpu.make_async_copy(top_in.at[own_parent], own_pair, sems.at[0])
    top_copy.start()
    select[...] = selection(group_far, top_far, own_parent, parents)
    for copy in copies[4:]:
        copy.wait()
    leaf_coupling(blocks, coupling, far_list, far_count, coefs, leaf_far)
    top_copy.wait()


def mid_apply(blocks, other):
    bf16 = jnp.bfloat16
    groups = other[2].shape[0]
    return pl.pallas_call(
        mid_kernel,
        out_shape=[
            shape(8, RANK),
            shape(16, 2 * groups, dtype=bf16),
            shape(FAR_TOP, RANK, RANK, dtype=bf16),
            shape(LEAVES, POINTS),
            shape(LEAVES, FAR, RANK, RANK, dtype=bf16),
            shape(FAR_GROUP, RANK, RANK, dtype=bf16),
            shape(LEAVES, POINTS),
        ],
        in_specs=[VMEM] + [HBM] * len(other),
        out_specs=[VMEM] * 7,
        scratch_shapes=[
            pltpu.SMEM((LEAVES, FAR), jnp.int32),
            pltpu.SMEM((LEAVES,), jnp.int32),
            pltpu.SMEM((groups,), jnp.int32),
            pltpu.SMEM((1, FAR_GROUP), jnp.int32),
            pltpu.SMEM(other[4].shape, jnp.int32),
            pltpu.VMEM((1, groups), jnp.int32),
            pltpu.VMEM((16, LANES), f32),
            pltpu.SemaphoreType.DMA((10,)),
        ],
        cost_estimate=cost(10**7, 2 * 10**6),
        compiler_params=pltpu.CompilerParams(vmem_limit_bytes=8 << 20),
    )(blocks, *in_hbm(*other))


def near_kernel(evaluate, *refs):
    if evaluate:
        (near_list_in, near_count_in, blocks, extra, values, own_near, noise, coords_in, tiles,
         base, near_list, near_count, sems, window, sources, coords, columns, scratch, near,
         spread, totals, kept, tile_sems) = refs
    else:
        (near_list_in, near_count_in, blocks, extra, values, own_near, noise, tiles, base,
         near_list, near_count, sems, window, scratch, near, spread, totals, kept,
         tile_sems) = refs
    slots = NEAR - 1
    pairs = [(near_list_in, near_list), (near_count_in, near_count)]
    copies = fetch(pairs + ([(coords_in, coords)] if evaluate else []), sems)
    if not evaluate:
        begin_tiles(slots, kept, tiles, tile_sems)
    wide = lax.axis_index("wide")
    first_group = wide - lax.rem(wide, 2)
    for device in range(PAIR + NARROW):
        held, index = (blocks, device) if device < PAIR else (extra, device - PAIR)
        more = PACK if device < PAIR else FIELD
        for leaf in range(LEAVES):
            at = device * LEAVES + leaf
            window[at] = held[index, leaf * PIECES : (leaf + 1) * PIECES, :]
            if evaluate:
                rows = more + leaf * FIELD
                sources[at] = held[index, rows : rows + FIELD, :]
    local_part = padded(noise, scratch) * values[...] + own_near[...]
    for copy in copies:
        copy.wait()
    if evaluate:
        for leaf in range(LEAVES):
            columns[leaf] = jnp.transpose(padded(coords.at[leaf], scratch))

    def fill(leaf, slot):
        listed = near_list[leaf, slot + 1]
        used = slot + 1 < near_count[leaf]
        of_group = lax.div(listed, GROUP)
        turn = of_group - first_group
        turn = jnp.where((turn >= 0) & (turn < 2), turn, 2)
        place = jnp.where(used, turn * GROUP + listed - of_group * GROUP, 0)
        field = window[place] * jnp.where(used, 1.0, 0.0).astype(f32)
        points = sources[place] if evaluate else None
        return lambda piece: field[piece : piece + 1], lambda at: points[at : at + 1]

    tile_products(
        evaluate, slots, fill, near, columns if evaluate else None, spread, totals, kept, tiles,
        tile_sems,
    )
    base[...] = local_part + near[...]
    if evaluate:
        end_tiles(slots, kept, tiles, tile_sems)


def loop_scratch(slots):
    return [
        pltpu.VMEM((slots, PIECES + FIELD, 8, LANES), f32),
        pltpu.VMEM((POINTS, LANES), f32),
        pltpu.VMEM((slots * LEAVES, POINTS, POINTS), f32),
        pltpu.SemaphoreType.DMA((LEAVES * PIECES,)),
    ]


def column_scratch():
    return [pltpu.VMEM((LEAVES, 3, POINTS), f32), pltpu.VMEM((LEAVES, POINTS, 8), f32)]


def own_apply(evaluate, values, other, later=(), lists=()):
    out_shape, out_specs = [shape(8, POINTS)], [VMEM]
    if evaluate:
        out_shape = [pltpu.HBM((LEAVES, POINTS, POINTS), f32)] + out_shape
        out_specs = [HBM] + out_specs
        scratch = column_scratch() + [
            pltpu.VMEM((8, POINTS), f32), pltpu.SemaphoreType.DMA((1,))
        ]
    else:
        out_shape.append(shape(8, RANK))
        out_specs.append(VMEM)
        scratch = [
            pltpu.SMEM((LEAVES, FAR), jnp.int32),
            pltpu.SMEM((LEAVES,), jnp.int32),
            pltpu.VMEM((16, LANES), f32),
            pltpu.SemaphoreType.DMA((2,)),
        ]
    return pl.pallas_call(
        functools.partial(own_kernel, evaluate),
        out_shape=out_shape,
        in_specs=[VMEM, HBM] + [VMEM] * len(later) + [HBM] * len(lists),
        out_specs=out_specs,
        scratch_shapes=scratch + loop_scratch(1),
        cost_estimate=cost(10**8, 4 * 10**6),
        compiler_params=pltpu.CompilerParams(vmem_limit_bytes=16 << 20),
    )(values, *in_hbm(other), *later, *in_hbm(*lists))


def near_apply(evaluate, lists, near_data, other):
    slots = NEAR - 1
    out_shape, out_specs = [shape(8, POINTS)], [VMEM]
    scratch = [
        pltpu.SMEM((LEAVES, NEAR), jnp.int32),
        pltpu.SMEM((LEAVES,), jnp.int32),
        pltpu.SemaphoreType.DMA((3,)),
        pltpu.VMEM((WINDOW, PIECES, LANES), f32),
    ]
    if evaluate:
        out_shape = [pltpu.HBM((slots * LEAVES, POINTS, POINTS), f32)] + out_shape
        out_specs = [HBM] + out_specs
        scratch += [pltpu.VMEM((WINDOW, FIELD, LANES), f32)] + column_scratch()
    scratch += [pltpu.VMEM((8, POINTS), f32)] * 2 + loop_scratch(slots)
    return pl.pallas_call(
        functools.partial(near_kernel, evaluate),
        out_shape=out_shape,
        in_specs=[HBM] * 2 + [VMEM] * 5 + [HBM],
        out_specs=out_specs,
        scratch_shapes=scratch,
        cost_estimate=cost(3 * 10**8, 2 * 10**7),
        compiler_params=pltpu.CompilerParams(vmem_limit_bytes=24 << 20),
    )(*in_hbm(*lists), *near_data, *in_hbm(other))


def far_field(rows, base, leaf_far, select, group_coupling, own_pair, top_transfer, transfer,
              basis):
    wide = lax.axis_index("wide")
    gathered = rows[...]
    picked = jnp.zeros((16, LANES), f32)
    for part in range(3):
        piece = gathered.astype(jnp.bfloat16)
        gathered = gathered - piece.astype(f32)
        picked = picked + jnp.dot(select[...], piece, preferred_element_type=f32)

    def listed(vectors, matrices, slots, first):
        out = times(vectors, matrices[...].reshape(slots * RANK, RANK), True)
        lane = lax.broadcasted_iota(jnp.int32, (16, LANES), 1)
        line = lax.broadcasted_iota(jnp.int32, (16, LANES), 0)
        total = jnp.zeros((16, LANES), f32)
        for two in range(slots // 2):
            own = line == first + 2 * two + jnp.where(lane < RANK, 0, 1)
            total = total + jnp.where(own, out[:, two * LANES : (two + 1) * LANES], 0.0)
        return fold_half(jnp.sum(total, axis=0, keepdims=True))

    top_in = listed(picked[:, RANK:], own_pair, FAR_TOP, FAR_GROUP)
    group_in = listed(picked[:, :RANK], group_coupling, FAR_GROUP, 0)
    group_in = group_in + times(jnp.broadcast_to(top_in, (8, RANK)), top_transfer[lax.rem(wide, 2)], True)
    leaf_in = leaf_far[...] + row_by_leaf(
        [times(group_in, transfer[leaf], True) for leaf in range(LEAVES)]
    )
    far = row_by_leaf([times(leaf_in, basis[leaf], False) for leaf in range(LEAVES)])
    sums = picked[FAR_GROUP + FAR_TOP : FAR_GROUP + FAR_TOP + 1, RANK:]
    return base[...] + far, jnp.sum(sums, axis=1, keepdims=True)


def residual_kernel(*refs):
    *common, observed, packed, residual, scratch = refs
    mapped, _ = far_field(*common)
    field = padded(observed, scratch) - mapped
    residual[...] = field
    pack(field, lane_sums(field * field), common[-1], common[-2], packed)


def second_kernel(*refs):
    *common, residual, packed, first, unit, norm = refs
    mapped, norm_now = far_field(*common)
    first[...] = mapped
    field = mapped * lax.rsqrt(norm_now)
    unit[...] = field
    norm[...] = jnp.broadcast_to(norm_now, norm.shape)
    scalar = lane_sums(residual[...] * mapped)
    pack(field, scalar, common[-1], common[-2], packed)


def third_kernel(*refs):
    *common, residual, first, norm, copies, lower, lower_mapped, step, curve = refs
    mapped, bend = far_field(*common)
    norm_now = norm[:1, :1]
    size = norm_now / bend
    before, image = residual[...], first[...]
    low = before - size * image
    low_mapped = image - (size * jnp.sqrt(norm_now)) * mapped
    lower[...] = low
    lower_mapped[...] = low_mapped
    step[...] = jnp.broadcast_to(size, step.shape)
    curve[...] = jnp.broadcast_to(bend, curve.shape)
    products = [low * low, low * low_mapped, before * low_mapped + low * image]
    sums = [lane_sums(product) for product in products] + [jnp.zeros((1, RANK), f32)]
    first_row = jnp.concatenate(sums[:2], axis=1)
    second_row = jnp.concatenate(sums[2:], axis=1)
    block = jnp.broadcast_to(first_row, (8, LANES))
    block = jnp.where(rows_of(block) == 0, block, second_row)
    copies[...] = jnp.broadcast_to(block[None], copies.shape)


def total_kernel(blocks, copies):
    total = blocks[0]
    for device in range(1, blocks.shape[0]):
        total = total + blocks[device]
    copies[...] = jnp.broadcast_to(total[:2][None], copies.shape)


def step_kernel(warm, residual, step, moved):
    moved[...] = warm[...] + step[:1, :1] * residual[...]


def end_kernel(blocks, moved, residual, first, lower, lower_mapped, norm, curve,
               solution_field, last_residual):
    total = jnp.sum(blocks[...], axis=0)
    norm_next = jnp.sum(total[:1, :RANK], axis=1, keepdims=True)
    bend = jnp.sum(total[:1, RANK:], axis=1, keepdims=True)
    cross = jnp.sum(total[1:2, :RANK], axis=1, keepdims=True)
    norm_now = norm[:1, :1]
    ratio = norm_next / norm_now
    second = norm_next / (bend + ratio * (cross + ratio * curve[:1, :1]))
    keep = slice(0, LEAVES)
    solution_field[...] = moved[keep] + second * (lower[keep] + ratio * residual[keep])
    last_residual[...] = lower[keep] - second * (lower_mapped[keep] + ratio * first[keep])


def simple(kernel, out_shape, in_specs, scratch=()):
    return pl.pallas_call(
        kernel,
        out_shape=out_shape,
        in_specs=in_specs,
        out_specs=[VMEM] * len(out_shape),
        scratch_shapes=list(scratch),
        cost_estimate=cost(10**6, 10**6),
        compiler_params=pltpu.CompilerParams(vmem_limit_bytes=8 << 20),
    )


def exchange(copies, stride):
    members = copies.shape[0]
    devices = lax.axis_size("wide") * lax.axis_size("narrow")
    span = members * stride
    groups = [
        [base + offset + stride * i for i in range(members)]
        for base in range(0, devices, span)
        for offset in range(stride)
    ]
    return lax.all_to_all(
        copies, ("wide", "narrow"), 0, 0, tiled=True, axis_index_groups=groups
    )


def neighbours(fields):
    wide = lax.axis_size("wide")
    across = []
    for first in range(1, wide - 1, 2):
        across += [(first, first + 1), (first + 1, first)]
    return lax.ppermute(fields, "wide", across)


def local(
    coords,
    noise_var,
    observed,
    warm_start,
    leaf_basis,
    leaf_transfer,
    leaf_coupling_matrices,
    group_coupling,
    top_transfer,
    top_coupling,
    near_list,
    near_count,
    far_list,
    far_count,
    group_far,
    parent,
    top_far,
):
    groups = parent.shape[0]
    pairs = groups // 2
    wide = lax.axis_index("wide")
    tops = lax.dynamic_slice_in_dim(top_transfer, wide // 2 * 2, 2, 0)
    field, scalar = shape(8, POINTS), shape(8, LANES)
    packed_shape = shape(PAIR, PACK, LANES)
    scratch = [pltpu.VMEM((8, POINTS), f32)]

    def wide_gather(blocks, *first):
        copies, fields = simple(
            fold_kernel,
            [shape(pairs, 4, LANES), shape(NARROW, blocks.shape[1] - 4, LANES)],
            [VMEM] * (2 + len(first)),
        )(blocks, tops, *first)
        extra = neighbours(fields)
        return extra, exchange(copies, PAIR).reshape(4 * pairs, LANES)

    def gather(packed, values):
        blocks = exchange(packed, 1)
        extra, rows = wide_gather(blocks)
        own_near, leaf_far = own_apply(
            False, values, own_tiles, (blocks, coupling), (far_list, far_count)
        )
        near = (blocks, extra, values, own_near, noise)
        (base,) = near_apply(False, (near_list, near_count), near, tiles)
        return rows, base, leaf_far

    packed, values, basis, transfer = simple(
        begin_kernel,
        [
            shape(PAIR, PACK + COORDS, LANES),
            field,
            shape(LEAVES, RANK, POINTS, dtype=jnp.bfloat16),
            shape(LEAVES, RANK, RANK, dtype=jnp.bfloat16),
        ],
        [HBM] * 4,
        [pltpu.VMEM((LEAVES, POINTS), f32), pltpu.VMEM((LEAVES, 3, POINTS), f32)]
        + scratch
        + [pltpu.SemaphoreType.DMA((4,))],
    )(*in_hbm(warm_start, coords, jnp.transpose(leaf_basis, (0, 2, 1)), leaf_transfer))
    blocks = exchange(packed, 1)
    own_tiles, own_near = own_apply(True, values, coords)
    extra, rows = wide_gather(blocks, own_near)
    leaf_far, select, own_pair, noise, coupling, group, observed = mid_apply(
        blocks,
        (
            far_list, far_count, parent, group_far, top_far.T, parent.reshape(1, groups),
            leaf_coupling_matrices, noise_var, group_coupling[0], observed, top_coupling,
        ),
    )
    near = (blocks, extra, values, own_near, noise)
    tiles, base = near_apply(True, (near_list, near_count), near, coords)
    far_data = (select, group, own_pair, tops, transfer, basis)
    packed, residual = simple(
        residual_kernel, [packed_shape, field], [VMEM] * 10, scratch
    )(rows, base, leaf_far, *far_data, observed)

    rows, *near = gather(packed, residual)
    packed, first, unit, norm = simple(
        second_kernel, [packed_shape, field, field, scalar], [VMEM] * 10
    )(rows, *near, *far_data, residual)

    rows, *near = gather(packed, unit)
    sums, lower, lower_mapped, step, curve = simple(
        third_kernel,
        [shape(PAIR, 8, LANES), field, field, scalar, scalar],
        [VMEM] * 12,
    )(rows, *near, *far_data, residual, first, norm)
    blocks = exchange(sums, 1)
    (copies,) = simple(total_kernel, [shape(pairs, 2, LANES)], [VMEM])(blocks)
    blocks = exchange(copies, PAIR)
    (moved,) = simple(step_kernel, [field], [VMEM] * 3)(values, residual, step)
    own = shape(LEAVES, POINTS)
    return tuple(
        simple(end_kernel, [own, own], [VMEM] * 8)(
            blocks, moved, residual, first, lower, lower_mapped, norm, curve
        )
    )


def solution(mesh):
    placed = (
        P(("wide", "narrow"), None, None),
        P(("wide", "narrow"), None),
        P(("wide", "narrow"), None),
        P(("wide", "narrow"), None),
        P(("wide", "narrow"), None, None),
        P(("wide", "narrow"), None, None),
        P(("wide", "narrow"), None, None, None),
        P("wide", None, None, None),
        P(),
        P(),
        P(("wide", "narrow"), None),
        P(("wide", "narrow")),
        P(("wide", "narrow"), None),
        P(("wide", "narrow")),
        P("wide", None),
        P(),
        P(),
    )
    return jax.shard_map(
        local,
        mesh=mesh,
        in_specs=placed,
        out_specs=(P(("wide", "narrow"), None), P(("wide", "narrow"), None)),
        check_vma=False,
    )
```

```python
import functools

import jax
import jax.numpy as jnp
from jax import lax
from jax.experimental import pallas as pl
from jax.experimental.pallas import tpu as pltpu
from jax.sharding import PartitionSpec as P

amplitude = 1.0 / 16.0
rate = 1.7320508075688772 / 1.5
log2_e = 1.4426950408889634
LEAVES = 3
NARROW = 4
GROUP = LEAVES * NARROW
POINTS = 512
RANK = 64
NEAR = 4
FAR = 8
FAR_GROUP = 6
FAR_TOP = 4
LANES = 128
PIECES = POINTS // LANES
FIELD = LEAVES * PIECES
PACK = FIELD + 4
COORDS = 3 * FIELD
PAIR = 2 * NARROW
WINDOW = 3 * GROUP
CHUNK = 64
QUARTER = 128
VMEM = pl.BlockSpec(memory_space=pltpu.VMEM)
HBM = pl.BlockSpec(memory_space=pltpu.HBM)
f32 = jnp.float32


def shape(*dims, dtype=f32):
    return jax.ShapeDtypeStruct(dims, dtype)


def in_hbm(*arrays):
    return tuple(pltpu.with_memory_space_constraint(one, pltpu.HBM) for one in arrays)


def cost(flops, bytes_accessed):
    return pl.CostEstimate(flops=flops, bytes_accessed=bytes_accessed, transcendentals=0)


def rows_of(array):
    return lax.broadcasted_iota(jnp.int32, array.shape, 0)


def times(vectors, matrix, transposed):
    high = vectors.astype(jnp.bfloat16).astype(f32)
    rest = vectors - high
    middle = rest.astype(jnp.bfloat16).astype(f32)
    parts = jnp.concatenate([high, middle, rest - middle], axis=0).astype(jnp.bfloat16)
    dims = (((1,), (1 if transposed else 0,)), ((), ()))
    out = lax.dot_general(parts, matrix, dims, preferred_element_type=f32)
    count = vectors.shape[0]
    return out[:count] + (out[count : 2 * count] + out[2 * count :])


def three_parts(vectors):
    high = vectors.astype(jnp.bfloat16).astype(f32)
    rest = vectors - high
    middle = rest.astype(jnp.bfloat16).astype(f32)
    return high, middle, rest - middle


def with_rows(vectors, third, fourth):
    row = rows_of(vectors)
    return jnp.where(row == 3, third, jnp.where(row == 4, fourth, vectors))


def target_factor(points):
    norm = three_parts(jnp.sum(points * points, axis=0, keepdims=True))
    high, middle, low = three_parts(points)
    first = [with_rows(one, 1.0, part) for one, part in zip((high, high, middle), norm)]
    return jnp.concatenate(first + [middle, high, low], axis=0)


def source_factor(points):
    norm = three_parts(jnp.sum(points * points, axis=0, keepdims=True))
    high, middle, low = three_parts(-2.0 * points)
    first = [with_rows(one, part, 1.0) for one, part in zip((high, middle, high), norm)]
    return jnp.concatenate(first + [middle, low, high], axis=0)


def row_by_leaf(terms):
    out = jnp.zeros_like(terms[0])
    for leaf, term in enumerate(terms):
        out = jnp.where(rows_of(term) == leaf, term, out)
    return out


def fold_half(row):
    return row[:, :RANK] + row[:, RANK:]


def lane_sums(product):
    total = jnp.sum(product, axis=0, keepdims=True)
    total = total[:, :128] + total[:, 128:256] + (total[:, 256:384] + total[:, 384:])
    return fold_half(total)


def pack(values, scalar, basis, transfer, packed):
    for leaf in range(LEAVES):
        for piece in range(PIECES):
            packed[0, pl.ds(leaf * PIECES + piece, 1), :] = values[
                leaf : leaf + 1, piece * LANES : (piece + 1) * LANES
            ]
    coefs = row_by_leaf([times(values, basis[leaf], True) for leaf in range(LEAVES)])
    partial = row_by_leaf([times(coefs, transfer[leaf], False) for leaf in range(LEAVES)])
    partial = jnp.sum(partial, axis=0, keepdims=True)
    empty = jnp.zeros((1, RANK), f32)
    beside = [scalar, empty, empty]
    for leaf in range(LEAVES):
        packed[0, pl.ds(FIELD + leaf, 1), :] = jnp.concatenate(
            [coefs[leaf : leaf + 1], beside[leaf]], axis=1
        )
    packed[0, pl.ds(FIELD + 3, 1), :] = jnp.concatenate([partial, empty], axis=1)
    whole = packed[0]
    for copy in range(1, PAIR):
        packed[copy] = whole


def padded(ref, scratch):
    scratch[...] = jnp.zeros(scratch.shape, f32)
    scratch[0:LEAVES, :] = ref[...]
    return scratch[...]


def fetch(pairs, sems):
    copies = [pltpu.make_async_copy(one, two, sems.at[i]) for i, (one, two) in enumerate(pairs)]
    for copy in copies:
        copy.start()
    return copies


def begin_kernel(warm_in, coords_in, basis_in, transfer_in, packed, values, basis, transfer,
                 warm, coords, scratch, sems):
    pairs = [(warm_in, warm), (coords_in, coords), (basis_in, basis), (transfer_in, transfer)]
    for copy in fetch(pairs, sems):
        copy.wait()
    field = padded(warm, scratch)
    values[...] = field
    for leaf in range(LEAVES):
        for axis in range(3):
            for piece in range(PIECES):
                packed[0, pl.ds(PACK + (leaf * 3 + axis) * PIECES + piece, 1), :] = coords[
                    leaf, axis : axis + 1, piece * LANES : (piece + 1) * LANES
                ]
    pack(field, jnp.zeros((1, RANK), f32), basis, transfer, packed)


def fold_kernel(blocks, top_transfer, *refs):
    copies, fields = refs[-2:]
    sums = []
    for row in (FIELD + 3, FIELD):
        for group in range(2):
            first = group * NARROW
            line = [blocks[first + i, row : row + 1, :] for i in range(NARROW)]
            line = (line[0] + line[1]) + (line[2] + line[3])
            if row == FIELD + 3:
                partial = jnp.broadcast_to(line[:, :RANK], (8, RANK))
                lifted = times(partial, top_transfer[group], False)[:1]
                line = jnp.concatenate([line[:, :RANK], lifted], axis=1)
            sums.append(line)
    sums = jnp.concatenate(sums, axis=0)
    copies[...] = jnp.broadcast_to(sums[None], copies.shape)
    own = lax.rem(lax.axis_index("wide"), 2)
    for i in range(NARROW):
        device = own * NARROW + i
        fields[i, 0:FIELD, :] = blocks[device, 0:FIELD, :]
        if fields.shape[1] > FIELD:
            fields[i, FIELD:, :] = blocks[device, PACK:, :]


def selection(group_far, top_far, own_parent, parent):
    count = 2 * parent.shape[1]
    at = lax.broadcasted_iota(jnp.int32, (16, count), 1)
    row = lax.broadcasted_iota(jnp.int32, (16, count), 0)
    kind = at & 3
    group = lax.broadcasted_iota(jnp.int32, (parent.shape[1], count), 0)
    spot = lax.broadcasted_iota(jnp.int32, (parent.shape[1], count), 1)
    spread = jnp.where((group >> 1) * 4 + (group & 1) == spot, 1.0, 0.0).astype(jnp.bfloat16)
    parents = jnp.broadcast_to(parent[...], (16, parent.shape[1])).astype(f32)
    parents = jnp.dot(parents.astype(jnp.bfloat16), spread, preferred_element_type=f32)
    chosen = (row == FAR_GROUP + FAR_TOP) & (kind >= 2)
    for slot in range(FAR_GROUP):
        one = group_far[0, slot]
        chosen = chosen | ((row == slot) & (at == (one >> 1) * 4 + (one & 1)))
    for slot in range(FAR_TOP):
        box = top_far[slot, own_parent].astype(f32)
        chosen = chosen | ((row == FAR_GROUP + slot) & (kind < 2) & (parents == box))
    return jnp.where(chosen, 1.0, 0.0).astype(jnp.bfloat16)


def tile_copy(evaluate, slots, kept, tiles, sems, leaf, quarter):
    part = (pl.ds(leaf * slots, slots), pl.ds(quarter * QUARTER, QUARTER), slice(None))
    source, target = (kept, tiles) if evaluate else (tiles, kept)
    return pltpu.make_async_copy(source.at[part], target.at[part], sems.at[leaf * PIECES + quarter])


def begin_tiles(slots, kept, tiles, sems):
    for leaf in range(LEAVES):
        for quarter in range(PIECES):
            tile_copy(False, slots, kept, tiles, sems, leaf, quarter).start()


def tile_products(
    evaluate, slots, fill, near, columns, spread, totals, kept, tiles, sems, factors=None
):
    rows_at_once = CHUNK if factors is None else QUARTER

    def leaf_step(leaf, _):
        for slot in range(slots):
            field, point = fill(leaf, slot)
            for piece in range(PIECES):
                spread[slot, piece] = jnp.broadcast_to(field(piece), (8, LANES))
            if evaluate and factors is None:
                for at in range(FIELD):
                    spread[slot, PIECES + at] = jnp.broadcast_to(point(at), (8, LANES))

        def quarter_step(quarter, _):
            if not evaluate:
                tile_copy(False, slots, kept, tiles, sems, leaf, quarter).wait()

            def step(chunk, _):
                start = pl.multiple_of(quarter * QUARTER + chunk * rows_at_once, rows_at_once)
                acc = jnp.zeros((rows_at_once // 8, 8, LANES), f32)
                if evaluate:
                    column = columns[leaf, pl.ds(start, rows_at_once), :]
                if evaluate and factors is None:
                    target = [
                        jnp.broadcast_to(column[:, axis : axis + 1], (rows_at_once, LANES)).reshape(
                            rows_at_once // 8, 8, LANES
                        )
                        for axis in range(3)
                    ]
                for slot in range(slots):
                    if factors is not None:
                        distances = jnp.dot(column, factors[slot], preferred_element_type=f32)
                    for piece in range(PIECES):
                        cut = slice(piece * LANES, (piece + 1) * LANES)
                        where = (leaf * slots + slot, pl.ds(start, rows_at_once), cut)
                        if factors is not None:
                            squared = distances[:, cut].reshape(rows_at_once // 8, 8, LANES)
                            squared = jnp.maximum(squared, 1e-30)
                            distance = squared * lax.rsqrt(squared)
                            decay = jnp.exp2(distance * -log2_e)
                            tile = (distance * amplitude + amplitude) * decay
                            kept[where] = tile.reshape(rows_at_once, LANES)
                        elif evaluate:
                            squared = None
                            for axis in range(3):
                                source = spread[slot, PIECES + axis * PIECES + piece]
                                between = target[axis] - source[None]
                                between = between * between
                                squared = between if squared is None else squared + between
                            squared = jnp.maximum(squared, 1e-30)
                            distance = squared * lax.rsqrt(squared)
                            decay = jnp.exp2(distance * (-rate * log2_e))
                            tile = (distance * (amplitude * rate) + amplitude) * decay
                            kept[where] = tile.reshape(rows_at_once, LANES)
                        else:
                            tile = kept[where].reshape(rows_at_once // 8, 8, LANES)
                        acc = acc + tile * spread[slot, piece][None]
                totals[pl.ds(start, rows_at_once), :] = acc.reshape(rows_at_once, LANES)
                return 0

            lax.fori_loop(0, QUARTER // rows_at_once, step, 0)
            if evaluate:
                tile_copy(True, slots, kept, tiles, sems, leaf, quarter).start()
            return 0

        lax.fori_loop(0, PIECES, quarter_step, 0)
        eye = lax.broadcasted_iota(jnp.int32, (LANES, LANES), 0) == lax.broadcasted_iota(
            jnp.int32, (LANES, LANES), 1
        )
        pieces = []
        for piece in range(PIECES):
            column = jnp.sum(totals[piece * LANES : (piece + 1) * LANES, :], axis=1, keepdims=True)
            pieces.append(jnp.sum(jnp.where(eye, column, 0.0), axis=0, keepdims=True))
        near[pl.ds(leaf, 1), :] = jnp.concatenate(pieces, axis=1)
        return 0

    near[...] = jnp.zeros(near.shape, f32)
    lax.fori_loop(0, LEAVES, leaf_step, 0)


def end_tiles(slots, kept, tiles, sems):
    for leaf in range(LEAVES):
        for quarter in range(PIECES):
            tile_copy(True, slots, kept, tiles, sems, leaf, quarter).wait()


def leaf_coupling(blocks, coupling, far_list, far_count, coefs, leaf_far):
    wide = lax.axis_index("wide")
    own = lax.rem(wide, 2)
    coefs[...] = jnp.zeros(coefs.shape, f32)
    for device in range(NARROW):
        coefs[device * LEAVES : (device + 1) * LEAVES, :] = blocks[
            own * NARROW + device, FIELD : FIELD + LEAVES, :
        ]
    lane = lax.broadcasted_iota(jnp.int32, (16, LANES), 1)
    row = lax.broadcasted_iota(jnp.int32, (16, LANES), 0)
    far_rows = []
    for leaf in range(LEAVES):
        out = times(coefs[:, :RANK], coupling[leaf].reshape(FAR * RANK, RANK), True)
        total = jnp.zeros((16, LANES), f32)
        for two in range(FAR // 2):
            at = []
            for slot in (2 * two, 2 * two + 1):
                member = far_list[leaf, slot] - wide * GROUP
                at.append(jnp.where(slot < far_count[leaf], member, -1))
            listed = jnp.where(lane < RANK, at[0], at[1]) == row
            total = total + jnp.where(listed, out[:, two * LANES : (two + 1) * LANES], 0.0)
        far_rows.append(fold_half(jnp.sum(total, axis=0, keepdims=True)))
    leaf_far[...] = row_by_leaf([jnp.broadcast_to(one, (8, RANK)) for one in far_rows])


def own_kernel(evaluate, *refs):
    if evaluate:
        values, coords_in, tiles, own_near, coords, columns, scratch, sem, *loop = refs
        (copy,) = fetch([(coords_in, coords)], sem)
        copy.wait()
        for leaf in range(LEAVES):
            columns[leaf] = jnp.transpose(padded(coords.at[leaf], scratch))
    else:
        (values, tiles, blocks, coupling, far_list_in, far_count_in, own_near, leaf_far, far_list,
         far_count, coefs, sem, *loop) = refs
        coords = columns = None
    spread, totals, kept, sems = loop
    if not evaluate:
        copies = fetch([(far_list_in, far_list), (far_count_in, far_count)], sem)
        begin_tiles(1, kept, tiles, sems)
        for copy in copies:
            copy.wait()
        leaf_coupling(blocks, coupling, far_list, far_count, coefs, leaf_far)

    def fill(leaf, slot):
        def field(piece):
            part = values[:, piece * LANES : (piece + 1) * LANES]
            return jnp.sum(jnp.where(rows_of(part) == leaf, part, 0.0), axis=0, keepdims=True)

        def point(at):
            axis, piece = divmod(at, PIECES)
            return coords[leaf, axis : axis + 1, piece * LANES : (piece + 1) * LANES]

        return field, point

    tile_products(evaluate, 1, fill, own_near, columns, spread, totals, kept, tiles, sems)
    if evaluate:
        end_tiles(1, kept, tiles, sems)


def mid_kernel(
    blocks, far_list_in, far_count_in, parent_in, group_far_in, top_far_in, parents_in,
    coupling_in, noise_in, group_in, observed_in, top_in,
    leaf_far, select, own_pair, noise, coupling, group, observed,
    far_list, far_count, parent, group_far, top_far, parents, coefs, sems,
):
    copies = fetch(
        [
            (parent_in, parent), (group_far_in, group_far), (top_far_in, top_far),
            (parents_in, parents), (far_list_in, far_list), (far_count_in, far_count),
            (coupling_in, coupling), (noise_in, noise), (group_in, group),
            (observed_in, observed),
        ],
        sems,
    )
    for copy in copies[:4]:
        copy.wait()
    own_parent = parent[lax.axis_index("wide")]
    top_copy = pltpu.make_async_copy(top_in.at[own_parent], own_pair, sems.at[0])
    top_copy.start()
    select[...] = selection(group_far, top_far, own_parent, parents)
    for copy in copies[4:]:
        copy.wait()
    leaf_coupling(blocks, coupling, far_list, far_count, coefs, leaf_far)
    top_copy.wait()


def mid_apply(blocks, other):
    bf16 = jnp.bfloat16
    groups = other[2].shape[0]
    return pl.pallas_call(
        mid_kernel,
        out_shape=[
            shape(8, RANK),
            shape(16, 2 * groups, dtype=bf16),
            shape(FAR_TOP, RANK, RANK, dtype=bf16),
            shape(LEAVES, POINTS),
            shape(LEAVES, FAR, RANK, RANK, dtype=bf16),
            shape(FAR_GROUP, RANK, RANK, dtype=bf16),
            shape(LEAVES, POINTS),
        ],
        in_specs=[VMEM] + [HBM] * len(other),
        out_specs=[VMEM] * 7,
        scratch_shapes=[
            pltpu.SMEM((LEAVES, FAR), jnp.int32),
            pltpu.SMEM((LEAVES,), jnp.int32),
            pltpu.SMEM((groups,), jnp.int32),
            pltpu.SMEM((1, FAR_GROUP), jnp.int32),
            pltpu.SMEM(other[4].shape, jnp.int32),
            pltpu.VMEM((1, groups), jnp.int32),
            pltpu.VMEM((16, LANES), f32),
            pltpu.SemaphoreType.DMA((10,)),
        ],
        cost_estimate=cost(10**7, 2 * 10**6),
        compiler_params=pltpu.CompilerParams(vmem_limit_bytes=8 << 20),
    )(blocks, *in_hbm(*other))


def near_kernel(evaluate, *refs):
    if evaluate:
        (near_list_in, near_count_in, blocks, extra, values, own_near, noise, coords_in, tiles,
         base, near_list, near_count, sems, window, sources, coords, columns, factors, centres,
         scratch, near, spread, totals, kept, tile_sems) = refs
    else:
        (near_list_in, near_count_in, blocks, extra, values, own_near, noise, tiles, base,
         near_list, near_count, sems, window, scratch, near, spread, totals, kept,
         tile_sems) = refs
    slots = NEAR - 1
    pairs = [(near_list_in, near_list), (near_count_in, near_count)]
    copies = fetch(pairs + ([(coords_in, coords)] if evaluate else []), sems)
    if not evaluate:
        begin_tiles(slots, kept, tiles, tile_sems)
    wide = lax.axis_index("wide")
    first_group = wide - lax.rem(wide, 2)
    for device in range(PAIR + NARROW):
        held, index = (blocks, device) if device < PAIR else (extra, device - PAIR)
        more = PACK if device < PAIR else FIELD
        for leaf in range(LEAVES):
            at = device * LEAVES + leaf
            window[at] = held[index, leaf * PIECES : (leaf + 1) * PIECES, :]
            if evaluate:
                rows = more + leaf * FIELD
                sources[at] = held[index, rows : rows + FIELD, :]
    local_part = padded(noise, scratch) * values[...] + own_near[...]
    for copy in copies:
        copy.wait()
    if evaluate:
        for leaf in range(LEAVES):
            points = padded(coords.at[leaf], scratch)
            centre = jnp.broadcast_to(points[:, :1], (8, POINTS))
            centres[leaf] = centre
            factor = target_factor((points - centre) * rate)
            columns[leaf] = jnp.transpose(factor).astype(jnp.bfloat16)

    def source(leaf, points):
        lines = jnp.zeros((8, POINTS), f32)
        for axis in range(3):
            line = [points[axis * PIECES + i : axis * PIECES + i + 1] for i in range(PIECES)]
            lines = jnp.where(rows_of(lines) == axis, jnp.concatenate(line, axis=1), lines)
        return source_factor((lines - centres[leaf]) * rate).astype(jnp.bfloat16)

    def fill(leaf, slot):
        listed = near_list[leaf, slot + 1]
        used = slot + 1 < near_count[leaf]
        of_group = lax.div(listed, GROUP)
        turn = of_group - first_group
        turn = jnp.where((turn >= 0) & (turn < 2), turn, 2)
        place = jnp.where(used, turn * GROUP + listed - of_group * GROUP, 0)
        field = window[place] * jnp.where(used, 1.0, 0.0).astype(f32)
        if evaluate:
            factors[slot] = source(leaf, sources[place])
        return lambda piece: field[piece : piece + 1], None

    tile_products(
        evaluate, slots, fill, near, columns if evaluate else None, spread, totals, kept, tiles,
        tile_sems, factors if evaluate else None,
    )
    base[...] = local_part + near[...]
    if evaluate:
        end_tiles(slots, kept, tiles, tile_sems)


def loop_scratch(slots):
    return [
        pltpu.VMEM((slots, PIECES + FIELD, 8, LANES), f32),
        pltpu.VMEM((POINTS, LANES), f32),
        pltpu.VMEM((slots * LEAVES, POINTS, POINTS), f32),
        pltpu.SemaphoreType.DMA((LEAVES * PIECES,)),
    ]


def column_scratch():
    return [pltpu.VMEM((LEAVES, 3, POINTS), f32), pltpu.VMEM((LEAVES, POINTS, 8), f32)]


def own_apply(evaluate, values, other, later=(), lists=()):
    out_shape, out_specs = [shape(8, POINTS)], [VMEM]
    if evaluate:
        out_shape = [pltpu.HBM((LEAVES, POINTS, POINTS), f32)] + out_shape
        out_specs = [HBM] + out_specs
        scratch = column_scratch() + [
            pltpu.VMEM((8, POINTS), f32), pltpu.SemaphoreType.DMA((1,))
        ]
    else:
        out_shape.append(shape(8, RANK))
        out_specs.append(VMEM)
        scratch = [
            pltpu.SMEM((LEAVES, FAR), jnp.int32),
            pltpu.SMEM((LEAVES,), jnp.int32),
            pltpu.VMEM((16, LANES), f32),
            pltpu.SemaphoreType.DMA((2,)),
        ]
    return pl.pallas_call(
        functools.partial(own_kernel, evaluate),
        out_shape=out_shape,
        in_specs=[VMEM, HBM] + [VMEM] * len(later) + [HBM] * len(lists),
        out_specs=out_specs,
        scratch_shapes=scratch + loop_scratch(1),
        cost_estimate=cost(10**8, 4 * 10**6),
        compiler_params=pltpu.CompilerParams(vmem_limit_bytes=16 << 20),
    )(values, *in_hbm(other), *later, *in_hbm(*lists))


def near_apply(evaluate, lists, near_data, other):
    slots = NEAR - 1
    out_shape, out_specs = [shape(8, POINTS)], [VMEM]
    scratch = [
        pltpu.SMEM((LEAVES, NEAR), jnp.int32),
        pltpu.SMEM((LEAVES,), jnp.int32),
        pltpu.SemaphoreType.DMA((3,)),
        pltpu.VMEM((WINDOW, PIECES, LANES), f32),
    ]
    if evaluate:
        out_shape = [pltpu.HBM((slots * LEAVES, POINTS, POINTS), f32)] + out_shape
        out_specs = [HBM] + out_specs
        scratch += [
            pltpu.VMEM((WINDOW, FIELD, LANES), f32),
            pltpu.VMEM((LEAVES, 3, POINTS), f32),
            pltpu.VMEM((LEAVES, POINTS, 48), jnp.bfloat16),
            pltpu.VMEM((slots, 48, POINTS), jnp.bfloat16),
            pltpu.VMEM((LEAVES, 8, POINTS), f32),
        ]
    scratch += [pltpu.VMEM((8, POINTS), f32)] * 2 + loop_scratch(slots)
    return pl.pallas_call(
        functools.partial(near_kernel, evaluate),
        out_shape=out_shape,
        in_specs=[HBM] * 2 + [VMEM] * 5 + [HBM],
        out_specs=out_specs,
        scratch_shapes=scratch,
        cost_estimate=cost(3 * 10**8, 2 * 10**7),
        compiler_params=pltpu.CompilerParams(vmem_limit_bytes=24 << 20),
    )(*in_hbm(*lists), *near_data, *in_hbm(other))


def far_field(rows, base, leaf_far, select, group_coupling, own_pair, top_transfer, transfer,
              basis):
    wide = lax.axis_index("wide")
    gathered = rows[...]
    picked = jnp.zeros((16, LANES), f32)
    for part in range(3):
        piece = gathered.astype(jnp.bfloat16)
        gathered = gathered - piece.astype(f32)
        picked = picked + jnp.dot(select[...], piece, preferred_element_type=f32)

    def listed(vectors, matrices, slots, first):
        out = times(vectors, matrices[...].reshape(slots * RANK, RANK), True)
        lane = lax.broadcasted_iota(jnp.int32, (16, LANES), 1)
        line = lax.broadcasted_iota(jnp.int32, (16, LANES), 0)
        total = jnp.zeros((16, LANES), f32)
        for two in range(slots // 2):
            own = line == first + 2 * two + jnp.where(lane < RANK, 0, 1)
            total = total + jnp.where(own, out[:, two * LANES : (two + 1) * LANES], 0.0)
        return fold_half(jnp.sum(total, axis=0, keepdims=True))

    top_in = listed(picked[:, RANK:], own_pair, FAR_TOP, FAR_GROUP)
    group_in = listed(picked[:, :RANK], group_coupling, FAR_GROUP, 0)
    group_in = group_in + times(jnp.broadcast_to(top_in, (8, RANK)), top_transfer[lax.rem(wide, 2)], True)
    leaf_in = leaf_far[...] + row_by_leaf(
        [times(group_in, transfer[leaf], True) for leaf in range(LEAVES)]
    )
    far = row_by_leaf([times(leaf_in, basis[leaf], False) for leaf in range(LEAVES)])
    sums = picked[FAR_GROUP + FAR_TOP : FAR_GROUP + FAR_TOP + 1, RANK:]
    return base[...] + far, jnp.sum(sums, axis=1, keepdims=True)


def residual_kernel(*refs):
    *common, observed, packed, residual, scratch = refs
    mapped, _ = far_field(*common)
    field = padded(observed, scratch) - mapped
    residual[...] = field
    pack(field, lane_sums(field * field), common[-1], common[-2], packed)


def second_kernel(*refs):
    *common, residual, packed, first, unit, norm = refs
    mapped, norm_now = far_field(*common)
    first[...] = mapped
    field = mapped * lax.rsqrt(norm_now)
    unit[...] = field
    norm[...] = jnp.broadcast_to(norm_now, norm.shape)
    scalar = lane_sums(residual[...] * mapped)
    pack(field, scalar, common[-1], common[-2], packed)


def third_kernel(*refs):
    *common, residual, first, norm, copies, lower, lower_mapped, step, curve = refs
    mapped, bend = far_field(*common)
    norm_now = norm[:1, :1]
    size = norm_now / bend
    before, image = residual[...], first[...]
    low = before - size * image
    low_mapped = image - (size * jnp.sqrt(norm_now)) * mapped
    lower[...] = low
    lower_mapped[...] = low_mapped
    step[...] = jnp.broadcast_to(size, step.shape)
    curve[...] = jnp.broadcast_to(bend, curve.shape)
    products = [low * low, low * low_mapped, before * low_mapped + low * image]
    sums = [lane_sums(product) for product in products] + [jnp.zeros((1, RANK), f32)]
    first_row = jnp.concatenate(sums[:2], axis=1)
    second_row = jnp.concatenate(sums[2:], axis=1)
    block = jnp.broadcast_to(first_row, (8, LANES))
    block = jnp.where(rows_of(block) == 0, block, second_row)
    copies[...] = jnp.broadcast_to(block[None], copies.shape)


def total_kernel(blocks, copies):
    total = blocks[0]
    for device in range(1, blocks.shape[0]):
        total = total + blocks[device]
    copies[...] = jnp.broadcast_to(total[:2][None], copies.shape)


def step_kernel(warm, residual, step, moved):
    moved[...] = warm[...] + step[:1, :1] * residual[...]


def end_kernel(blocks, moved, residual, first, lower, lower_mapped, norm, curve,
               solution_field, last_residual):
    total = jnp.sum(blocks[...], axis=0)
    norm_next = jnp.sum(total[:1, :RANK], axis=1, keepdims=True)
    bend = jnp.sum(total[:1, RANK:], axis=1, keepdims=True)
    cross = jnp.sum(total[1:2, :RANK], axis=1, keepdims=True)
    norm_now = norm[:1, :1]
    ratio = norm_next / norm_now
    second = norm_next / (bend + ratio * (cross + ratio * curve[:1, :1]))
    keep = slice(0, LEAVES)
    solution_field[...] = moved[keep] + second * (lower[keep] + ratio * residual[keep])
    last_residual[...] = lower[keep] - second * (lower_mapped[keep] + ratio * first[keep])


def simple(kernel, out_shape, in_specs, scratch=()):
    return pl.pallas_call(
        kernel,
        out_shape=out_shape,
        in_specs=in_specs,
        out_specs=[VMEM] * len(out_shape),
        scratch_shapes=list(scratch),
        cost_estimate=cost(10**6, 10**6),
        compiler_params=pltpu.CompilerParams(vmem_limit_bytes=8 << 20),
    )


def exchange(copies, stride):
    members = copies.shape[0]
    devices = lax.axis_size("wide") * lax.axis_size("narrow")
    span = members * stride
    groups = [
        [base + offset + stride * i for i in range(members)]
        for base in range(0, devices, span)
        for offset in range(stride)
    ]
    return lax.all_to_all(
        copies, ("wide", "narrow"), 0, 0, tiled=True, axis_index_groups=groups
    )


def neighbours(fields):
    wide = lax.axis_size("wide")
    across = []
    for first in range(1, wide - 1, 2):
        across += [(first, first + 1), (first + 1, first)]
    return lax.ppermute(fields, "wide", across)


def local(
    coords,
    noise_var,
    observed,
    warm_start,
    leaf_basis,
    leaf_transfer,
    leaf_coupling_matrices,
    group_coupling,
    top_transfer,
    top_coupling,
    near_list,
    near_count,
    far_list,
    far_count,
    group_far,
    parent,
    top_far,
):
    groups = parent.shape[0]
    pairs = groups // 2
    wide = lax.axis_index("wide")
    tops = lax.dynamic_slice_in_dim(top_transfer, wide // 2 * 2, 2, 0)
    field, scalar = shape(8, POINTS), shape(8, LANES)
    packed_shape = shape(PAIR, PACK, LANES)
    scratch = [pltpu.VMEM((8, POINTS), f32)]

    def wide_gather(blocks, *first):
        copies, fields = simple(
            fold_kernel,
            [shape(pairs, 4, LANES), shape(NARROW, blocks.shape[1] - 4, LANES)],
            [VMEM] * (2 + len(first)),
        )(blocks, tops, *first)
        extra = neighbours(fields)
        return extra, exchange(copies, PAIR).reshape(4 * pairs, LANES)

    def gather(packed, values):
        blocks = exchange(packed, 1)
        extra, rows = wide_gather(blocks)
        own_near, leaf_far = own_apply(
            False, values, own_tiles, (blocks, coupling), (far_list, far_count)
        )
        near = (blocks, extra, values, own_near, noise)
        (base,) = near_apply(False, (near_list, near_count), near, tiles)
        return rows, base, leaf_far

    packed, values, basis, transfer = simple(
        begin_kernel,
        [
            shape(PAIR, PACK + COORDS, LANES),
            field,
            shape(LEAVES, RANK, POINTS, dtype=jnp.bfloat16),
            shape(LEAVES, RANK, RANK, dtype=jnp.bfloat16),
        ],
        [HBM] * 4,
        [pltpu.VMEM((LEAVES, POINTS), f32), pltpu.VMEM((LEAVES, 3, POINTS), f32)]
        + scratch
        + [pltpu.SemaphoreType.DMA((4,))],
    )(*in_hbm(warm_start, coords, jnp.transpose(leaf_basis, (0, 2, 1)), leaf_transfer))
    blocks = exchange(packed, 1)
    own_tiles, own_near = own_apply(True, values, coords)
    extra, rows = wide_gather(blocks, own_near)
    leaf_far, select, own_pair, noise, coupling, group, observed = mid_apply(
        blocks,
        (
            far_list, far_count, parent, group_far, top_far.T, parent.reshape(1, groups),
            leaf_coupling_matrices, noise_var, group_coupling[0], observed, top_coupling,
        ),
    )
    near = (blocks, extra, values, own_near, noise)
    tiles, base = near_apply(True, (near_list, near_count), near, coords)
    far_data = (select, group, own_pair, tops, transfer, basis)
    packed, residual = simple(
        residual_kernel, [packed_shape, field], [VMEM] * 10, scratch
    )(rows, base, leaf_far, *far_data, observed)

    rows, *near = gather(packed, residual)
    packed, first, unit, norm = simple(
        second_kernel, [packed_shape, field, field, scalar], [VMEM] * 10
    )(rows, *near, *far_data, residual)

    rows, *near = gather(packed, unit)
    sums, lower, lower_mapped, step, curve = simple(
        third_kernel,
        [shape(PAIR, 8, LANES), field, field, scalar, scalar],
        [VMEM] * 12,
    )(rows, *near, *far_data, residual, first, norm)
    blocks = exchange(sums, 1)
    (copies,) = simple(total_kernel, [shape(pairs, 2, LANES)], [VMEM])(blocks)
    blocks = exchange(copies, PAIR)
    (moved,) = simple(step_kernel, [field], [VMEM] * 3)(values, residual, step)
    own = shape(LEAVES, POINTS)
    return tuple(
        simple(end_kernel, [own, own], [VMEM] * 8)(
            blocks, moved, residual, first, lower, lower_mapped, norm, curve
        )
    )


def solution(mesh):
    placed = (
        P(("wide", "narrow"), None, None),
        P(("wide", "narrow"), None),
        P(("wide", "narrow"), None),
        P(("wide", "narrow"), None),
        P(("wide", "narrow"), None, None),
        P(("wide", "narrow"), None, None),
        P(("wide", "narrow"), None, None, None),
        P("wide", None, None, None),
        P(),
        P(),
        P(("wide", "narrow"), None),
        P(("wide", "narrow")),
        P(("wide", "narrow"), None),
        P(("wide", "narrow")),
        P("wide", None),
        P(),
        P(),
    )
    return jax.shard_map(
        local,
        mesh=mesh,
        in_specs=placed,
        out_specs=(P(("wide", "narrow"), None), P(("wide", "narrow"), None)),
        check_vma=False,
    )
```

```python
import functools

import jax
import jax.numpy as jnp
from jax import lax
from jax.experimental import pallas as pl
from jax.experimental.pallas import tpu as pltpu
from jax.sharding import PartitionSpec as P

amplitude = 1.0 / 16.0
rate = 1.7320508075688772 / 1.5
log2_e = 1.4426950408889634
LEAVES = 3
NARROW = 4
GROUP = LEAVES * NARROW
POINTS = 512
RANK = 64
NEAR = 4
FAR = 8
FAR_GROUP = 6
FAR_TOP = 4
LANES = 128
PIECES = POINTS // LANES
FIELD = LEAVES * PIECES
PACK = FIELD + 4
COORDS = 3 * FIELD
PAIR = 2 * NARROW
WINDOW = 3 * GROUP
CHUNK = 64
QUARTER = 128
VMEM = pl.BlockSpec(memory_space=pltpu.VMEM)
HBM = pl.BlockSpec(memory_space=pltpu.HBM)
f32 = jnp.float32


def shape(*dims, dtype=f32):
    return jax.ShapeDtypeStruct(dims, dtype)


def in_hbm(*arrays):
    return tuple(pltpu.with_memory_space_constraint(one, pltpu.HBM) for one in arrays)


def cost(flops, bytes_accessed):
    return pl.CostEstimate(flops=flops, bytes_accessed=bytes_accessed, transcendentals=0)


def rows_of(array):
    return lax.broadcasted_iota(jnp.int32, array.shape, 0)


def times(vectors, matrix, transposed):
    high = vectors.astype(jnp.bfloat16).astype(f32)
    rest = vectors - high
    middle = rest.astype(jnp.bfloat16).astype(f32)
    parts = jnp.concatenate([high, middle, rest - middle], axis=0).astype(jnp.bfloat16)
    dims = (((1,), (1 if transposed else 0,)), ((), ()))
    out = lax.dot_general(parts, matrix, dims, preferred_element_type=f32)
    count = vectors.shape[0]
    return out[:count] + (out[count : 2 * count] + out[2 * count :])


def three_parts(vectors):
    high = vectors.astype(jnp.bfloat16).astype(f32)
    rest = vectors - high
    middle = rest.astype(jnp.bfloat16).astype(f32)
    return high, middle, rest - middle


def with_rows(vectors, third, fourth):
    row = rows_of(vectors)
    return jnp.where(row == 3, third, jnp.where(row == 4, fourth, vectors))


def target_factor(points):
    norm = three_parts(jnp.sum(points * points, axis=0, keepdims=True))
    high, middle, low = three_parts(points)
    first = [with_rows(one, 1.0, part) for one, part in zip((high, high, middle), norm)]
    return jnp.concatenate(first + [middle, high, low], axis=0)


def source_factor(points):
    norm = three_parts(jnp.sum(points * points, axis=0, keepdims=True))
    high, middle, low = three_parts(-2.0 * points)
    first = [with_rows(one, part, 1.0) for one, part in zip((high, middle, high), norm)]
    return jnp.concatenate(first + [middle, low, high], axis=0)


def row_by_leaf(terms):
    out = jnp.zeros_like(terms[0])
    for leaf, term in enumerate(terms):
        out = jnp.where(rows_of(term) == leaf, term, out)
    return out


def fold_half(row):
    return row[:, :RANK] + row[:, RANK:]


def lane_sums(product):
    total = jnp.sum(product, axis=0, keepdims=True)
    total = total[:, :128] + total[:, 128:256] + (total[:, 256:384] + total[:, 384:])
    return fold_half(total)


def pack(values, scalar, basis, transfer, packed):
    for leaf in range(LEAVES):
        for piece in range(PIECES):
            packed[0, pl.ds(leaf * PIECES + piece, 1), :] = values[
                leaf : leaf + 1, piece * LANES : (piece + 1) * LANES
            ]
    coefs = row_by_leaf([times(values, basis[leaf], True) for leaf in range(LEAVES)])
    partial = row_by_leaf([times(coefs, transfer[leaf], False) for leaf in range(LEAVES)])
    partial = jnp.sum(partial, axis=0, keepdims=True)
    empty = jnp.zeros((1, RANK), f32)
    beside = [scalar, empty, empty]
    for leaf in range(LEAVES):
        packed[0, pl.ds(FIELD + leaf, 1), :] = jnp.concatenate(
            [coefs[leaf : leaf + 1], beside[leaf]], axis=1
        )
    packed[0, pl.ds(FIELD + 3, 1), :] = jnp.concatenate([partial, empty], axis=1)
    whole = packed[0]
    for copy in range(1, PAIR):
        packed[copy] = whole


def padded(ref, scratch):
    scratch[...] = jnp.zeros(scratch.shape, f32)
    scratch[0:LEAVES, :] = ref[...]
    return scratch[...]


def fetch(pairs, sems):
    copies = [pltpu.make_async_copy(one, two, sems.at[i]) for i, (one, two) in enumerate(pairs)]
    for copy in copies:
        copy.start()
    return copies


def begin_kernel(warm_in, coords_in, basis_in, transfer_in, packed, values, basis, transfer,
                 warm, coords, scratch, sems):
    pairs = [(warm_in, warm), (coords_in, coords), (basis_in, basis), (transfer_in, transfer)]
    for copy in fetch(pairs, sems):
        copy.wait()
    field = padded(warm, scratch)
    values[...] = field
    for leaf in range(LEAVES):
        for axis in range(3):
            for piece in range(PIECES):
                packed[0, pl.ds(PACK + (leaf * 3 + axis) * PIECES + piece, 1), :] = coords[
                    leaf, axis : axis + 1, piece * LANES : (piece + 1) * LANES
                ]
    pack(field, jnp.zeros((1, RANK), f32), basis, transfer, packed)


def fold_kernel(blocks, top_transfer, *refs):
    copies, fields = refs[-2:]
    sums = []
    for row in (FIELD + 3, FIELD):
        for group in range(2):
            first = group * NARROW
            line = [blocks[first + i, row : row + 1, :] for i in range(NARROW)]
            line = (line[0] + line[1]) + (line[2] + line[3])
            if row == FIELD + 3:
                partial = jnp.broadcast_to(line[:, :RANK], (8, RANK))
                lifted = times(partial, top_transfer[group], False)[:1]
                line = jnp.concatenate([line[:, :RANK], lifted], axis=1)
            sums.append(line)
    sums = jnp.concatenate(sums, axis=0)
    copies[...] = jnp.broadcast_to(sums[None], copies.shape)
    own = lax.rem(lax.axis_index("wide"), 2)
    for i in range(NARROW):
        device = own * NARROW + i
        fields[i, 0:FIELD, :] = blocks[device, 0:FIELD, :]
        if fields.shape[1] > FIELD:
            fields[i, FIELD:, :] = blocks[device, PACK:, :]


def selection(group_far, top_far, own_parent, parent):
    count = 2 * parent.shape[1]
    at = lax.broadcasted_iota(jnp.int32, (16, count), 1)
    row = lax.broadcasted_iota(jnp.int32, (16, count), 0)
    kind = at & 3
    group = lax.broadcasted_iota(jnp.int32, (parent.shape[1], count), 0)
    spot = lax.broadcasted_iota(jnp.int32, (parent.shape[1], count), 1)
    spread = jnp.where((group >> 1) * 4 + (group & 1) == spot, 1.0, 0.0).astype(jnp.bfloat16)
    parents = jnp.broadcast_to(parent[...], (16, parent.shape[1])).astype(f32)
    parents = jnp.dot(parents.astype(jnp.bfloat16), spread, preferred_element_type=f32)
    chosen = (row == FAR_GROUP + FAR_TOP) & (kind >= 2)
    for slot in range(FAR_GROUP):
        one = group_far[0, slot]
        chosen = chosen | ((row == slot) & (at == (one >> 1) * 4 + (one & 1)))
    for slot in range(FAR_TOP):
        box = top_far[slot, own_parent].astype(f32)
        chosen = chosen | ((row == FAR_GROUP + slot) & (kind < 2) & (parents == box))
    return jnp.where(chosen, 1.0, 0.0).astype(jnp.bfloat16)


def tile_copy(evaluate, slots, kept, tiles, sems, leaf, quarter):
    part = (pl.ds(leaf * slots, slots), pl.ds(quarter * QUARTER, QUARTER), slice(None))
    source, target = (kept, tiles) if evaluate else (tiles, kept)
    return pltpu.make_async_copy(source.at[part], target.at[part], sems.at[leaf * PIECES + quarter])


def begin_tiles(slots, kept, tiles, sems, first=0):
    for leaf in range(first, LEAVES):
        for quarter in range(PIECES):
            tile_copy(False, slots, kept, tiles, sems, leaf, quarter).start()


def tile_products(
    evaluate, slots, fill, near, columns, spread, totals, kept, tiles, sems, factors=None,
    leaves=(0, LEAVES), held=False,
):
    rows_at_once = CHUNK if factors is None else QUARTER

    def leaf_step(leaf, _):
        for slot in range(slots):
            field, point = fill(leaf, slot)
            for piece in range(PIECES):
                spread[slot, piece] = jnp.broadcast_to(field(piece), (8, LANES))
            if evaluate and factors is None:
                for at in range(FIELD):
                    spread[slot, PIECES + at] = jnp.broadcast_to(point(at), (8, LANES))

        def quarter_step(quarter, _):
            if not evaluate and not held:
                tile_copy(False, slots, kept, tiles, sems, leaf, quarter).wait()

            def step(chunk, _):
                start = pl.multiple_of(quarter * QUARTER + chunk * rows_at_once, rows_at_once)
                acc = jnp.zeros((rows_at_once // 8, 8, LANES), f32)
                if evaluate:
                    column = columns[leaf, pl.ds(start, rows_at_once), :]
                if evaluate and factors is None:
                    target = [
                        jnp.broadcast_to(column[:, axis : axis + 1], (rows_at_once, LANES)).reshape(
                            rows_at_once // 8, 8, LANES
                        )
                        for axis in range(3)
                    ]
                for slot in range(slots):
                    if factors is not None:
                        distances = jnp.dot(column, factors[slot], preferred_element_type=f32)
                    for piece in range(PIECES):
                        cut = slice(piece * LANES, (piece + 1) * LANES)
                        where = (leaf * slots + slot, pl.ds(start, rows_at_once), cut)
                        if factors is not None:
                            squared = distances[:, cut].reshape(rows_at_once // 8, 8, LANES)
                            squared = jnp.maximum(squared, 1e-30)
                            distance = squared * lax.rsqrt(squared)
                            decay = jnp.exp2(distance * -log2_e)
                            tile = (distance * amplitude + amplitude) * decay
                            kept[where] = tile.reshape(rows_at_once, LANES)
                        elif evaluate:
                            squared = None
                            for axis in range(3):
                                source = spread[slot, PIECES + axis * PIECES + piece]
                                between = target[axis] - source[None]
                                between = between * between
                                squared = between if squared is None else squared + between
                            squared = jnp.maximum(squared, 1e-30)
                            distance = squared * lax.rsqrt(squared)
                            decay = jnp.exp2(distance * (-rate * log2_e))
                            tile = (distance * (amplitude * rate) + amplitude) * decay
                            kept[where] = tile.reshape(rows_at_once, LANES)
                        else:
                            tile = kept[where].reshape(rows_at_once // 8, 8, LANES)
                        acc = acc + tile * spread[slot, piece][None]
                totals[pl.ds(start, rows_at_once), :] = acc.reshape(rows_at_once, LANES)
                return 0

            lax.fori_loop(0, QUARTER // rows_at_once, step, 0)
            if evaluate:
                tile_copy(True, slots, kept, tiles, sems, leaf, quarter).start()
            return 0

        lax.fori_loop(0, PIECES, quarter_step, 0)
        eye = lax.broadcasted_iota(jnp.int32, (LANES, LANES), 0) == lax.broadcasted_iota(
            jnp.int32, (LANES, LANES), 1
        )
        pieces = []
        for piece in range(PIECES):
            column = jnp.sum(totals[piece * LANES : (piece + 1) * LANES, :], axis=1, keepdims=True)
            pieces.append(jnp.sum(jnp.where(eye, column, 0.0), axis=0, keepdims=True))
        near[pl.ds(leaf, 1), :] = jnp.concatenate(pieces, axis=1)
        return 0

    if leaves[0] == 0:
        near[...] = jnp.zeros(near.shape, f32)
    lax.fori_loop(*leaves, leaf_step, 0)


def end_tiles(slots, kept, tiles, sems):
    for leaf in range(LEAVES):
        for quarter in range(PIECES):
            tile_copy(True, slots, kept, tiles, sems, leaf, quarter).wait()


def leaf_coupling(blocks, coupling, far_list, far_count, coefs, leaf_far):
    wide = lax.axis_index("wide")
    own = lax.rem(wide, 2)
    coefs[...] = jnp.zeros(coefs.shape, f32)
    for device in range(NARROW):
        coefs[device * LEAVES : (device + 1) * LEAVES, :] = blocks[
            own * NARROW + device, FIELD : FIELD + LEAVES, :
        ]
    lane = lax.broadcasted_iota(jnp.int32, (16, LANES), 1)
    row = lax.broadcasted_iota(jnp.int32, (16, LANES), 0)
    far_rows = []
    for leaf in range(LEAVES):
        out = times(coefs[:, :RANK], coupling[leaf].reshape(FAR * RANK, RANK), True)
        total = jnp.zeros((16, LANES), f32)
        for two in range(FAR // 2):
            at = []
            for slot in (2 * two, 2 * two + 1):
                member = far_list[leaf, slot] - wide * GROUP
                at.append(jnp.where(slot < far_count[leaf], member, -1))
            listed = jnp.where(lane < RANK, at[0], at[1]) == row
            total = total + jnp.where(listed, out[:, two * LANES : (two + 1) * LANES], 0.0)
        far_rows.append(fold_half(jnp.sum(total, axis=0, keepdims=True)))
    leaf_far[...] = row_by_leaf([jnp.broadcast_to(one, (8, RANK)) for one in far_rows])


def own_kernel(evaluate, *refs):
    if evaluate:
        values, coords_in, tiles, own_near, coords, columns, scratch, sem, *loop = refs
        (copy,) = fetch([(coords_in, coords)], sem)
        copy.wait()
        for leaf in range(LEAVES):
            columns[leaf] = jnp.transpose(padded(coords.at[leaf], scratch))
    else:
        (values, tiles, blocks, coupling, far_list_in, far_count_in, others, own_near, leaf_far,
         early, far_list, far_count, coefs, sem, *loop) = refs
        coords = columns = None
    spread, totals, kept, sems = loop
    if not evaluate:
        copies = fetch([(far_list_in, far_list), (far_count_in, far_count)], sem)
        begin_tiles(1, kept, tiles, sems)
        early_copy = pltpu.make_async_copy(others.at[pl.ds(0, NEAR - 1)], early, sem.at[2])
        early_copy.start()
        for copy in copies:
            copy.wait()
        leaf_coupling(blocks, coupling, far_list, far_count, coefs, leaf_far)

    def fill(leaf, slot):
        def field(piece):
            part = values[:, piece * LANES : (piece + 1) * LANES]
            return jnp.sum(jnp.where(rows_of(part) == leaf, part, 0.0), axis=0, keepdims=True)

        def point(at):
            axis, piece = divmod(at, PIECES)
            return coords[leaf, axis : axis + 1, piece * LANES : (piece + 1) * LANES]

        return field, point

    tile_products(evaluate, 1, fill, own_near, columns, spread, totals, kept, tiles, sems)
    if evaluate:
        end_tiles(1, kept, tiles, sems)
    else:
        early_copy.wait()


def mid_kernel(
    blocks, far_list_in, far_count_in, parent_in, group_far_in, top_far_in, parents_in,
    coupling_in, noise_in, group_in, observed_in, top_in,
    leaf_far, select, own_pair, noise, coupling, group, observed,
    far_list, far_count, parent, group_far, top_far, parents, coefs, sems,
):
    copies = fetch(
        [
            (parent_in, parent), (group_far_in, group_far), (top_far_in, top_far),
            (parents_in, parents), (far_list_in, far_list), (far_count_in, far_count),
            (coupling_in, coupling), (noise_in, noise), (group_in, group),
            (observed_in, observed),
        ],
        sems,
    )
    for copy in copies[:4]:
        copy.wait()
    own_parent = parent[lax.axis_index("wide")]
    top_copy = pltpu.make_async_copy(top_in.at[own_parent], own_pair, sems.at[0])
    top_copy.start()
    select[...] = selection(group_far, top_far, own_parent, parents)
    for copy in copies[4:]:
        copy.wait()
    leaf_coupling(blocks, coupling, far_list, far_count, coefs, leaf_far)
    top_copy.wait()


def mid_apply(blocks, other):
    bf16 = jnp.bfloat16
    groups = other[2].shape[0]
    return pl.pallas_call(
        mid_kernel,
        out_shape=[
            shape(8, RANK),
            shape(16, 2 * groups, dtype=bf16),
            shape(FAR_TOP, RANK, RANK, dtype=bf16),
            shape(LEAVES, POINTS),
            shape(LEAVES, FAR, RANK, RANK, dtype=bf16),
            shape(FAR_GROUP, RANK, RANK, dtype=bf16),
            shape(LEAVES, POINTS),
        ],
        in_specs=[VMEM] + [HBM] * len(other),
        out_specs=[VMEM] * 7,
        scratch_shapes=[
            pltpu.SMEM((LEAVES, FAR), jnp.int32),
            pltpu.SMEM((LEAVES,), jnp.int32),
            pltpu.SMEM((groups,), jnp.int32),
            pltpu.SMEM((1, FAR_GROUP), jnp.int32),
            pltpu.SMEM(other[4].shape, jnp.int32),
            pltpu.VMEM((1, groups), jnp.int32),
            pltpu.VMEM((16, LANES), f32),
            pltpu.SemaphoreType.DMA((10,)),
        ],
        cost_estimate=cost(10**7, 2 * 10**6),
        compiler_params=pltpu.CompilerParams(vmem_limit_bytes=8 << 20),
    )(blocks, *in_hbm(*other))


def near_kernel(evaluate, *refs):
    if evaluate:
        (near_list_in, near_count_in, blocks, extra, values, own_near, noise, coords_in, tiles,
         base, near_list, near_count, sems, window, sources, coords, columns, factors, centres,
         scratch, near, spread, totals, kept, tile_sems) = refs
    else:
        (near_list_in, near_count_in, blocks, extra, values, own_near, noise, early, tiles, base,
         near_list, near_count, sems, window, scratch, near, spread, totals, kept,
         tile_sems) = refs
    slots = NEAR - 1
    pairs = [(near_list_in, near_list), (near_count_in, near_count)]
    copies = fetch(pairs + ([(coords_in, coords)] if evaluate else []), sems)
    if not evaluate:
        begin_tiles(slots, kept, tiles, tile_sems, 1)
    wide = lax.axis_index("wide")
    first_group = wide - lax.rem(wide, 2)
    for device in range(PAIR + NARROW):
        held, index = (blocks, device) if device < PAIR else (extra, device - PAIR)
        more = PACK if device < PAIR else FIELD
        for leaf in range(LEAVES):
            at = device * LEAVES + leaf
            window[at] = held[index, leaf * PIECES : (leaf + 1) * PIECES, :]
            if evaluate:
                rows = more + leaf * FIELD
                sources[at] = held[index, rows : rows + FIELD, :]
    local_part = padded(noise, scratch) * values[...] + own_near[...]
    for copy in copies:
        copy.wait()
    if evaluate:
        for leaf in range(LEAVES):
            points = padded(coords.at[leaf], scratch)
            centre = jnp.broadcast_to(points[:, :1], (8, POINTS))
            centres[leaf] = centre
            factor = target_factor((points - centre) * rate)
            columns[leaf] = jnp.transpose(factor).astype(jnp.bfloat16)

    def source(leaf, points):
        lines = jnp.zeros((8, POINTS), f32)
        for axis in range(3):
            line = [points[axis * PIECES + i : axis * PIECES + i + 1] for i in range(PIECES)]
            lines = jnp.where(rows_of(lines) == axis, jnp.concatenate(line, axis=1), lines)
        return source_factor((lines - centres[leaf]) * rate).astype(jnp.bfloat16)

    def fill(leaf, slot):
        listed = near_list[leaf, slot + 1]
        used = slot + 1 < near_count[leaf]
        of_group = lax.div(listed, GROUP)
        turn = of_group - first_group
        turn = jnp.where((turn >= 0) & (turn < 2), turn, 2)
        place = jnp.where(used, turn * GROUP + listed - of_group * GROUP, 0)
        field = window[place] * jnp.where(used, 1.0, 0.0).astype(f32)
        if evaluate:
            factors[slot] = source(leaf, sources[place])
        return lambda piece: field[piece : piece + 1], None

    if evaluate:
        tile_products(
            True, slots, fill, near, columns, spread, totals, kept, tiles, tile_sems, factors
        )
    else:
        rest = (tiles, tile_sems, None)
        tile_products(
            False, slots, fill, near, None, spread, totals, early, *rest, (0, 1), True
        )
        tile_products(False, slots, fill, near, None, spread, totals, kept, *rest, (1, LEAVES))
    base[...] = local_part + near[...]
    if evaluate:
        end_tiles(slots, kept, tiles, tile_sems)


def loop_scratch(slots):
    return [
        pltpu.VMEM((slots, PIECES + FIELD, 8, LANES), f32),
        pltpu.VMEM((POINTS, LANES), f32),
        pltpu.VMEM((slots * LEAVES, POINTS, POINTS), f32),
        pltpu.SemaphoreType.DMA((LEAVES * PIECES,)),
    ]


def column_scratch():
    return [pltpu.VMEM((LEAVES, 3, POINTS), f32), pltpu.VMEM((LEAVES, POINTS, 8), f32)]


def own_apply(evaluate, values, other, later=(), lists=()):
    out_shape, out_specs = [shape(8, POINTS)], [VMEM]
    if evaluate:
        out_shape = [pltpu.HBM((LEAVES, POINTS, POINTS), f32)] + out_shape
        out_specs = [HBM] + out_specs
        scratch = column_scratch() + [
            pltpu.VMEM((8, POINTS), f32), pltpu.SemaphoreType.DMA((1,))
        ]
    else:
        out_shape += [shape(8, RANK), shape(NEAR - 1, POINTS, POINTS)]
        out_specs += [VMEM] * 2
        scratch = [
            pltpu.SMEM((LEAVES, FAR), jnp.int32),
            pltpu.SMEM((LEAVES,), jnp.int32),
            pltpu.VMEM((16, LANES), f32),
            pltpu.SemaphoreType.DMA((3,)),
        ]
    return pl.pallas_call(
        functools.partial(own_kernel, evaluate),
        out_shape=out_shape,
        in_specs=[VMEM, HBM] + [VMEM] * len(later) + [HBM] * len(lists),
        out_specs=out_specs,
        scratch_shapes=scratch + loop_scratch(1),
        cost_estimate=cost(10**8, 4 * 10**6),
        compiler_params=pltpu.CompilerParams(vmem_limit_bytes=16 << 20),
    )(values, *in_hbm(other), *later, *in_hbm(*lists))


def near_apply(evaluate, lists, near_data, other):
    slots = NEAR - 1
    out_shape, out_specs = [shape(8, POINTS)], [VMEM]
    scratch = [
        pltpu.SMEM((LEAVES, NEAR), jnp.int32),
        pltpu.SMEM((LEAVES,), jnp.int32),
        pltpu.SemaphoreType.DMA((3,)),
        pltpu.VMEM((WINDOW, PIECES, LANES), f32),
    ]
    if evaluate:
        out_shape = [pltpu.HBM((slots * LEAVES, POINTS, POINTS), f32)] + out_shape
        out_specs = [HBM] + out_specs
        scratch += [
            pltpu.VMEM((WINDOW, FIELD, LANES), f32),
            pltpu.VMEM((LEAVES, 3, POINTS), f32),
            pltpu.VMEM((LEAVES, POINTS, 48), jnp.bfloat16),
            pltpu.VMEM((slots, 48, POINTS), jnp.bfloat16),
            pltpu.VMEM((LEAVES, 8, POINTS), f32),
        ]
    scratch += [pltpu.VMEM((8, POINTS), f32)] * 2 + loop_scratch(slots)
    return pl.pallas_call(
        functools.partial(near_kernel, evaluate),
        out_shape=out_shape,
        in_specs=[HBM] * 2 + [VMEM] * len(near_data) + [HBM],
        out_specs=out_specs,
        scratch_shapes=scratch,
        cost_estimate=cost(3 * 10**8, 2 * 10**7),
        compiler_params=pltpu.CompilerParams(vmem_limit_bytes=24 << 20),
    )(*in_hbm(*lists), *near_data, *in_hbm(other))


def far_field(rows, base, leaf_far, select, group_coupling, own_pair, top_transfer, transfer,
              basis):
    wide = lax.axis_index("wide")
    gathered = rows[...]
    picked = jnp.zeros((16, LANES), f32)
    for part in range(3):
        piece = gathered.astype(jnp.bfloat16)
        gathered = gathered - piece.astype(f32)
        picked = picked + jnp.dot(select[...], piece, preferred_element_type=f32)

    def listed(vectors, matrices, slots, first):
        out = times(vectors, matrices[...].reshape(slots * RANK, RANK), True)
        lane = lax.broadcasted_iota(jnp.int32, (16, LANES), 1)
        line = lax.broadcasted_iota(jnp.int32, (16, LANES), 0)
        total = jnp.zeros((16, LANES), f32)
        for two in range(slots // 2):
            own = line == first + 2 * two + jnp.where(lane < RANK, 0, 1)
            total = total + jnp.where(own, out[:, two * LANES : (two + 1) * LANES], 0.0)
        return fold_half(jnp.sum(total, axis=0, keepdims=True))

    top_in = listed(picked[:, RANK:], own_pair, FAR_TOP, FAR_GROUP)
    group_in = listed(picked[:, :RANK], group_coupling, FAR_GROUP, 0)
    group_in = group_in + times(jnp.broadcast_to(top_in, (8, RANK)), top_transfer[lax.rem(wide, 2)], True)
    leaf_in = leaf_far[...] + row_by_leaf(
        [times(group_in, transfer[leaf], True) for leaf in range(LEAVES)]
    )
    far = row_by_leaf([times(leaf_in, basis[leaf], False) for leaf in range(LEAVES)])
    sums = picked[FAR_GROUP + FAR_TOP : FAR_GROUP + FAR_TOP + 1, RANK:]
    return base[...] + far, jnp.sum(sums, axis=1, keepdims=True)


def residual_kernel(*refs):
    *common, observed, packed, residual, scratch = refs
    mapped, _ = far_field(*common)
    field = padded(observed, scratch) - mapped
    residual[...] = field
    pack(field, lane_sums(field * field), common[-1], common[-2], packed)


def second_kernel(*refs):
    *common, residual, packed, first, unit, norm = refs
    mapped, norm_now = far_field(*common)
    first[...] = mapped
    field = mapped * lax.rsqrt(norm_now)
    unit[...] = field
    norm[...] = jnp.broadcast_to(norm_now, norm.shape)
    scalar = lane_sums(residual[...] * mapped)
    pack(field, scalar, common[-1], common[-2], packed)


def third_kernel(*refs):
    *common, residual, first, norm, copies, lower, lower_mapped, step, curve = refs
    mapped, bend = far_field(*common)
    norm_now = norm[:1, :1]
    size = norm_now / bend
    before, image = residual[...], first[...]
    low = before - size * image
    low_mapped = image - (size * jnp.sqrt(norm_now)) * mapped
    lower[...] = low
    lower_mapped[...] = low_mapped
    step[...] = jnp.broadcast_to(size, step.shape)
    curve[...] = jnp.broadcast_to(bend, curve.shape)
    products = [low * low, low * low_mapped, before * low_mapped + low * image]
    sums = [lane_sums(product) for product in products] + [jnp.zeros((1, RANK), f32)]
    first_row = jnp.concatenate(sums[:2], axis=1)
    second_row = jnp.concatenate(sums[2:], axis=1)
    block = jnp.broadcast_to(first_row, (8, LANES))
    block = jnp.where(rows_of(block) == 0, block, second_row)
    copies[...] = jnp.broadcast_to(block[None], copies.shape)


def total_kernel(blocks, copies):
    total = blocks[0]
    for device in range(1, blocks.shape[0]):
        total = total + blocks[device]
    copies[...] = jnp.broadcast_to(total[:2][None], copies.shape)


def step_kernel(warm, residual, step, moved):
    moved[...] = warm[...] + step[:1, :1] * residual[...]


def end_kernel(blocks, moved, residual, first, lower, lower_mapped, norm, curve,
               solution_field, last_residual):
    total = jnp.sum(blocks[...], axis=0)
    norm_next = jnp.sum(total[:1, :RANK], axis=1, keepdims=True)
    bend = jnp.sum(total[:1, RANK:], axis=1, keepdims=True)
    cross = jnp.sum(total[1:2, :RANK], axis=1, keepdims=True)
    norm_now = norm[:1, :1]
    ratio = norm_next / norm_now
    second = norm_next / (bend + ratio * (cross + ratio * curve[:1, :1]))
    keep = slice(0, LEAVES)
    solution_field[...] = moved[keep] + second * (lower[keep] + ratio * residual[keep])
    last_residual[...] = lower[keep] - second * (lower_mapped[keep] + ratio * first[keep])


def simple(kernel, out_shape, in_specs, scratch=()):
    return pl.pallas_call(
        kernel,
        out_shape=out_shape,
        in_specs=in_specs,
        out_specs=[VMEM] * len(out_shape),
        scratch_shapes=list(scratch),
        cost_estimate=cost(10**6, 10**6),
        compiler_params=pltpu.CompilerParams(vmem_limit_bytes=8 << 20),
    )


def exchange(copies, stride):
    members = copies.shape[0]
    devices = lax.axis_size("wide") * lax.axis_size("narrow")
    span = members * stride
    groups = [
        [base + offset + stride * i for i in range(members)]
        for base in range(0, devices, span)
        for offset in range(stride)
    ]
    return lax.all_to_all(
        copies, ("wide", "narrow"), 0, 0, tiled=True, axis_index_groups=groups
    )


def neighbours(fields):
    wide = lax.axis_size("wide")
    across = []
    for first in range(1, wide - 1, 2):
        across += [(first, first + 1), (first + 1, first)]
    return lax.ppermute(fields, "wide", across)


def local(
    coords,
    noise_var,
    observed,
    warm_start,
    leaf_basis,
    leaf_transfer,
    leaf_coupling_matrices,
    group_coupling,
    top_transfer,
    top_coupling,
    near_list,
    near_count,
    far_list,
    far_count,
    group_far,
    parent,
    top_far,
):
    groups = parent.shape[0]
    pairs = groups // 2
    wide = lax.axis_index("wide")
    tops = lax.dynamic_slice_in_dim(top_transfer, wide // 2 * 2, 2, 0)
    field, scalar = shape(8, POINTS), shape(8, LANES)
    packed_shape = shape(PAIR, PACK, LANES)
    scratch = [pltpu.VMEM((8, POINTS), f32)]

    def wide_gather(blocks, *first):
        copies, fields = simple(
            fold_kernel,
            [shape(pairs, 4, LANES), shape(NARROW, blocks.shape[1] - 4, LANES)],
            [VMEM] * (2 + len(first)),
        )(blocks, tops, *first)
        extra = neighbours(fields)
        return extra, exchange(copies, PAIR).reshape(4 * pairs, LANES)

    def gather(packed, values):
        blocks = exchange(packed, 1)
        extra, rows = wide_gather(blocks)
        own_near, leaf_far, early = own_apply(
            False, values, own_tiles, (blocks, coupling), (far_list, far_count, tiles)
        )
        near = (blocks, extra, values, own_near, noise, early)
        (base,) = near_apply(False, (near_list, near_count), near, tiles)
        return rows, base, leaf_far

    packed, values, basis, transfer = simple(
        begin_kernel,
        [
            shape(PAIR, PACK + COORDS, LANES),
            field,
            shape(LEAVES, RANK, POINTS, dtype=jnp.bfloat16),
            shape(LEAVES, RANK, RANK, dtype=jnp.bfloat16),
        ],
        [HBM] * 4,
        [pltpu.VMEM((LEAVES, POINTS), f32), pltpu.VMEM((LEAVES, 3, POINTS), f32)]
        + scratch
        + [pltpu.SemaphoreType.DMA((4,))],
    )(*in_hbm(warm_start, coords, jnp.transpose(leaf_basis, (0, 2, 1)), leaf_transfer))
    blocks = exchange(packed, 1)
    own_tiles, own_near = own_apply(True, values, coords)
    extra, rows = wide_gather(blocks, own_near)
    leaf_far, select, own_pair, noise, coupling, group, observed = mid_apply(
        blocks,
        (
            far_list, far_count, parent, group_far, top_far.T, parent.reshape(1, groups),
            leaf_coupling_matrices, noise_var, group_coupling[0], observed, top_coupling,
        ),
    )
    near = (blocks, extra, values, own_near, noise)
    tiles, base = near_apply(True, (near_list, near_count), near, coords)
    far_data = (select, group, own_pair, tops, transfer, basis)
    packed, residual = simple(
        residual_kernel, [packed_shape, field], [VMEM] * 10, scratch
    )(rows, base, leaf_far, *far_data, observed)

    rows, *near = gather(packed, residual)
    packed, first, unit, norm = simple(
        second_kernel, [packed_shape, field, field, scalar], [VMEM] * 10
    )(rows, *near, *far_data, residual)

    rows, *near = gather(packed, unit)
    sums, lower, lower_mapped, step, curve = simple(
        third_kernel,
        [shape(PAIR, 8, LANES), field, field, scalar, scalar],
        [VMEM] * 12,
    )(rows, *near, *far_data, residual, first, norm)
    blocks = exchange(sums, 1)
    (copies,) = simple(total_kernel, [shape(pairs, 2, LANES)], [VMEM])(blocks)
    blocks = exchange(copies, PAIR)
    (moved,) = simple(step_kernel, [field], [VMEM] * 3)(values, residual, step)
    own = shape(LEAVES, POINTS)
    return tuple(
        simple(end_kernel, [own, own], [VMEM] * 8)(
            blocks, moved, residual, first, lower, lower_mapped, norm, curve
        )
    )


def solution(mesh):
    placed = (
        P(("wide", "narrow"), None, None),
        P(("wide", "narrow"), None),
        P(("wide", "narrow"), None),
        P(("wide", "narrow"), None),
        P(("wide", "narrow"), None, None),
        P(("wide", "narrow"), None, None),
        P(("wide", "narrow"), None, None, None),
        P("wide", None, None, None),
        P(),
        P(),
        P(("wide", "narrow"), None),
        P(("wide", "narrow")),
        P(("wide", "narrow"), None),
        P(("wide", "narrow")),
        P("wide", None),
        P(),
        P(),
    )
    return jax.shard_map(
        local,
        mesh=mesh,
        in_specs=placed,
        out_specs=(P(("wide", "narrow"), None), P(("wide", "narrow"), None)),
        check_vma=False,
    )
```
